256 devices in a mesh: gx: 4 (over y), gy: 8 (over x, core), gz: 8 (over z).
Axes of the slice: x: 4, y: 4, z: 8, core: 2. Of those that a mesh axis runs over, the one named last changes fastest.
Arguments:
- activation: bfloat16 [2, 16, 64, 64, 128], P(None, 'gx', 'gy', 'gz'), may hold values from -6 to 6
- w_in: bfloat16 [3456, 256], replicated, may hold values from -0.109375 to 0.109375
- w_up: bfloat16 [2048, 128], replicated, may hold values from -0.375 to 0.375
- w_out: bfloat16 [6912, 128], replicated, may hold values from -0.078125 to 0.078125
- cotangent: bfloat16 [2, 16, 64, 64, 128], P(None, 'gx', 'gy', 'gz'), may hold values from -6 to 6
Outputs:
- output: bfloat16 [2, 16, 64, 64, 128], P(None, 'gx', 'gy', 'gz')
- d_activation: bfloat16 [2, 16, 64, 64, 128], P(None, 'gx', 'gy', 'gz')
- clipped: float32 [2031616], P(('gx', 'gy', 'gz'))
The draws below stay inside these ranges and needn't reach their ends.
All inputs are finite; a program needn't handle non-finite values.
Results may differ from the reference program's by a relative error of at most 0.0024.
Values may be sent and summed in bfloat16 or wider, within the bound.
No kernel may reach another device: no remote copies, remote signals or barrier semaphores. Data moves between devices by JAX's collectives and lax.ppermute only.
A program may use at most 128 MiB of HBM per device.

```python
import jax
import jax.numpy as jnp
from jax import lax

S = 2
C3 = 128
C4 = 256
NX = 16
NY = 64
NZ = 64
PARAMS = 2031616


def levels(key, extent, shards, least, largest):
    def one(axis_at, shards_of):
        steps = jax.random.uniform(jax.random.fold_in(jax.random.fold_in(key, 6), axis_at), (shards_of,), jnp.float32, least / len(shards), largest / len(shards))
        return jnp.repeat(jnp.exp(steps), extent[axis_at] // shards_of).reshape((-1,) + (1,) * (len(extent) - axis_at - 1))

    gain = one(*shards[0])
    for cut in shards[1:]:
        gain = gain * one(*cut)
    return gain


def centred(rng, extent, width, bound, cuts=(), kind=jnp.bfloat16):
    loudness = levels(rng, extent, cuts, -0.22, 0.18) if cuts else 1.0
    values = jax.random.normal(rng, extent, jnp.float32) * width * loudness
    return jnp.minimum(jnp.maximum(values, -bound), bound).astype(kind)


def setup_inputs(seed: int = 0) -> dict:
    seeds = jax.random.split(jax.random.key(seed), 6)
    activation = centred(seeds[0], (S, NX, NY, NZ, C3), 1.0, 6.0, ((1, 4), (2, 8), (3, 8)))
    w_in = centred(seeds[1], (27 * C3, C4), (27 * C3) ** -0.5, 0.109375)
    w_up = centred(seeds[2], (8 * C4, C3), C4 ** -0.5, 0.375)
    w_out = centred(seeds[3], (54 * C3, C3), (54 * C3) ** -0.5, 0.078125)
    cotangent = centred(seeds[4], (S, NX, NY, NZ, C3), 1.0, 6.0, ((1, 4), (2, 8), (3, 8)))
    return dict(activation=activation, w_in=w_in, w_up=w_up, w_out=w_out, cotangent=cotangent)


def pad_one(volume):
    return jnp.pad(volume, ((0, 0), (1, 1), (1, 1), (1, 1), (0, 0)))

def conv_forward(padded, weight):
    in_chan = padded.shape[4]
    tap_weights = weight.astype(jnp.float32).reshape(27, in_chan, -1)
    padded = padded.astype(jnp.float32)
    extent_x, extent_y, extent_z = (padded.shape[1] - 2, padded.shape[2] - 2, padded.shape[3] - 2)
    summed = None
    for tap_index in range(27):
        shift_x, shift_y, shift_z = (tap_index // 9, tap_index // 3 % 3, tap_index % 3)
        window = padded[:, shift_x:shift_x + extent_x, shift_y:shift_y + extent_y, shift_z:shift_z + extent_z, :]
        product = jnp.einsum('sxyzc,co->sxyzo', window, tap_weights[tap_index])
        summed = product if summed is None else summed + product
    return summed

def conv_transpose(padded, weight):
    out_chan = padded.shape[4]
    tap_weights = weight.astype(jnp.float32).reshape(27, -1, out_chan)
    padded = padded.astype(jnp.float32)
    extent_x, extent_y, extent_z = (padded.shape[1] - 2, padded.shape[2] - 2, padded.shape[3] - 2)
    summed = None
    for tap_index in range(27):
        shift_x, shift_y, shift_z = (2 - tap_index // 9, 2 - tap_index // 3 % 3, 2 - tap_index % 3)
        window = padded[:, shift_x:shift_x + extent_x, shift_y:shift_y + extent_y, shift_z:shift_z + extent_z, :]
        product = jnp.einsum('sxyzo,co->sxyzc', window, tap_weights[tap_index])
        summed = product if summed is None else summed + product
    return summed

def conv_weight(padded, gradient):
    in_chan = padded.shape[4]
    padded = padded.astype(jnp.float32)
    gradient = gradient.astype(jnp.float32)
    extent_x, extent_y, extent_z = (padded.shape[1] - 2, padded.shape[2] - 2, padded.shape[3] - 2)
    pieces = []
    for tap_index in range(27):
        shift_x, shift_y, shift_z = (tap_index // 9, tap_index // 3 % 3, tap_index % 3)
        window = padded[:, shift_x:shift_x + extent_x, shift_y:shift_y + extent_y, shift_z:shift_z + extent_z, :]
        pieces.append(jnp.einsum('sxyzc,sxyzo->co', window, gradient))
    return jnp.stack(pieces).reshape(27 * in_chan, -1)

def pool_half(volume):
    samples, size_x, size_y, size_z, chans = volume.shape
    blocks = volume.astype(jnp.float32).reshape(samples, size_x // 2, 2, size_y // 2, 2, size_z // 2, 2, chans)
    return lax.optimization_barrier(jnp.mean(blocks, axis=(2, 4, 6)))

def spread(volume):
    samples, size_x, size_y, size_z, chans = volume.shape
    wide = jnp.broadcast_to(volume[:, :, None, :, None, :, None, :], (samples, size_x, 2, size_y, 2, size_z, 2, chans))
    return wide.reshape(samples, 2 * size_x, 2 * size_y, 2 * size_z, chans)

def up_conv(bottom, w_up):
    samples, size_x, size_y, size_z, wide = bottom.shape
    kernel = w_up.astype(jnp.float32).reshape(2, 2, 2, wide, -1)
    result = jnp.einsum('sijkc,abeco->siajbkeo', bottom.astype(jnp.float32), kernel)
    return result.reshape(samples, 2 * size_x, 2 * size_y, 2 * size_z, -1)

def up_back(bottom, d_upward, w_up):
    samples, size_x, size_y, size_z, wide = bottom.shape
    kernel = w_up.astype(jnp.float32).reshape(2, 2, 2, wide, -1)
    blocks = d_upward.astype(jnp.float32).reshape(samples, size_x, 2, size_y, 2, size_z, 2, -1)
    grad_up = jnp.einsum('sijkc,siajbkeo->abeco', bottom.astype(jnp.float32), blocks).reshape(8 * wide, -1)
    d_bottom = jnp.einsum('siajbkeo,abeco->sijkc', blocks, kernel)
    return (grad_up, d_bottom)

def reference(activation, w_in, w_up, w_out, cotangent):
    pooled = pool_half(activation).astype(jnp.bfloat16)
    pooled_pad = pad_one(pooled)
    before = conv_forward(pooled_pad, w_in)
    bottom = jax.nn.silu(before).astype(jnp.bfloat16)
    upward = up_conv(bottom, w_up).astype(jnp.bfloat16)
    joined_pad = pad_one(jnp.concatenate([activation, upward], axis=4))
    output = conv_forward(joined_pad, w_out).astype(jnp.bfloat16)
    grad_out = conv_weight(joined_pad, cotangent)
    d_joined = conv_transpose(pad_one(cotangent), w_out)
    d_upward = d_joined[..., C3:].astype(jnp.bfloat16)
    grad_up, d_bottom = up_back(bottom, d_upward, w_up)
    squash = jax.nn.sigmoid(before)
    d_before = (d_bottom * squash * (1.0 + before * (1.0 - squash))).astype(jnp.bfloat16)
    grad_in = conv_weight(pooled_pad, d_before)
    d_pooled = conv_transpose(pad_one(d_before), w_in)
    d_activation = (d_joined[..., :C3] + spread(d_pooled) * 0.125).astype(jnp.bfloat16)
    square_sum = jnp.sum(grad_in * grad_in) + jnp.sum(grad_up * grad_up) + jnp.sum(grad_out * grad_out)
    factor = jnp.minimum(1.0, jnp.sqrt(PARAMS / (square_sum + 1e-06)))
    clipped = jnp.concatenate([grad_in.ravel(), grad_up.ravel(), grad_out.ravel()]) * factor
    return (output, d_activation, clipped)
```

```python
import jax
import jax.numpy as jnp
from jax import lax
from jax.sharding import Mesh, PartitionSpec as P

F32 = jnp.float32
BF16 = jnp.bfloat16
CELLS = ("gx", ("x", "core"), "gz")


def swap_faces(arrays, axis, dim):
    count = lax.axis_size(axis)
    up = [(i, i + 1) for i in range(count - 1)]
    down = [(j, i) for i, j in up]
    lasts = [lax.slice_in_dim(a, a.shape[dim] - 1, a.shape[dim], axis=dim) for a in arrays]
    firsts = [lax.slice_in_dim(a, 0, 1, axis=dim) for a in arrays]

    def pack(parts):
        return jnp.concatenate([p.reshape(-1, 128) for p in parts], axis=0)

    before = lax.ppermute(pack(lasts), axis, up)
    after = lax.ppermute(pack(firsts), axis, down)
    grown, at = [], 0
    for array, face in zip(arrays, firsts):
        rows = face.size // 128
        low = before[at : at + rows].reshape(face.shape)
        high = after[at : at + rows].reshape(face.shape)
        grown.append(jnp.concatenate([low, array, high], axis=dim))
        at += rows
    return grown


def extended(arrays):
    for dim, axis in enumerate(CELLS):
        arrays = swap_faces(arrays, axis, dim + 1)
    return arrays


def conv_forward(padded, weight):
    kernel = weight.reshape(3, 3, 3, padded.shape[4], -1)
    return lax.conv_general_dilated(
        padded, kernel, (1, 1, 1), "VALID",
        dimension_numbers=("NXYZC", "XYZIO", "NXYZC"), preferred_element_type=F32,
    )


def conv_transpose(padded, weight):
    kernel = weight.reshape(3, 3, 3, -1, padded.shape[4])[::-1, ::-1, ::-1]
    return lax.conv_general_dilated(
        padded, kernel, (1, 1, 1), "VALID",
        dimension_numbers=("NXYZC", "XYZOI", "NXYZC"), preferred_element_type=F32,
    )


def flipped(volume):
    return volume[:, ::-1, ::-1, ::-1]


def conv_weight(padded, gradient):
    return lax.conv_general_dilated(
        padded, gradient, (1, 1, 1), "VALID",
        dimension_numbers=("CXYZN", "IXYZO", "XYZNC"), preferred_element_type=F32,
    ).reshape(27, padded.shape[4], gradient.shape[4])


def conv_weight_back(local, padded):
    return lax.conv_general_dilated(
        flipped(padded), flipped(local), (1, 1, 1), "VALID",
        dimension_numbers=("CXYZN", "IXYZO", "XYZCN"), preferred_element_type=F32,
    ).reshape(27, local.shape[4], padded.shape[4])


def pool_half(volume):
    samples, size_x, size_y, size_z, chans = volume.shape
    blocks = volume.astype(F32).reshape(samples, size_x // 2, 2, size_y // 2, 2, size_z // 2, 2, chans)
    return jnp.mean(blocks, axis=(2, 4, 6))


def spread(volume):
    samples, size_x, size_y, size_z, chans = volume.shape
    wide = jnp.broadcast_to(
        volume[:, :, None, :, None, :, None, :], (samples, size_x, 2, size_y, 2, size_z, 2, chans)
    )
    return wide.reshape(samples, 2 * size_x, 2 * size_y, 2 * size_z, chans)


def up_conv(bottom, w_up):
    samples, size_x, size_y, size_z, wide = bottom.shape
    kernel = w_up.reshape(2, 2, 2, wide, -1)
    result = jnp.einsum("sijkc,abeco->siajbkeo", bottom, kernel, preferred_element_type=F32)
    return result.reshape(samples, 2 * size_x, 2 * size_y, 2 * size_z, -1)


def up_back(bottom, d_upward, w_up):
    samples, size_x, size_y, size_z, wide = bottom.shape
    kernel = w_up.reshape(2, 2, 2, wide, -1)
    blocks = d_upward.reshape(samples, size_x, 2, size_y, 2, size_z, 2, -1)
    grad_up = jnp.einsum("sijkc,siajbkeo->abeco", bottom, blocks, preferred_element_type=F32)
    d_bottom = jnp.einsum("siajbkeo,abeco->sijkc", blocks, kernel, preferred_element_type=F32)
    return (grad_up.reshape(8 * wide, -1), d_bottom)


def at(array, index, axis):
    return lax.dynamic_index_in_dim(array, index, axis, keepdims=False)


def turned(array, axis, shift):
    count = lax.axis_size(axis)
    return lax.ppermute(array, axis, [(i, (i + shift) % count) for i in range(count)])


def paired(array, axis, bit):
    count = lax.axis_size(axis)
    return lax.ppermute(array, axis, [(i, i ^ bit) for i in range(count)])


def scattered_sum(rows):
    gx, x, core, gz = (lax.axis_index(a) for a in ("gx", "x", "core", "gz"))
    blocks = rows.reshape(4, 4, 2, 496, 128)
    blocks = at(blocks, core, 2) + paired(at(blocks, 1 - core, 2), "core", 1)
    one, two = blocks[:, :, :248], blocks[:, :, 248:]
    got_one, got_two = [], []
    for s in (2, 1, 3):
        got_one.append(turned(at(one, (gx + s) % 4, 0).astype(BF16), "gx", s))
        got_two.append(turned(at(two, (x + s) % 4, 1).astype(BF16), "x", s))
    one = at(one, gx, 0) + sum(g.astype(F32) for g in got_one)
    two = at(two, x, 1) + sum(g.astype(F32) for g in got_two)
    got_one, got_two = [], []
    for s in (2, 1, 3):
        got_one.append(turned(at(one, (x + s) % 4, 0), "x", s))
        got_two.append(turned(at(two, (gx + s) % 4, 0), "gx", s))
    one = at(one, x, 0) + sum(got_one)
    two = at(two, gx, 0) + sum(got_two)
    mine = jnp.concatenate([one, two], axis=0).reshape(2, 2, 2, 62, 128)
    for bit in (1, 2, 4):
        half = (gz // bit) % 2
        axis = mine.ndim - 3
        mine = at(mine, half, axis) + paired(at(mine, 1 - half, axis), "gz", bit)
    return mine


def summed_everywhere(value):
    for axis, bits in (("core", (1,)), ("gx", (1, 2)), ("x", (1, 2)), ("gz", (1, 2, 4))):
        for bit in bits:
            value = value + paired(value, axis, bit)
    return value


def local(activation, w_in, w_up, w_out, cotangent):
    channels = activation.shape[4]
    pooled = pool_half(activation).astype(BF16)
    active_pad, cotan_pad, pooled_pad = extended([activation, cotangent, pooled])

    before = conv_forward(pooled_pad, w_in)
    squash = jax.nn.sigmoid(before)
    bottom = (before * squash).astype(BF16)
    upward = up_conv(bottom, w_up).astype(BF16)
    joined = jnp.concatenate([activation, upward], axis=4)
    grad_out = conv_weight_back(joined, cotan_pad)
    d_joined = conv_transpose(cotan_pad, w_out)
    d_upward = d_joined[..., channels:].astype(BF16)
    grad_up, d_bottom = up_back(bottom, d_upward, w_up)
    d_before = (d_bottom * squash * (1.0 + before * (1.0 - squash))).astype(BF16)
    grad_in = conv_weight(pooled_pad, d_before)

    rows = jnp.concatenate([g.reshape(-1, 128) for g in (grad_in, grad_up, grad_out)], axis=0)
    mine = scattered_sum(rows)
    total = jnp.sum(summed_everywhere(jnp.sum(mine * mine, axis=0, keepdims=True)))
    factor = jnp.minimum(1.0, jnp.sqrt(rows.size / (total + 1e-06)))
    clipped = (mine * factor).reshape(-1)

    bottom_pad, slope_pad = extended([bottom, d_before])
    upward_pad = up_conv(bottom_pad, w_up).astype(BF16)[:, 1:-1, 1:-1, 1:-1]
    output = conv_forward(jnp.concatenate([active_pad, upward_pad], axis=4), w_out).astype(BF16)
    d_pooled = conv_transpose(slope_pad, w_in)
    d_activation = (d_joined[..., :channels] + spread(d_pooled) * 0.125).astype(BF16)
    return (output, d_activation, clipped)


def solution(mesh):
    gx, gy, gz = mesh.devices.shape
    split = Mesh(mesh.devices.reshape(gx, gy // 2, 2, gz), ("gx", "x", "core", "gz"))
    cells = P(None, "gx", ("x", "core"), "gz", None)
    return jax.shard_map(
        local, mesh=split, in_specs=(cells, P(), P(), P(), cells),
        out_specs=(cells, cells, P(("gx", "x", "core", "gz"))), check_vma=False,
    )
```

```python
import itertools

import jax
import jax.numpy as jnp
import numpy as np
from jax import lax
from jax.experimental import pallas as pl
from jax.experimental.pallas import tpu as pltpu
from jax.sharding import Mesh, PartitionSpec as P

F32 = jnp.float32
BF16 = jnp.bfloat16
PARAMS = 2031616
CELLS = ("gx", ("x", "core"), "gz")


def traded_faces(arrays, axis, dim):
    count = lax.axis_size(axis)
    even = lax.axis_index(axis) % 2 == 0
    first_pairs = [(i, i ^ 1) for i in range(count)]
    second_pairs = [(i, j) for i in range(count) for j in [((i + 1) ^ 1) - 1] if 0 <= j < count]

    def face(last):
        parts = []
        for array in arrays:
            at = array.shape[dim] - 1 if last else 0
            parts.append(lax.slice_in_dim(array, at, at + 1, axis=dim).reshape(-1, 128))
        return jnp.concatenate(parts, axis=0)

    lasts, firsts = face(True), face(False)
    one = lax.ppermute(jnp.where(even, lasts, firsts), axis, first_pairs)
    two = lax.ppermute(jnp.where(even, firsts, lasts), axis, second_pairs)
    lows, highs = jnp.where(even, two, one), jnp.where(even, one, two)
    faces, at = [], 0
    for array in arrays:
        shape = array.shape[:dim] + (1,) + array.shape[dim + 1 :]
        rows = array.size // array.shape[dim] // 128
        faces.append((lows[at : at + rows].reshape(shape), highs[at : at + rows].reshape(shape)))
        at += rows
    return faces


def joined_faces(arrays, faces, dim):
    return [jnp.concatenate([low, array, high], axis=dim) for array, (low, high) in zip(arrays, faces)]


def extended(arrays, axes=CELLS):
    for dim, axis in enumerate(axes):
        arrays = joined_faces(arrays, traded_faces(arrays, axis, dim + 1), dim + 1)
    return arrays


def conv_forward(padded, weight):
    kernel = weight.reshape(3, 3, 3, padded.shape[4], -1)
    return lax.conv_general_dilated(
        padded, kernel, (1, 1, 1), "VALID",
        dimension_numbers=("NXYZC", "XYZIO", "NXYZC"), preferred_element_type=F32,
    )


def conv_transpose(padded, weight):
    kernel = weight.reshape(3, 3, 3, -1, padded.shape[4])[::-1, ::-1, ::-1]
    return lax.conv_general_dilated(
        padded, kernel, (1, 1, 1), "VALID",
        dimension_numbers=("NXYZC", "XYZOI", "NXYZC"), preferred_element_type=F32,
    )


def pool_half(volume):
    samples, size_x, size_y, size_z, chans = volume.shape
    blocks = volume.astype(F32).reshape(samples, size_x // 2, 2, size_y // 2, 2, size_z // 2, 2, chans)
    return jnp.mean(blocks, axis=(2, 4, 6))


def spread(volume):
    samples, size_x, size_y, size_z, chans = volume.shape
    wide = jnp.broadcast_to(
        volume[:, :, None, :, None, :, None, :], (samples, size_x, 2, size_y, 2, size_z, 2, chans)
    )
    return wide.reshape(samples, 2 * size_x, 2 * size_y, 2 * size_z, chans)


def up_conv(bottom, w_up):
    samples, size_x, size_y, size_z, wide = bottom.shape
    kernel = w_up.reshape(2, 2, 2, wide, -1)
    result = jnp.einsum("sijkc,abeco->siajbkeo", bottom, kernel, preferred_element_type=F32)
    return result.reshape(samples, 2 * size_x, 2 * size_y, 2 * size_z, -1)


def _select_pooled():
    sel = np.zeros((9, 2, 4, 4, 4, 288), np.float32)
    for dy in range(3):
        for dz in range(3):
            for s, x, y, z in itertools.product(range(2), range(4), range(4), range(4)):
                line, k = (s * 4 + x) * 6 + y + dy, z + dz - 1
                source = 192 + line if k < 0 else 240 + line if k > 3 else line * 4 + k
                sel[3 * dy + dz, s, x, y, z, source] = 1
    return sel.reshape(1152, 288)


def _fine_from_blocks():
    perm = np.zeros((512, 512), np.float32)
    for s, x, y, z in itertools.product(range(2), range(4), range(8), range(8)):
        fine = ((s * 4 + x) * 8 + y) * 8 + z
        part = (x % 2) * 4 + (y % 2) * 2 + z % 2
        perm[fine, part * 64 + ((s * 2 + x // 2) * 4 + y // 2) * 4 + z // 2] = 1
    return perm


def _dot(a, b, contract=((1,), (0,))):
    return lax.dot_general(a, b, (contract, ((), ())), preferred_element_type=F32)


def _gradients_kernel(
    core_ref, act_ref, cot_ref, cot_low_ref, cot_high_ref, pool_ref, sel_ref, perm_ref, perm_t_ref,
    w_in_hbm, w_back_hbm, w_up_hbm,
    keep_hbm, send_hbm, bottom_ref, slope_ref, d_act_ref,
    w_in, w_back, w_up, lines, shifted, pooled, spaced, sums, sem_in, sem_out,
):
    loads = [
        pltpu.make_async_copy(source, target, sem_in.at[i])
        for i, (source, target) in enumerate(((w_in_hbm, w_in), (w_up_hbm, w_up), (w_back_hbm, w_back)))
    ]
    for load in loads:
        load.start()
    core = core_ref[0]
    side = (core, 1 - core)

    def put(row, value, stride=1):
        done, count = 0, value.shape[0]
        while done < count:
            first = row + stride * done
            block = first // 496
            here = min(count - done, -((first - 496 * (block + 1)) // stride))
            where = pl.ds(first % 496, here) if stride == 1 else pl.ds(first % 496, here, stride)
            sums[side[block % 2], block // 2, where, :] = value[done : done + here]
            done += here

    def ship(index, first, last):
        copies = [
            pltpu.make_async_copy(sums.at[i, pl.ds(first, last - first)], hbm.at[pl.ds(first, last - first)], sem_out.at[index, i])
            for i, hbm in enumerate((keep_hbm, send_hbm))
        ]
        for copy in copies:
            copy.start()
        return copies

    picked = _dot(sel_ref[...], pool_ref[...])
    for u in range(9):
        pooled[:, :, :, u * 128 : (u + 1) * 128] = picked[u * 128 : (u + 1) * 128].reshape(2, 4, 16, 128).astype(BF16)
    loads[0].wait()
    before = jnp.zeros((64, 256), F32)
    for dx in range(3):
        before += _dot(pooled[:, dx : dx + 2].reshape(64, 1152), w_in[dx * 1152 : (dx + 1) * 1152, :])
    squash = 1.0 / (1.0 + jnp.exp(-before))
    bottom32 = (before * squash).astype(BF16).astype(F32)
    bottom = bottom32.astype(BF16)
    bottom_ref[...] = bottom
    loads[1].wait()
    parts = [_dot(bottom, w_up[p * 256 : (p + 1) * 256, :]).astype(BF16) for p in range(8)]
    upward = _dot(perm_ref[...], jnp.concatenate(parts, axis=0))

    lines[:, 8:16, :] = cot_ref[...].astype(F32).reshape(120, 8, 128)
    lines[:, 7:8, :] = cot_low_ref[...].astype(F32)[:, None, :]
    lines[:, 16:17, :] = cot_high_ref[...].astype(F32)[:, None, :]
    for dz in range(3):
        window = lines[:, 7 + dz : 15 + dz, :].reshape(2, 6, 10, 8, 128)
        for dy in range(3):
            u = 3 * dy + dz
            shifted[:, :, :, u * 128 : (u + 1) * 128] = window[:, :, dy : dy + 8].reshape(2, 6, 64, 128).astype(BF16)

    loads[2].wait()
    d_joined = jnp.zeros((512, 256), F32)
    for dx in range(3):
        d_joined += _dot(shifted[:, dx : dx + 4].reshape(512, 1152), w_back[dx * 1152 : (dx + 1) * 1152, :])
    d_act_ref[...] = d_joined[:, :128]

    joined_t = jnp.concatenate([act_ref[...].astype(F32).T, upward.T], axis=0).astype(BF16)
    for dx in range(3):
        grad = _dot(joined_t, shifted[:, dx : dx + 4].reshape(512, 1152))
        for u in range(9):
            put(8960 + (26 - 9 * dx - u) * 256, grad[:, u * 128 : (u + 1) * 128])
    copies = ship(0, 10, 16)

    blocks = _dot(perm_t_ref[...], d_joined[:, 128:].astype(BF16)).astype(BF16)
    d_bottom = jnp.zeros((64, 256), F32)
    for p in range(8):
        d_bottom += _dot(blocks[p * 64 : (p + 1) * 64], w_up[p * 256 : (p + 1) * 256, :], ((1,), (1,)))
    bottom_t = bottom32.T.astype(BF16)
    for p in range(8):
        put(6912 + p * 256, _dot(bottom_t, blocks[p * 64 : (p + 1) * 64]))
    slope = (d_bottom * squash * (1.0 + before * (1.0 - squash))).astype(BF16)
    slope_ref[...] = slope

    spaced[...] = jnp.zeros((128, 768), BF16)
    for s in range(2):
        for dx in range(3):
            spaced[s * 64 + dx * 16 : s * 64 + dx * 16 + 32, dx * 256 : (dx + 1) * 256] = slope[s * 32 : (s + 1) * 32]
    for u in range(9):
        picked_t = picked[u * 128 : (u + 1) * 128].T.astype(BF16)
        grad = _dot(picked_t, spaced[...])
        for dx in range(3):
            for h in range(2):
                put((9 * dx + u) * 256 + h, grad[:, dx * 256 + h * 128 : dx * 256 + (h + 1) * 128], 2)
    copies += ship(1, 0, 10)
    for copy in copies:
        copy.wait()


def gradients(core, act, cot, cot_low, cot_high, pool, w_in, w_back, w_up):
    shape = jax.ShapeDtypeStruct
    vmem, hbm = pl.BlockSpec(memory_space=pltpu.VMEM), pl.BlockSpec(memory_space=pl.ANY)
    return pl.pallas_call(
        _gradients_kernel,
        out_shape=(
            shape((16, 496, 128), F32), shape((16, 496, 128), F32),
            shape((64, 256), BF16), shape((64, 256), BF16), shape((512, 128), F32),
        ),
        in_specs=[pl.BlockSpec(memory_space=pltpu.SMEM)] + [vmem] * 8 + [hbm] * 3,
        out_specs=(hbm, hbm, vmem, vmem, vmem),
        scratch_shapes=[
            pltpu.VMEM((3456, 256), BF16), pltpu.VMEM((3456, 256), BF16), pltpu.VMEM((2048, 128), BF16),
            pltpu.VMEM((120, 24, 128), F32), pltpu.VMEM((2, 6, 64, 1152), BF16),
            pltpu.VMEM((2, 4, 16, 1152), BF16), pltpu.VMEM((128, 768), BF16),
            pltpu.VMEM((2, 16, 496, 128), F32),
            pltpu.SemaphoreType.DMA((3,)), pltpu.SemaphoreType.DMA((2, 2)),
        ],
        compiler_params=pltpu.CompilerParams(vmem_limit_bytes=48 * 1024 * 1024),
        cost_estimate=pl.CostEstimate(flops=2_500_000_000, bytes_accessed=16_000_000, transcendentals=16384),
    )(
        core, act, cot, cot_low, cot_high, pool,
        jnp.asarray(_select_pooled(), BF16), jnp.asarray(_fine_from_blocks(), BF16), jnp.asarray(_fine_from_blocks().T, BF16),
        w_in, w_back, w_up,
    )


def at(array, index, axis):
    return lax.dynamic_index_in_dim(array, index, axis, keepdims=False)


def turned(array, axis, shift):
    count = lax.axis_size(axis)
    return lax.ppermute(array, axis, [(i, (i + shift) % count) for i in range(count)])


def paired(array, axis, bit):
    count = lax.axis_size(axis)
    return lax.ppermute(array, axis, [(i, i ^ bit) for i in range(count)])


def scattered_sum(keep, send):
    gx, x, gz = (lax.axis_index(a) for a in ("gx", "x", "gz"))
    blocks = (keep + paired(send, "core", 1)).reshape(4, 4, 496, 128)
    one, two = blocks[:, :, :248], blocks[:, :, 248:]
    got_one, got_two = [], []
    for s in (2, 1, 3):
        got_one.append(turned(at(one, (gx + s) % 4, 0).astype(BF16), "gx", s))
        got_two.append(turned(at(two, (x + s) % 4, 1).astype(BF16), "x", s))
    one = at(one, gx, 0) + sum(g.astype(F32) for g in got_one)
    two = at(two, x, 1) + sum(g.astype(F32) for g in got_two)
    got_one, got_two = [], []
    for s in (2, 1, 3):
        got_one.append(turned(at(one, (x + s) % 4, 0), "x", s))
        got_two.append(turned(at(two, (gx + s) % 4, 0), "gx", s))
    one = at(one, x, 0) + sum(got_one)
    two = at(two, gx, 0) + sum(got_two)
    mine = jnp.concatenate([one, two], axis=0).reshape(2, 2, 2, 62, 128)
    for bit in (1, 2, 4):
        half = (gz // bit) % 2
        axis = mine.ndim - 3
        mine = at(mine, half, axis) + paired(at(mine, 1 - half, axis), "gz", bit)
    return mine


def summed_everywhere(value):
    for axis, bits in (("core", (1,)), ("gx", (1, 2)), ("x", (1, 2)), ("gz", (1, 2, 4))):
        for bit in bits:
            value = value + paired(value, axis, bit)
    return value


def local(activation, w_in, w_up, w_out, cotangent):
    pooled = pool_half(activation).astype(BF16)
    arrays = extended([activation, cotangent, pooled], CELLS[:2])
    faces = traded_faces(arrays, "gz", 3)
    active_pad = jnp.concatenate([faces[0][0], arrays[0], faces[0][1]], axis=3)
    cot_low, cot_high = (face.reshape(120, 128) for face in faces[1])
    pool_rows = jnp.concatenate([p.reshape(-1, 128) for p in (arrays[2], *faces[2])], axis=0)
    w_back = w_out.reshape(27, 256, 128)[::-1].transpose(0, 2, 1).reshape(3456, 256)

    core = lax.axis_index("core").astype(jnp.int32)[None]
    keep, send, bottom, d_before, d_direct = gradients(
        core, activation.reshape(512, 128), arrays[1].reshape(960, 128), cot_low, cot_high,
        pool_rows, w_in, w_back, w_up,
    )
    mine = scattered_sum(keep, send)
    total = jnp.sum(summed_everywhere(jnp.sum(mine * mine, axis=0, keepdims=True)))
    factor = jnp.minimum(1.0, jnp.sqrt(PARAMS / (total + 1e-06)))
    clipped = (mine * factor).reshape(-1)

    bottom_pad, slope_pad = extended([bottom.reshape(2, 2, 4, 4, 256), d_before.reshape(2, 2, 4, 4, 256)])
    upward_pad = up_conv(bottom_pad, w_up).astype(BF16)[:, 1:-1, 1:-1, 1:-1]
    output = conv_forward(jnp.concatenate([active_pad, upward_pad], axis=4), w_out).astype(BF16)
    d_pooled = conv_transpose(slope_pad, w_in)
    d_activation = (d_direct.reshape(activation.shape) + spread(d_pooled) * 0.125).astype(BF16)
    return (output, d_activation, clipped)


def solution(mesh):
    gx, gy, gz = mesh.devices.shape
    split = Mesh(mesh.devices.reshape(gx, gy // 2, 2, gz), ("gx", "x", "core", "gz"))
    cells = P(None, "gx", ("x", "core"), "gz", None)
    return jax.shard_map(
        local, mesh=split, in_specs=(cells, P(), P(), P(), cells),
        out_specs=(cells, cells, P(("gx", "x", "core", "gz"))), check_vma=False,
    )
```

```python
import itertools

import jax
import jax.numpy as jnp
import numpy as np
from jax import lax
from jax.experimental import pallas as pl
from jax.experimental.pallas import tpu as pltpu
from jax.sharding import Mesh, PartitionSpec as P

F32 = jnp.float32
BF16 = jnp.bfloat16
PARAMS = 2031616


def conv_forward(padded, weight):
    kernel = weight.reshape(3, 3, 3, padded.shape[4], -1)
    return lax.conv_general_dilated(
        padded, kernel, (1, 1, 1), "VALID",
        dimension_numbers=("NXYZC", "XYZIO", "NXYZC"), preferred_element_type=F32,
    )


def conv_transpose(padded, weight):
    kernel = weight.reshape(3, 3, 3, -1, padded.shape[4])[::-1, ::-1, ::-1]
    return lax.conv_general_dilated(
        padded, kernel, (1, 1, 1), "VALID",
        dimension_numbers=("NXYZC", "XYZOI", "NXYZC"), preferred_element_type=F32,
    )


def spread(volume):
    samples, size_x, size_y, size_z, chans = volume.shape
    wide = jnp.broadcast_to(
        volume[:, :, None, :, None, :, None, :], (samples, size_x, 2, size_y, 2, size_z, 2, chans)
    )
    return wide.reshape(samples, 2 * size_x, 2 * size_y, 2 * size_z, chans)


def up_conv(bottom, w_up):
    samples, size_x, size_y, size_z, wide = bottom.shape
    kernel = w_up.reshape(2, 2, 2, wide, -1)
    result = jnp.einsum("sijkc,abeco->siajbkeo", bottom, kernel, preferred_element_type=F32)
    return result.reshape(samples, 2 * size_x, 2 * size_y, 2 * size_z, -1)


def _select_pooled():
    sel = np.zeros((9, 4, 4, 48), np.float32)
    for dy, dz, y, z in itertools.product(range(3), range(3), range(4), range(4)):
        line, k = y + dy, z + dz - 1
        sel[3 * dy + dz, y, z, 24 + line if k < 0 else 32 + line if k > 3 else line * 4 + k] = 1
    return sel.reshape(144, 48)


def _fine_from_blocks():
    perm = np.zeros((128, 128), np.float32)
    for a, y, z in itertools.product(range(2), range(8), range(8)):
        perm[(a * 8 + y) * 8 + z, (a * 4 + (y % 2) * 2 + z % 2) * 16 + (y // 2) * 4 + z // 2] = 1
    return perm


def _picks(sources, width):
    picks = np.zeros((len(sources), width), np.float32)
    picks[np.arange(len(sources)), sources] = 1
    return picks


def _at_y(s, x, y, z):
    line = s * 2 + x
    return 64 + line * 4 + z if y < 0 else 80 + line * 4 + z if y > 3 else (line * 4 + y) * 4 + z


def _at_x(s, x, y, z):
    line = s * 6 + y + 1
    return 96 + line * 4 + z if x < 0 else 144 + line * 4 + z if x > 1 else _at_y(s, x, y, z)


def _at_z(s, x, y, z):
    line = (s * 4 + x + 1) * 6 + y + 1
    return 192 + line if z < 0 else 240 + line if z > 3 else _at_x(s, x, y, z)


def _pool_of():
    pool = np.zeros((16, 128), np.float32)
    for a, y, z in itertools.product(range(2), range(8), range(8)):
        pool[(y // 2) * 4 + z // 2, (a * 8 + y) * 8 + z] = 0.125
    return pool


S2, X2, Y4, Z4 = range(2), range(2), range(4), range(4)
X4, Y6, Z6 = range(-1, 3), range(-1, 5), range(-1, 5)
Y_FACES = _picks([_at_y(s, x, y, z) for y in (0, 3) for s in S2 for x in X2 for z in Z4], 64)
X_FACES = _picks([_at_y(s, x, y, z) for x in (0, 1) for s in S2 for y in Y6 for z in Z4], 96)
Z_FACES = _picks([_at_x(s, x, y, z) for z in (0, 3) for s in S2 for x in X4 for y in Y6], 192)
POOL_OF = _pool_of()
POOL_Y_FACES = _picks([p * 16 + y * 4 + z for y in (0, 3) for p in range(8) for z in Z4], 128)
POOL_GROW_Y = _picks(
    [128 + p * 4 + z if y < 0 else 160 + p * 4 + z if y > 3 else p * 16 + y * 4 + z for p in range(8) for y in Y6 for z in Z4], 192
)
POOL_Z_FACES = _picks([(p * 6 + y) * 4 + z if y < 6 else 192 for z in (0, 3) for p in range(8) for y in range(8)], 193)[:, :192]
PADDED = _picks([_at_z(s, x, y, z) for s in S2 for x in X4 for y in Y6 for z in Z6], 288)


def _dot(a, b, contract=((1,), (0,))):
    return lax.dot_general(a, b, (contract, ((), ())), preferred_element_type=F32)


def _flag(condition):
    return jnp.where(condition, 1.0, 0.0)


def _wide(rows, count):
    return jnp.concatenate([rows[i * count : (i + 1) * count] for i in range(4)], axis=1)


def _call(kernel, outs, *args, scratch=()):
    vmem = pl.BlockSpec(memory_space=pltpu.VMEM)
    return pl.pallas_call(
        kernel,
        out_shape=tuple(jax.ShapeDtypeStruct(shape, kind) for shape, kind in outs),
        in_specs=[pl.BlockSpec(memory_space=pltpu.SMEM)] + [vmem] * (len(args) - 1),
        out_specs=(vmem,) * len(outs),
        scratch_shapes=[pltpu.VMEM(shape, F32) for shape in scratch],
        compiler_params=pltpu.CompilerParams(vmem_limit_bytes=24 * 1024 * 1024),
        cost_estimate=pl.CostEstimate(flops=1_000_000, bytes_accessed=4_000_000, transcendentals=0),
    )(*args)


def _sides(place_index, here, there):
    even = _flag(place_index % 2 == 0)
    here, there = here[...].astype(F32), there[...].astype(F32)
    return there * even + here * (1.0 - even), here * even + there * (1.0 - even)


def _pack(place_index, first, last, here_ref, there_ref):
    even = _flag(place_index % 2 == 0)
    here_ref[...] = (last * even + first * (1.0 - even)).astype(BF16)
    there_ref[...] = (first * even + last * (1.0 - even)).astype(BF16)


def _pool_kernel(place_ref, pool_of_ref, act_ref, cot_ref, pooled_ref, here_ref, there_ref):
    planes = [_dot(pool_of_ref[...], act_ref[g * 128 : (g + 1) * 128, :]) for g in range(4)]
    pooled = jnp.concatenate(planes, axis=0).astype(BF16)
    pooled_ref[...] = pooled

    def face(x):
        fine = [ref[s * 256 + x * 192 : s * 256 + x * 192 + 64, :] for ref in (act_ref, cot_ref) for s in range(2)]
        return jnp.concatenate(fine + [pooled[s * 32 + x * 16 : s * 32 + x * 16 + 16] for s in range(2)], axis=0).astype(F32)

    _pack(place_ref[0], face(0), face(1), here_ref, there_ref)


def _grow_x_kernel(
    place_ref, pool_faces_ref, act_ref, cot_ref, pooled_ref, got_here, got_there,
    act_out, cot_out, pooled_out, here_ref, there_ref,
):
    low, high = _sides(place_ref[0], got_here, got_there)
    firsts, lasts = [], []
    for i, (ref, out) in enumerate(((act_ref, act_out), (cot_ref, cot_out))):
        fine = ref[...].astype(F32)
        parts = []
        for s in range(2):
            at_face = slice(i * 128 + s * 64, i * 128 + s * 64 + 64)
            parts += [low[at_face], fine[s * 256 : (s + 1) * 256], high[at_face]]
        grown = jnp.concatenate(parts, axis=0)
        out[...] = grown
        firsts += [grown[p * 64 : p * 64 + 8] for p in range(12)]
        lasts += [grown[p * 64 + 56 : p * 64 + 64] for p in range(12)]
    pooled = pooled_ref[...].astype(F32)
    parts = []
    for s in range(2):
        at_face = slice(256 + s * 16, 272 + s * 16)
        parts += [low[at_face], pooled[s * 32 : (s + 1) * 32], high[at_face]]
    grown = jnp.concatenate(parts, axis=0).astype(BF16)
    pooled_out[...] = grown
    faces = _dot(pool_faces_ref[...], grown)
    first = jnp.concatenate(firsts + [faces[0:32]], axis=0)
    last = jnp.concatenate(lasts + [faces[32:64]], axis=0)
    _pack(place_ref[2], first, last, here_ref, there_ref)


def _grow_y_kernel(
    place_ref, pool_grow_ref, pool_faces_ref, act_ref, cot_ref, pooled_ref, got_here, got_there,
    act_out, cot_out, pooled_out, here_ref, there_ref,
):
    low, high = _sides(place_ref[2], got_here, got_there)
    firsts, lasts = [], []
    for i, (ref, out) in enumerate(((act_ref, act_out), (cot_ref, cot_out))):
        for p in range(12):
            at_face = slice(i * 96 + p * 8, i * 96 + p * 8 + 8)
            out[p * 80 : p * 80 + 8, :] = low[at_face]
            out[p * 80 + 8 : p * 80 + 72, :] = ref[p * 64 : (p + 1) * 64, :]
            out[p * 80 + 72 : p * 80 + 80, :] = high[at_face]
        firsts.append(out[pl.ds(0, 120, 8), :])
        lasts.append(out[pl.ds(7, 120, 8), :])
    rows = jnp.concatenate([pooled_ref[...], low[192:224].astype(BF16), high[192:224].astype(BF16)], axis=0)
    grown = _dot(pool_grow_ref[...], rows)
    pooled_out[...] = grown
    faces = _dot(pool_faces_ref[...], grown.astype(BF16))
    first = jnp.concatenate(firsts + [faces[0:64]], axis=0)
    last = jnp.concatenate(lasts + [faces[64:128]], axis=0)
    _pack(place_ref[3], first, last, here_ref, there_ref)


def _grow_z_kernel(place_ref, act_ref, got_here, got_there, out_ref, lines):
    low, high = _sides(place_ref[3], got_here, got_there)
    lines[:, 8:16, :] = act_ref[...].reshape(120, 8, 128)
    lines[:, 7:8, :] = low[0:120][:, None, :]
    lines[:, 16:17, :] = high[0:120][:, None, :]
    out_ref[...] = lines[:, 7:17, :].astype(BF16)


def traded(here, there, axis):
    count = lax.axis_size(axis)
    first_pairs = [(i, i ^ 1) for i in range(count)]
    second_pairs = [(i, j) for i in range(count) for j in [((i + 1) ^ 1) - 1] if 0 <= j < count]
    return lax.ppermute(here, axis, first_pairs), lax.ppermute(there, axis, second_pairs)


def extended(place, act, cot):
    rows, f32_rows = lambda n: ((n, 128), BF16), lambda n: ((n, 128), F32)
    pooled, *faces = _call(_pool_kernel, (rows(64), rows(288), rows(288)), place, jnp.asarray(POOL_OF, BF16), act, cot)
    outs = (f32_rows(768), f32_rows(768), rows(128), rows(224), rows(224))
    act, cot, pooled, *faces = _call(
        _grow_x_kernel, outs, place, jnp.asarray(POOL_Y_FACES, BF16), act, cot, pooled, *traded(*faces, "gx")
    )
    outs = (f32_rows(960), f32_rows(960), f32_rows(192), rows(304), rows(304))
    act, cot, pooled, *faces = _call(
        _grow_y_kernel, outs, place, jnp.asarray(POOL_GROW_Y, BF16), jnp.asarray(POOL_Z_FACES, BF16),
        act, cot, pooled, *traded(*faces, ("x", "core")),
    )
    return act, cot, pooled, traded(*faces, "gz")


def _gradients_kernel(
    place_ref, act_ref, cot_ref, pool_ref, got_here, got_there, sel_ref, perm_ref, perm_t_ref, y_faces_ref,
    w_in_hbm, w_back_hbm, w_up_hbm,
    keep_ref, send_ref, coarse_ref, d_act_ref,
    w_in, w_back, w_up, lines, shifted, pooled, spaced, sums, sem_in, sem_out,
):
    loads = [
        pltpu.make_async_copy(source, target, sem_in.at[i])
        for i, (source, target) in enumerate(((w_in_hbm, w_in), (w_up_hbm, w_up), (w_back_hbm, w_back)))
    ]
    for load in loads:
        load.start()
    core = place_ref[2]
    side = (core, 1 - core)

    def put(row, value, stride=1):
        done, count = 0, value.shape[0]
        while done < count:
            first = row + stride * done
            block = first // 496
            here = min(count - done, -((first - 496 * (block + 1)) // stride))
            start = block // 2 * 496 + first % 496
            where = pl.ds(start, here) if stride == 1 else pl.ds(start, here, stride)
            sums[side[block % 2], where, :] = value[done : done + here]
            done += here

    def ship(index, first, last):
        copies = [
            pltpu.make_async_copy(sums.at[i, pl.ds(first, end - first)], target.at[pl.ds(first, end - first)], sem_out.at[index, i])
            for i, (target, end) in enumerate(((keep_ref, min(last, 7936)), (send_ref, last)))
            if end > first
        ]
        for copy in copies:
            copy.start()
        return copies

    low, high = _sides(place_ref[3], got_here, got_there)
    lines[:, 8:16, :] = cot_ref[...].reshape(120, 8, 128)
    lines[:, 7:8, :] = low[120:240][:, None, :]
    lines[:, 16:17, :] = high[120:240][:, None, :]
    for dz in range(3):
        window = lines[:, 7 + dz : 15 + dz, :].reshape(2, 6, 10, 8, 128)
        for dy in range(3):
            u = 8 - 3 * dy - dz
            shifted[:, :, :, u * 128 : (u + 1) * 128] = window[:, :, dy : dy + 8].reshape(2, 6, 64, 128).astype(BF16)

    for g in range(8):
        at_face = slice(240 + g * 8, 248 + g * 8)
        plane = [pool_ref[g * 24 : (g + 1) * 24, :], low[at_face], high[at_face], jnp.zeros((8, 128), F32)]
        picked = _dot(sel_ref[...], jnp.concatenate(plane, axis=0).astype(BF16))
        for u in range(9):
            pooled[g // 4, g % 4, :, u * 128 : (u + 1) * 128] = picked[u * 16 : (u + 1) * 16].astype(BF16)
    loads[0].wait()
    before = jnp.zeros((64, 256), F32)
    for dx in range(3):
        before += _dot(pooled[:, dx : dx + 2].reshape(64, 1152), w_in[dx * 1152 : (dx + 1) * 1152, :])
    squash = 1.0 / (1.0 + jnp.exp(-before))
    bottom32 = (before * squash).astype(BF16).astype(F32)
    bottom = bottom32.astype(BF16)
    loads[1].wait()
    parts = [_dot(bottom, w_up[p * 256 : (p + 1) * 256, :]).astype(BF16) for p in range(8)]
    upward = jnp.concatenate(
        [_dot(perm_ref[...], jnp.concatenate([p[g * 16 : (g + 1) * 16] for p in parts], axis=0)) for g in range(4)], axis=0
    )

    loads[2].wait()
    d_joined = jnp.zeros((512, 256), F32)
    for dx in range(3):
        d_joined += _dot(shifted[:, dx : dx + 4].reshape(512, 1152), w_back[(2 - dx) * 1152 : (3 - dx) * 1152, :])
    d_act_ref[...] = d_joined[:, :128]

    joined_t = jnp.concatenate([act_ref[...].astype(F32).T, upward.T], axis=0).astype(BF16)
    for dx in range(3):
        grad = _dot(joined_t, shifted[:, dx : dx + 4].reshape(512, 1152))
        for u in range(9):
            put(8960 + (18 - 9 * dx + u) * 256, grad[:, u * 128 : (u + 1) * 128])
    copies = ship(0, 4960, 7936)

    d_upward = d_joined[:, 128:].astype(BF16)
    planes = [_dot(perm_t_ref[...], d_upward[g * 128 : (g + 1) * 128]).astype(BF16) for g in range(4)]
    blocks = [jnp.concatenate([plane[p * 16 : (p + 1) * 16] for plane in planes], axis=0) for p in range(8)]
    d_bottom = jnp.zeros((64, 256), F32)
    for p in range(8):
        d_bottom += _dot(blocks[p], w_up[p * 256 : (p + 1) * 256, :], ((1,), (1,)))
    bottom_t = bottom32.T.astype(BF16)
    for p in range(8):
        put(6912 + p * 256, _dot(bottom_t, blocks[p]))
    slope = (d_bottom * squash * (1.0 + before * (1.0 - squash))).astype(BF16)
    coarse = jnp.concatenate([bottom, slope], axis=1)
    coarse_ref[...] = coarse
    faces = _dot(y_faces_ref[...], coarse)
    for lane in range(4):
        sums[1, 7936 + lane * 32 : 7968 + lane * 32, :] = faces[:, lane * 128 : (lane + 1) * 128]
    copies += ship(1, 7936, 8064)

    spaced[...] = jnp.zeros((128, 768), BF16)
    for s in range(2):
        for dx in range(3):
            spaced[s * 64 + dx * 16 : s * 64 + dx * 16 + 32, dx * 256 : (dx + 1) * 256] = slope[s * 32 : (s + 1) * 32]
    for u in range(9):
        picked_t = pooled[:, :, :, u * 128 : (u + 1) * 128].reshape(128, 128).astype(F32).T.astype(BF16)
        grad = _dot(picked_t, spaced[...])
        for dx in range(3):
            for h in range(2):
                put((9 * dx + u) * 256 + h, grad[:, dx * 256 + h * 128 : dx * 256 + (h + 1) * 128], 2)
    copies += ship(2, 0, 4960)
    for copy in copies:
        copy.wait()


def gradients(place, act, cot, pool, got_here, got_there, w_in, w_back, w_up):
    shape = jax.ShapeDtypeStruct
    vmem, hbm = pl.BlockSpec(memory_space=pltpu.VMEM), pl.BlockSpec(memory_space=pltpu.HBM)
    return pl.pallas_call(
        _gradients_kernel,
        out_shape=(
            shape((7936, 128), F32), shape((8064, 128), F32), shape((64, 512), BF16), shape((512, 128), F32),
        ),
        in_specs=[pl.BlockSpec(memory_space=pltpu.SMEM)] + [vmem] * 9 + [hbm] * 3,
        out_specs=(vmem,) * 4,
        scratch_shapes=[
            pltpu.VMEM((3456, 256), BF16), pltpu.VMEM((3456, 256), BF16), pltpu.VMEM((2048, 128), BF16),
            pltpu.VMEM((120, 24, 128), F32), pltpu.VMEM((2, 6, 64, 1152), BF16),
            pltpu.VMEM((2, 4, 16, 1152), BF16), pltpu.VMEM((128, 768), BF16),
            pltpu.VMEM((2, 8064, 128), F32),
            pltpu.SemaphoreType.DMA((3,)), pltpu.SemaphoreType.DMA((3, 2)),
        ],
        compiler_params=pltpu.CompilerParams(vmem_limit_bytes=36 * 1024 * 1024),
        cost_estimate=pl.CostEstimate(flops=2_500_000_000, bytes_accessed=16_000_000, transcendentals=16384),
    )(
        place, act, cot, pool, got_here, got_there,
        jnp.asarray(_select_pooled(), BF16), jnp.asarray(_fine_from_blocks(), BF16), jnp.asarray(_fine_from_blocks().T, BF16),
        jnp.asarray(Y_FACES, BF16), w_in, w_back, w_up,
    )


def at(array, index, axis):
    return lax.dynamic_index_in_dim(array, index, axis, keepdims=False)


def turned(array, axis, shift):
    count = lax.axis_size(axis)
    return lax.ppermute(array, axis, [(i, (i + shift) % count) for i in range(count)])


def paired(array, axis, bit):
    count = lax.axis_size(axis)
    return lax.ppermute(array, axis, [(i, i ^ bit) for i in range(count)])


def _split_kernel(place_ref, keep_ref, got_ref, one_ref, two_ref, faces_ref, *sends):
    for s in range(4):
        rows = [pl.multiple_of(((place_ref[0] + s) % 4 * 4 + j) * 496, 8) for j in range(4)]
        one = jnp.concatenate([keep_ref[pl.ds(r, 248), :] + got_ref[pl.ds(r, 248), :] for r in rows], axis=0)
        rows = [pl.multiple_of((j * 4 + (place_ref[1] + s) % 4) * 496 + 248, 8) for j in range(4)]
        two = jnp.concatenate([keep_ref[pl.ds(r, 248), :] + got_ref[pl.ds(r, 248), :] for r in rows], axis=0)
        if s == 0:
            one_ref[...] = one
            two_ref[...] = two
        else:
            sends[s - 1][...] = one.astype(BF16)
            sends[s + 2][0:992, :] = two.astype(BF16)
    faces = got_ref[7936:8064, :].astype(BF16)
    faces_ref[...] = faces
    for lane in range(4):
        sends[3][992 + lane * 16 : 1008 + lane * 16, :] = faces[lane * 32 + 16 : lane * 32 + 32]
        sends[5][992 + lane * 16 : 1008 + lane * 16, :] = faces[lane * 32 : lane * 32 + 16]


def _second_kernel(
    place_ref, coarse_ref, faces_ref, x_faces_ref, one_ref, one_1, one_2, one_3, two_ref, two_1, two_2, two_3,
    grown_ref, own_one, own_two, send_one_1, send_one_2, send_one_3, send_two_1, send_two_2, send_two_3, one, two,
):
    gx, x, core = place_ref[0], place_ref[1], place_ref[2]
    one[...] = one_ref[...] + (one_1[...].astype(F32) + one_2[...].astype(F32) + one_3[...].astype(F32))
    two[...] = two_ref[...] + (two_1[0:992, :].astype(F32) + two_2[...].astype(F32) + two_3[0:992, :].astype(F32))
    for s, (to_one, to_two) in enumerate(
        ((own_one, own_two), (send_one_1, send_two_1), (send_one_2, send_two_2), (send_one_3, send_two_3))
    ):
        to_one[...] = one[pl.ds(pl.multiple_of((x + s) % 4 * 248, 8), 248), :]
        to_two[0:248, :] = two[pl.ds(pl.multiple_of((gx + s) % 4 * 248, 8), 248), :]
    near = faces_ref[...].astype(F32)
    near_first = jnp.concatenate([near[i * 32 : i * 32 + 16] for i in range(4)], axis=0)
    near_last = jnp.concatenate([near[i * 32 + 16 : i * 32 + 32] for i in range(4)], axis=0)
    low = two_1[992:1056, :].astype(F32) * _flag((core == 0) & (x > 0)) + near_last * _flag(core == 1)
    high = two_3[992:1056, :].astype(F32) * _flag((core == 1) & (x < 3)) + near_first * _flag(core == 0)
    grown = jnp.concatenate([coarse_ref[...], _wide(low, 16).astype(BF16), _wide(high, 16).astype(BF16)], axis=0)
    grown_ref[...] = grown
    faces = _dot(x_faces_ref[...], grown)
    for lane in range(4):
        send_two_1[248 + lane * 48 : 296 + lane * 48, :] = faces[48:96, lane * 128 : (lane + 1) * 128]
        send_two_3[248 + lane * 48 : 296 + lane * 48, :] = faces[0:48, lane * 128 : (lane + 1) * 128]


def _third_kernel(
    place_ref, grown_ref, z_faces_ref, one_ref, one_1, one_2, one_3, two_ref, two_1, two_2, two_3,
    grown_out, keep_ref, send_ref, other_ref, rows, chunks,
):
    gx, gz = place_ref[0], place_ref[3]
    rows[0:248, :] = one_ref[...] + (one_1[...] + one_2[...] + one_3[...])
    rows[248:496, :] = two_ref[...] + (two_1[0:248, :] + two_2[...] + two_3[0:248, :])
    chunks[...] = jnp.zeros((2, 256, 128), F32)
    for r, q, p in itertools.product(range(2), repeat=3):
        chunk, place = 4 * r + 2 * q + p, ((q ^ r) * 2 + r) * 64
        chunks[p ^ r, place : place + 62, :] = rows[chunk * 62 : (chunk + 1) * 62, :]
    half = (gz + gz // 4) % 2
    keep_ref[...] = chunks[half]
    send_ref[0:256, :] = chunks[1 - half]
    low = _wide(two_1[248:440, :] * _flag(gx > 0), 48).astype(BF16)
    high = _wide(two_3[248:440, :] * _flag(gx < 3), 48).astype(BF16)
    grown = jnp.concatenate([grown_ref[...], low, high], axis=0)
    grown_out[...] = grown
    faces = _dot(z_faces_ref[...], grown)
    even = _flag(gz % 2 == 0)
    here = faces[48:96] * even + faces[0:48] * (1.0 - even)
    there = (faces[0:48] * even + faces[48:96] * (1.0 - even)).astype(BF16)
    for lane in range(4):
        send_ref[256 + lane * 48 : 304 + lane * 48, :] = here[:, lane * 128 : (lane + 1) * 128]
        other_ref[lane * 48 : (lane + 1) * 48, :] = there[:, lane * 128 : (lane + 1) * 128]


def _fourth_kernel(place_ref, grown_ref, padded_ref, keep_ref, got_ref, other_ref, bottom_ref, slope_ref, keep_out, send_out, both):
    gz = place_ref[3]
    mine = keep_ref[...] + got_ref[0:256, :]
    both[0] = mine[0:128]
    both[1] = mine[128:256]
    half = (gz // 2 + gz // 4) % 2
    keep_out[...] = both[half]
    send_out[...] = both[1 - half]
    even = _flag(gz % 2 == 0)
    here, there = got_ref[256:448, :], other_ref[...].astype(F32)
    low = _wide(there * even + here * (1.0 - even), 48).astype(BF16)
    high = _wide(here * even + there * (1.0 - even), 48).astype(BF16)
    padded = _dot(padded_ref[...], jnp.concatenate([grown_ref[...], low, high], axis=0)).astype(BF16)
    bottom_ref[...] = padded[:, 0:256]
    slope_ref[...] = padded[:, 256:512]


def scattered_sum(place, keep, send, coarse):
    gz = lax.axis_index("gz")
    half, quarter = ((992, 128), BF16), ((248, 128), F32)
    half_and_faces, quarter_and_faces = ((1056, 128), BF16), ((440, 128), F32)
    got = paired(send, "core", 1)
    outs = (((992, 128), F32),) * 2 + (((128, 128), BF16),) + (half,) * 3 + (half_and_faces, half, half_and_faces)
    one, two, faces, *sends = _call(_split_kernel, outs, place, keep, got)
    got_one = [turned(sends[s - 1], "gx", s) for s in (1, 2, 3)]
    got_two = [turned(sends[s + 2], "x", s) for s in (1, 2, 3)]
    outs = (((96, 512), BF16),) + (quarter,) * 5 + (quarter_and_faces, quarter, quarter_and_faces)
    grown, one, two, *sends = _call(
        _second_kernel, outs, place, coarse, faces, jnp.asarray(X_FACES, BF16), one, *got_one, two, *got_two,
        scratch=((992, 128), (992, 128)),
    )
    got_one = [turned(sends[s - 1], "x", s) for s in (1, 2, 3)]
    got_two = [turned(sends[s + 2], "gx", s) for s in (1, 2, 3)]
    outs = (((192, 512), BF16), ((256, 128), F32), ((448, 128), F32), ((192, 128), BF16))
    grown, keep, send, other = _call(
        _third_kernel, outs, place, grown, jnp.asarray(Z_FACES, BF16), one, *got_one, two, *got_two,
        scratch=((496, 128), (2, 256, 128)),
    )
    got = paired(send, "gz", 1)
    other = lax.ppermute(other, "gz", [(i, j) for i in range(8) for j in [((i + 1) ^ 1) - 1] if 0 <= j < 8])
    outs = (((288, 256), BF16),) * 2 + (((128, 128), F32),) * 2
    bottom_pad, slope_pad, keep, send = _call(
        _fourth_kernel, outs, place, grown, jnp.asarray(PADDED, BF16), keep, got, other, scratch=((2, 128, 128),)
    )
    mine = keep + paired(send, "gz", 2)
    mine = mine + paired(mine, "gz", 7)
    squares = jnp.sum(mine * mine, axis=0, keepdims=True)
    pads = [p.reshape(2, 4, 6, 6, 256) for p in (bottom_pad, slope_pad)]
    return at(mine.reshape(2, 64, 128), gz // 4, 0)[:62], squares, pads


def local(activation, w_in, w_up, w_out, cotangent):
    place = jnp.stack([lax.axis_index(a) for a in ("gx", "x", "core", "gz")]).astype(jnp.int32)
    own = activation.reshape(512, 128)
    act, cot, pooled, faces = extended(place, own, cotangent.reshape(512, 128))
    w_back = w_out.reshape(27, 256, 128).transpose(0, 2, 1).reshape(3456, 256)
    keep, send, coarse, d_direct = gradients(place, own, cot, pooled, *faces, w_in, w_back, w_up)
    mine, total, (bottom_pad, slope_pad) = scattered_sum(place, keep, send, coarse)

    def rounds(value, *others, axis, masks):
        for mask in masks:
            value = value + paired(value, axis, mask)
        return lax.optimization_barrier((value, *others))

    total, bottom_pad, act = rounds(total, bottom_pad, act, axis="core", masks=(1,))
    (active_pad,) = _call(_grow_z_kernel, (((120, 10, 128), BF16),), place, act, *faces, scratch=((120, 24, 128),))
    active_pad = active_pad.reshape(2, 6, 10, 10, 128)
    upward_pad = up_conv(bottom_pad, w_up).astype(BF16)[:, 1:-1, 1:-1, 1:-1]
    joined_pad = jnp.concatenate([active_pad, upward_pad], axis=4)
    total, joined_pad = rounds(total, joined_pad, axis="gx", masks=(1,))
    output = conv_forward(joined_pad, w_out).astype(BF16)
    total, output, slope_pad = rounds(total, output, slope_pad, axis="gx", masks=(3,))
    d_pooled = conv_transpose(slope_pad, w_in)
    d_activation = (d_direct.reshape(activation.shape) + spread(d_pooled) * 0.125).astype(BF16)
    total, d_activation = rounds(total, d_activation, axis="x", masks=(1,))
    (total,) = rounds(total, axis="x", masks=(3,))
    (total,) = rounds(total, axis="gz", masks=(1, 2))
    factor = jnp.minimum(1.0, jnp.sqrt(PARAMS / (jnp.sum(total) + 1e-06)))
    return (output, d_activation, (mine * factor).reshape(-1))


def solution(mesh):
    gx, gy, gz = mesh.devices.shape
    split = Mesh(mesh.devices.reshape(gx, gy // 2, 2, gz), ("gx", "x", "core", "gz"))
    cells = P(None, "gx", ("x", "core"), "gz", None)
    return jax.shard_map(
        local, mesh=split, in_specs=(cells, P(), P(), P(), cells),
        out_specs=(cells, cells, P(("gx", "x", "core", "gz"))), check_vma=False,
    )
```

```python
import itertools

import jax
import jax.numpy as jnp
import numpy as np
from jax import lax
from jax.experimental import pallas as pl
from jax.experimental.pallas import tpu as pltpu
from jax.sharding import Mesh, PartitionSpec as P

F32 = jnp.float32
BF16 = jnp.bfloat16
PARAMS = 2031616


def conv_forward(padded, weight):
    kernel = weight.reshape(3, 3, 3, padded.shape[4], -1)
    return lax.conv_general_dilated(
        padded, kernel, (1, 1, 1), "VALID",
        dimension_numbers=("NXYZC", "XYZIO", "NXYZC"), preferred_element_type=F32,
    )


def conv_transpose(padded, weight):
    kernel = weight.reshape(3, 3, 3, -1, padded.shape[4])[::-1, ::-1, ::-1]
    return lax.conv_general_dilated(
        padded, kernel, (1, 1, 1), "VALID",
        dimension_numbers=("NXYZC", "XYZOI", "NXYZC"), preferred_element_type=F32,
    )


def spread(volume):
    samples, size_x, size_y, size_z, chans = volume.shape
    wide = jnp.broadcast_to(
        volume[:, :, None, :, None, :, None, :], (samples, size_x, 2, size_y, 2, size_z, 2, chans)
    )
    return wide.reshape(samples, 2 * size_x, 2 * size_y, 2 * size_z, chans)


def up_conv(bottom, w_up):
    samples, size_x, size_y, size_z, wide = bottom.shape
    kernel = w_up.reshape(2, 2, 2, wide, -1)
    result = jnp.einsum("sijkc,abeco->siajbkeo", bottom, kernel, preferred_element_type=F32)
    return result.reshape(samples, 2 * size_x, 2 * size_y, 2 * size_z, -1)


def _select_pooled():
    sel = np.zeros((9, 4, 4, 48), np.float32)
    for dy, dz, y, z in itertools.product(range(3), range(3), range(4), range(4)):
        line, k = y + dy, z + dz - 1
        sel[3 * dy + dz, y, z, 24 + line if k < 0 else 32 + line if k > 3 else line * 4 + k] = 1
    return sel.reshape(144, 48)


def _fine_from_blocks():
    perm = np.zeros((128, 128), np.float32)
    for a, y, z in itertools.product(range(2), range(8), range(8)):
        perm[(a * 8 + y) * 8 + z, (a * 4 + (y % 2) * 2 + z % 2) * 16 + (y // 2) * 4 + z // 2] = 1
    return perm


def _picks(sources, width):
    picks = np.zeros((len(sources), width), np.float32)
    picks[np.arange(len(sources)), sources] = 1
    return picks


def _at_y(s, x, y, z):
    line = s * 2 + x
    return 64 + line * 4 + z if y < 0 else 80 + line * 4 + z if y > 3 else (line * 4 + y) * 4 + z


def _at_x(s, x, y, z):
    if 0 <= x <= 1:
        return _at_y(s, x, y, z)
    base = 96 if x < 0 else 144
    return base + (s * 4 + y) * 4 + z if 0 <= y <= 3 else base + 32 + (s * 2 + int(y > 3)) * 4 + z


def _at_z(s, x, y, z):
    line = (s * 4 + x + 1) * 6 + y + 1
    return 192 + line if z < 0 else 240 + line if z > 3 else _at_x(s, x, y, z)


S2, X2, Y4, Z4 = range(2), range(2), range(4), range(4)
X4, Y6, Z6 = range(-1, 3), range(-1, 5), range(-1, 5)
Y_FACES = _picks([_at_y(s, x, y, z) for y in (0, 3) for s in S2 for x in X2 for z in Z4], 64)
X_EDGES = _picks([e * 16 + (s * 2 + x) * 4 + z for x in (0, 1) for s in S2 for e in range(2) for z in Z4], 32)
Z_FACES = _picks([_at_x(s, x, y, z) for z in (0, 3) for s in S2 for x in X4 for y in Y6], 192)
PADDED = _picks([_at_z(s, x, y, z) for s in S2 for x in X4 for y in Y6 for z in Z6], 288)


def _dot(a, b, contract=((1,), (0,))):
    return lax.dot_general(a, b, (contract, ((), ())), preferred_element_type=F32)


def _flag(condition):
    return jnp.where(condition, 1.0, 0.0)


def _wide(rows, count):
    return jnp.concatenate([rows[i * count : (i + 1) * count] for i in range(4)], axis=1)


def _call(kernel, outs, *args, scratch=()):
    vmem = pl.BlockSpec(memory_space=pltpu.VMEM)
    return pl.pallas_call(
        kernel,
        out_shape=tuple(jax.ShapeDtypeStruct(shape, kind) for shape, kind in outs),
        in_specs=[pl.BlockSpec(memory_space=pltpu.SMEM)] + [vmem] * (len(args) - 1),
        out_specs=(vmem,) * len(outs),
        scratch_shapes=[pltpu.VMEM(shape, F32) for shape in scratch],
        compiler_params=pltpu.CompilerParams(vmem_limit_bytes=24 * 1024 * 1024),
        cost_estimate=pl.CostEstimate(flops=1_000_000, bytes_accessed=4_000_000, transcendentals=0),
    )(*args)


def _sides(place_index, here, there):
    even = _flag(place_index % 2 == 0)
    here, there = here[...].astype(F32), there[...].astype(F32)
    return there * even + here * (1.0 - even), here * even + there * (1.0 - even)


def _pack(place_index, first, last, here_ref, there_ref):
    even = _flag(place_index % 2 == 0)
    here_ref[...] = (last * even + first * (1.0 - even)).astype(BF16)
    there_ref[...] = (first * even + last * (1.0 - even)).astype(BF16)


def _table(rows, columns, chosen, value=1.0):
    row = lax.broadcasted_iota(jnp.int32, (rows, columns), 0)
    column = lax.broadcasted_iota(jnp.int32, (rows, columns), 1)
    return jnp.where(chosen(row, column), value, 0.0).astype(BF16)


def _pool_of(r, c):
    return (((c >> 4) & 3) == (r >> 2)) & (((c >> 1) & 3) == (r & 3))


def _pool_y_faces(r, c):
    return c == ((r >> 2) & 7) * 16 + (r >> 5) * 12 + (r & 3)


def _pool_grow_y(r, c):
    plane = (r * 2731) >> 16
    y, z = (r - plane * 24) >> 2, r & 3
    inside = plane * 16 + (y - 1) * 4 + z
    return c == jnp.where(y == 0, 128 + plane * 4 + z, jnp.where(y == 5, 160 + plane * 4 + z, inside))


def _pool_z_faces(r, c):
    y = r & 7
    return (c == (((r >> 3) & 7) * 6 + y) * 4 + (r >> 6) * 3) & (y < 6)


def _pool_kernel(place_ref, act_ref, cot_ref, act_out, cot_out, pooled_ref, here_ref, there_ref):
    act_out[...] = act_ref[...]
    cot_out[...] = cot_ref[...]
    pool_of = _table(16, 128, _pool_of, 0.125)
    planes = [_dot(pool_of, act_ref[g * 128 : (g + 1) * 128, :]) for g in range(4)]
    pooled = jnp.concatenate(planes, axis=0).astype(BF16)
    pooled_ref[...] = pooled

    def face(x):
        fine = [ref[s * 256 + x * 192 : s * 256 + x * 192 + 64, :] for ref in (act_ref, cot_ref) for s in range(2)]
        return jnp.concatenate(fine + [pooled[s * 32 + x * 16 : s * 32 + x * 16 + 16] for s in range(2)], axis=0).astype(F32)

    _pack(place_ref[0], face(0), face(1), here_ref, there_ref)


def _grow_x_kernel(
    place_ref, act_ref, cot_ref, pooled_ref, got_here, got_there,
    act_out, cot_out, pooled_out, here_ref, there_ref,
):
    low, high = _sides(place_ref[0], got_here, got_there)
    firsts, lasts = [], []
    for i, (ref, out) in enumerate(((act_ref, act_out), (cot_ref, cot_out))):
        fine = ref[...].astype(F32)
        parts = []
        for s in range(2):
            at_face = slice(i * 128 + s * 64, i * 128 + s * 64 + 64)
            parts += [low[at_face], fine[s * 256 : (s + 1) * 256], high[at_face]]
        grown = jnp.concatenate(parts, axis=0)
        out[...] = grown
        firsts += [grown[p * 64 : p * 64 + 8] for p in range(12)]
        lasts += [grown[p * 64 + 56 : p * 64 + 64] for p in range(12)]
    pooled = pooled_ref[...].astype(F32)
    parts = []
    for s in range(2):
        at_face = slice(256 + s * 16, 272 + s * 16)
        parts += [low[at_face], pooled[s * 32 : (s + 1) * 32], high[at_face]]
    grown = jnp.concatenate(parts, axis=0).astype(BF16)
    pooled_out[...] = grown
    faces = _dot(_table(64, 128, _pool_y_faces), grown)
    first = jnp.concatenate(firsts + [faces[0:32]], axis=0)
    last = jnp.concatenate(lasts + [faces[32:64]], axis=0)
    _pack(place_ref[2], first, last, here_ref, there_ref)


def _grow_y_kernel(
    place_ref, act_ref, cot_ref, pooled_ref, got_here, got_there,
    act_out, cot_out, pooled_out, here_ref, there_ref, act_lines,
):
    low, high = _sides(place_ref[2], got_here, got_there)
    firsts, lasts = [], []
    for i, (ref, out) in enumerate(((act_ref, act_lines), (cot_ref, cot_out))):
        for p in range(12):
            at_face = slice(i * 96 + p * 8, i * 96 + p * 8 + 8)
            out[p * 80 : p * 80 + 8, :] = low[at_face]
            out[p * 80 + 8 : p * 80 + 72, :] = ref[p * 64 : (p + 1) * 64, :]
            out[p * 80 + 72 : p * 80 + 80, :] = high[at_face]
        firsts.append(out[pl.ds(0, 120, 8), :])
        lasts.append(out[pl.ds(7, 120, 8), :])
    rows = jnp.concatenate([pooled_ref[...], low[192:224].astype(BF16), high[192:224].astype(BF16)], axis=0)
    act_out[...] = act_lines[...].astype(BF16)
    grown = _dot(_table(192, 192, _pool_grow_y), rows)
    pooled_out[...] = grown
    faces = _dot(_table(128, 192, _pool_z_faces), grown.astype(BF16))
    first = jnp.concatenate(firsts + [faces[0:64]], axis=0)
    last = jnp.concatenate(lasts + [faces[64:128]], axis=0)
    _pack(place_ref[3], first, last, here_ref, there_ref)


def _grow_z_kernel(place_ref, act_ref, got_here, got_there, out_ref, lines):
    low, high = _sides(place_ref[3], got_here, got_there)
    lines[:, 8:16, :] = act_ref[...].astype(F32).reshape(120, 8, 128)
    lines[:, 7:8, :] = low[0:120][:, None, :]
    lines[:, 16:17, :] = high[0:120][:, None, :]
    out_ref[...] = lines[:, 7:17, :].astype(BF16)


def traded(here, there, axis):
    count = lax.axis_size(axis)
    first_pairs = [(i, i ^ 1) for i in range(count)]
    second_pairs = [(i, j) for i in range(count) for j in [((i + 1) ^ 1) - 1] if 0 <= j < count]
    return lax.ppermute(here, axis, first_pairs), lax.ppermute(there, axis, second_pairs)


def extended(place, act, cot):
    rows, f32_rows = lambda n: ((n, 128), BF16), lambda n: ((n, 128), F32)
    own, cot, pooled, *faces = _call(_pool_kernel, (rows(512), rows(512), rows(64), rows(288), rows(288)), place, act, cot)
    outs = (f32_rows(768), f32_rows(768), rows(128), rows(224), rows(224))
    act, cot, pooled, *faces = _call(_grow_x_kernel, outs, place, own, cot, pooled, *traded(*faces, "gx"))
    outs = (rows(960), f32_rows(960), f32_rows(192), rows(304), rows(304))
    act, cot, pooled, *faces = _call(
        _grow_y_kernel, outs, place, act, cot, pooled, *traded(*faces, ("x", "core")), scratch=((960, 128),)
    )
    return own, act, cot, pooled, traded(*faces, "gz")


def _gradients_kernel(
    place_ref, act_ref, cot_ref, pool_ref, got_here, got_there, sel_ref, perm_ref, perm_t_ref, y_faces_ref,
    w_in_hbm, w_back_hbm, w_up_hbm,
    keep_ref, send_ref, coarse_ref, d_act_ref,
    w_in, w_back, w_up, lines, shifted, pooled, spaced, sums, sem_in, sem_out,
):
    loads = [
        pltpu.make_async_copy(source, target, sem_in.at[i])
        for i, (source, target) in enumerate(((w_in_hbm, w_in), (w_up_hbm, w_up), (w_back_hbm, w_back)))
    ]
    for load in loads:
        load.start()
    core = place_ref[2]
    side = (core, 1 - core)

    def put(row, value, stride=1):
        done, count = 0, value.shape[0]
        while done < count:
            first = row + stride * done
            block = first // 496
            here = min(count - done, -((first - 496 * (block + 1)) // stride))
            start = block // 2 * 496 + first % 496
            where = pl.ds(start, here) if stride == 1 else pl.ds(start, here, stride)
            sums[side[block % 2], where, :] = value[done : done + here]
            done += here

    def ship(index, first, last):
        copy = pltpu.make_async_copy(sums.at[0, pl.ds(first, last - first)], keep_ref.at[pl.ds(first, last - first)], sem_out.at[index])
        copy.start()
        send_ref[first:last, :] = sums[1, first:last, :].astype(BF16)
        return copy

    low, high = _sides(place_ref[3], got_here, got_there)
    lines[:, 8:16, :] = cot_ref[...].reshape(120, 8, 128)
    lines[:, 7:8, :] = low[120:240][:, None, :]
    lines[:, 16:17, :] = high[120:240][:, None, :]
    for dz in range(3):
        window = lines[:, 7 + dz : 15 + dz, :].reshape(2, 6, 10, 8, 128)
        for dy in range(3):
            u = 8 - 3 * dy - dz
            shifted[:, :, :, u * 128 : (u + 1) * 128] = window[:, :, dy : dy + 8].reshape(2, 6, 64, 128).astype(BF16)

    for g in range(8):
        at_face = slice(240 + g * 8, 248 + g * 8)
        plane = [pool_ref[g * 24 : (g + 1) * 24, :], low[at_face], high[at_face], jnp.zeros((8, 128), F32)]
        picked = _dot(sel_ref[...], jnp.concatenate(plane, axis=0).astype(BF16))
        for u in range(9):
            pooled[g // 4, g % 4, :, u * 128 : (u + 1) * 128] = picked[u * 16 : (u + 1) * 16].astype(BF16)
    loads[0].wait()
    before = jnp.zeros((64, 256), F32)
    for dx in range(3):
        before += _dot(pooled[:, dx : dx + 2].reshape(64, 1152), w_in[dx * 1152 : (dx + 1) * 1152, :])
    squash = 1.0 / (1.0 + jnp.exp(-before))
    bottom32 = (before * squash).astype(BF16).astype(F32)
    bottom = bottom32.astype(BF16)
    loads[1].wait()
    parts = [_dot(bottom, w_up[p * 256 : (p + 1) * 256, :]).astype(BF16) for p in range(8)]
    upward = jnp.concatenate(
        [_dot(perm_ref[...], jnp.concatenate([p[g * 16 : (g + 1) * 16] for p in parts], axis=0)) for g in range(4)], axis=0
    )

    loads[2].wait()
    d_joined = jnp.zeros((512, 256), F32)
    for dx in range(3):
        d_joined += _dot(shifted[:, dx : dx + 4].reshape(512, 1152), w_back[(2 - dx) * 1152 : (3 - dx) * 1152, :])
    d_act_ref[...] = d_joined[:, :128]

    joined_t = jnp.concatenate([act_ref[...].astype(F32).T, upward.T], axis=0).astype(BF16)
    for dx in range(3):
        grad = _dot(joined_t, shifted[:, dx : dx + 4].reshape(512, 1152))
        for u in range(9):
            put(8960 + (18 - 9 * dx + u) * 256, grad[:, u * 128 : (u + 1) * 128])
    copies = [ship(0, 4960, 7936)]

    d_upward = d_joined[:, 128:].astype(BF16)
    planes = [_dot(perm_t_ref[...], d_upward[g * 128 : (g + 1) * 128]).astype(BF16) for g in range(4)]
    blocks = [jnp.concatenate([plane[p * 16 : (p + 1) * 16] for plane in planes], axis=0) for p in range(8)]
    d_bottom = jnp.zeros((64, 256), F32)
    for p in range(8):
        d_bottom += _dot(blocks[p], w_up[p * 256 : (p + 1) * 256, :], ((1,), (1,)))
    bottom_t = bottom32.T.astype(BF16)
    for p in range(8):
        put(6912 + p * 256, _dot(bottom_t, blocks[p]))
    slope = (d_bottom * squash * (1.0 + before * (1.0 - squash))).astype(BF16)
    coarse = jnp.concatenate([bottom, slope], axis=1)
    coarse_ref[...] = coarse
    faces = _dot(y_faces_ref[...], coarse)
    for lane in range(4):
        send_ref[7936 + lane * 32 : 7968 + lane * 32, :] = faces[:, lane * 128 : (lane + 1) * 128].astype(BF16)

    spaced[...] = jnp.zeros((128, 768), BF16)
    for s in range(2):
        for dx in range(3):
            spaced[s * 64 + dx * 16 : s * 64 + dx * 16 + 32, dx * 256 : (dx + 1) * 256] = slope[s * 32 : (s + 1) * 32]
    for u in range(9):
        picked_t = pooled[:, :, :, u * 128 : (u + 1) * 128].reshape(128, 128).astype(F32).T.astype(BF16)
        grad = _dot(picked_t, spaced[...])
        for dx in range(3):
            for h in range(2):
                put((9 * dx + u) * 256 + h, grad[:, dx * 256 + h * 128 : dx * 256 + (h + 1) * 128], 2)
    copies.append(ship(1, 0, 4960))
    for copy in copies:
        copy.wait()


def gradients(place, act, cot, pool, got_here, got_there, w_in, w_back, w_up):
    shape = jax.ShapeDtypeStruct
    vmem, hbm = pl.BlockSpec(memory_space=pltpu.VMEM), pl.BlockSpec(memory_space=pltpu.HBM)
    return pl.pallas_call(
        _gradients_kernel,
        out_shape=(
            shape((7936, 128), F32), shape((8064, 128), BF16), shape((64, 512), BF16), shape((512, 128), F32),
        ),
        in_specs=[pl.BlockSpec(memory_space=pltpu.SMEM)] + [vmem] * 9 + [hbm] * 3,
        out_specs=(vmem,) * 4,
        scratch_shapes=[
            pltpu.VMEM((3456, 256), BF16), pltpu.VMEM((3456, 256), BF16), pltpu.VMEM((2048, 128), BF16),
            pltpu.VMEM((120, 24, 128), F32), pltpu.VMEM((2, 6, 64, 1152), BF16),
            pltpu.VMEM((2, 4, 16, 1152), BF16), pltpu.VMEM((128, 768), BF16),
            pltpu.VMEM((2, 7936, 128), F32),
            pltpu.SemaphoreType.DMA((3,)), pltpu.SemaphoreType.DMA((2,)),
        ],
        compiler_params=pltpu.CompilerParams(vmem_limit_bytes=32 * 1024 * 1024),
        cost_estimate=pl.CostEstimate(flops=2_500_000_000, bytes_accessed=16_000_000, transcendentals=16384),
    )(
        place, act, cot, pool, got_here, got_there,
        jnp.asarray(_select_pooled(), BF16), jnp.asarray(_fine_from_blocks(), BF16), jnp.asarray(_fine_from_blocks().T, BF16),
        jnp.asarray(Y_FACES, BF16), w_in, w_back, w_up,
    )


def turned(array, axis, shift):
    count = lax.axis_size(axis)
    return lax.ppermute(array, axis, [(i, (i + shift) % count) for i in range(count)])


def paired(array, axis, bit):
    count = lax.axis_size(axis)
    return lax.ppermute(array, axis, [(i, i ^ bit) for i in range(count)])


def _split_kernel(place_ref, keep_ref, got_ref, coarse_ref, one_ref, two_ref, faces_ref, *sends):
    for s in range(4):
        rows = [pl.multiple_of(((place_ref[0] + s) % 4 * 4 + j) * 496, 16) for j in range(4)]
        one = jnp.concatenate([keep_ref[pl.ds(r, 248), :] + got_ref[pl.ds(r, 256), :].astype(F32)[:248] for r in rows], axis=0)
        rows = [pl.multiple_of((j * 4 + (place_ref[1] + s) % 4) * 496 + 240, 16) for j in range(4)]
        two = jnp.concatenate([keep_ref[pl.ds(r + 8, 248), :] + got_ref[pl.ds(r, 256), :].astype(F32)[8:] for r in rows], axis=0)
        if s == 0:
            one_ref[...] = one
            two_ref[...] = two
        else:
            sends[s - 1][0:992, :] = one.astype(BF16)
            sends[s + 2][0:992, :] = two.astype(BF16)
    faces = got_ref[7936:8064, :]
    faces_ref[...] = faces
    for lane in range(4):
        sends[3][992 + lane * 16 : 1008 + lane * 16, :] = faces[lane * 32 + 16 : lane * 32 + 32]
        sends[5][992 + lane * 16 : 1008 + lane * 16, :] = faces[lane * 32 : lane * 32 + 16]
        for s in range(2):
            start, channels = 992 + lane * 32 + s * 16, slice(lane * 128, (lane + 1) * 128)
            sends[0][start : start + 16, :] = coarse_ref[s * 32 + 16 : s * 32 + 32, channels]
            sends[2][start : start + 16, :] = coarse_ref[s * 32 : s * 32 + 16, channels]


def _second_one_kernel(place_ref, one_ref, got_1, got_2, got_3, own, send_1, send_2, send_3, one):
    one[...] = one_ref[...] + (got_1[0:992, :].astype(F32) + got_2[...].astype(F32) + got_3[0:992, :].astype(F32))
    for s, out in enumerate((own, send_1, send_2, send_3)):
        out[...] = one[pl.ds(pl.multiple_of((place_ref[1] + s) % 4 * 248, 8), 248), :]


def _second_two_kernel(
    place_ref, faces_ref, x_edges_ref, two_ref, got_1, got_2, got_3, sides_ref, own, send_1, send_2, send_3, two
):
    x, core = place_ref[1], place_ref[2]
    two[...] = two_ref[...] + (got_1[0:992, :].astype(F32) + got_2[...].astype(F32) + got_3[0:992, :].astype(F32))
    for s, out in enumerate((own, send_1, send_2, send_3)):
        out[0:248, :] = two[pl.ds(pl.multiple_of((place_ref[0] + s) % 4 * 248, 8), 248), :]
    near = faces_ref[...].astype(F32)
    near_first = jnp.concatenate([near[i * 32 : i * 32 + 16] for i in range(4)], axis=0)
    near_last = jnp.concatenate([near[i * 32 + 16 : i * 32 + 32] for i in range(4)], axis=0)
    low = got_1[992:1056, :].astype(F32) * _flag((core == 0) & (x > 0)) + near_last * _flag(core == 1)
    high = got_3[992:1056, :].astype(F32) * _flag((core == 1) & (x < 3)) + near_first * _flag(core == 0)
    sides = jnp.concatenate([_wide(low, 16).astype(BF16), _wide(high, 16).astype(BF16)], axis=0)
    sides_ref[...] = sides
    edges = _dot(x_edges_ref[...], sides)
    for lane in range(4):
        send_1[248 + lane * 16 : 264 + lane * 16, :] = edges[16:32, lane * 128 : (lane + 1) * 128]
        send_3[248 + lane * 16 : 264 + lane * 16, :] = edges[0:16, lane * 128 : (lane + 1) * 128]


def _third_kernel(
    place_ref, coarse_ref, sides_ref, x_low, x_high, z_faces_ref, one_ref, one_1, one_2, one_3, two_ref, two_1, two_2, two_3,
    grown_out, keep_ref, send_ref, other_ref, rows, chunks,
):
    gx, gz = place_ref[0], place_ref[3]
    rows[0:248, :] = one_ref[...] + (one_1[...] + one_2[...] + one_3[...])
    rows[248:496, :] = two_ref[...] + (two_1[0:248, :] + two_2[...] + two_3[0:248, :])
    chunks[...] = jnp.zeros((2, 256, 128), F32)
    for r, q, p in itertools.product(range(2), repeat=3):
        chunk, place = 4 * r + 2 * q + p, ((q ^ r) * 2 + r) * 64
        chunks[p ^ r, place : place + 62, :] = rows[chunk * 62 : (chunk + 1) * 62, :]
    half = (gz + gz // 4) % 2
    keep_ref[...] = chunks[half]
    send_ref[0:256, :] = chunks[1 - half]
    grown = [coarse_ref[...], sides_ref[...]]
    for cells, edges, there in ((x_low, two_1, _flag(gx > 0)), (x_high, two_3, _flag(gx < 3))):
        grown.append(_wide(cells[992:1120, :].astype(F32) * there, 32).astype(BF16))
        grown.append(_wide(edges[248:312, :] * there, 16).astype(BF16))
    grown = jnp.concatenate(grown, axis=0)
    grown_out[...] = grown
    faces = _dot(z_faces_ref[...], grown)
    even = _flag(gz % 2 == 0)
    here = faces[48:96] * even + faces[0:48] * (1.0 - even)
    there = (faces[0:48] * even + faces[48:96] * (1.0 - even)).astype(BF16)
    for lane in range(4):
        send_ref[256 + lane * 48 : 304 + lane * 48, :] = here[:, lane * 128 : (lane + 1) * 128]
        other_ref[lane * 48 : (lane + 1) * 48, :] = there[:, lane * 128 : (lane + 1) * 128]


def _fourth_kernel(place_ref, keep_ref, got_ref, keep_out, send_out, both):
    gz = place_ref[3]
    mine = keep_ref[...] + got_ref[0:256, :]
    both[0] = mine[0:128]
    both[1] = mine[128:256]
    half = (gz // 2 + gz // 4) % 2
    keep_out[...] = both[half]
    send_out[...] = both[1 - half]


def _pad_kernel(place_ref, grown_ref, padded_ref, got_ref, other_ref, bottom_ref, slope_ref):
    even = _flag(place_ref[3] % 2 == 0)
    here, there = got_ref[256:448, :], other_ref[...].astype(F32)
    low = _wide(there * even + here * (1.0 - even), 48).astype(BF16)
    high = _wide(here * even + there * (1.0 - even), 48).astype(BF16)
    padded = _dot(padded_ref[...], jnp.concatenate([grown_ref[...], low, high], axis=0)).astype(BF16)
    bottom_ref[...] = padded[:, 0:256]
    slope_ref[...] = padded[:, 256:512]


def _clip_kernel(place_ref, total_ref, both_ref, out_ref):
    total = jnp.sum(total_ref[...], axis=1, keepdims=True)
    factor = jnp.minimum(1.0, jnp.sqrt(PARAMS / (total + 1e-06)))
    out_ref[...] = both_ref[pl.ds(pl.multiple_of(place_ref[3] // 4 * 64, 64), 62), :] * factor


def scattered_sum(place, keep, send, coarse):
    def f32_rows(n):
        return ((n, 128), F32)

    def rows(n):
        return ((n, 128), BF16)

    got = paired(send, "core", 1)
    outs = (f32_rows(992), f32_rows(992), rows(128), rows(1120), rows(992), rows(1120), rows(1056), rows(992), rows(1056))
    one, two, faces, *sends = _call(_split_kernel, outs, place, keep, got, coarse)
    got_one = [turned(sends[s - 1], "gx", s) for s in (1, 2, 3)]
    got_two = [turned(sends[s + 2], "x", s) for s in (1, 2, 3)]
    one, *sends_one = _call(_second_one_kernel, (f32_rows(248),) * 4, place, one, *got_one, scratch=((992, 128),))
    x_low, x_high = got_one[0], got_one[2]
    got_one = [turned(sends_one[s - 1], "x", s) for s in (1, 2, 3)]
    outs = (((32, 512), BF16), f32_rows(248), f32_rows(312), f32_rows(248), f32_rows(312))
    sides, two, *sends_two = _call(
        _second_two_kernel, outs, place, faces, jnp.asarray(X_EDGES, BF16), two, *got_two, scratch=((992, 128),)
    )
    got_two = [turned(sends_two[s - 1], "gx", s) for s in (1, 2, 3)]
    outs = (((192, 512), BF16), f32_rows(256), f32_rows(448), rows(192))
    grown, keep, send, other = _call(
        _third_kernel, outs, place, coarse, sides, x_low, x_high, jnp.asarray(Z_FACES, BF16), one, *got_one, two, *got_two,
        scratch=((496, 128), (2, 256, 128)),
    )
    got = paired(send, "gz", 1)
    other = lax.ppermute(other, "gz", [(i, j) for i in range(8) for j in [((i + 1) ^ 1) - 1] if 0 <= j < 8])
    keep, send = _call(_fourth_kernel, (f32_rows(128),) * 2, place, keep, got, scratch=((2, 128, 128),))
    pads = _call(_pad_kernel, (((288, 256), BF16),) * 2, place, grown, jnp.asarray(PADDED, BF16), got, other)
    return keep, send, [p.reshape(2, 4, 6, 6, 256) for p in pads]


def local(activation, w_in, w_up, w_out, cotangent):
    place = jnp.stack([lax.axis_index(a) for a in ("gx", "x", "core", "gz")]).astype(jnp.int32)
    own, act, cot, pooled, faces = extended(place, activation.reshape(512, 128), cotangent.reshape(512, 128))
    w_back = w_out.reshape(27, 256, 128).transpose(0, 2, 1).reshape(3456, 256)
    keep, send, coarse, d_direct = gradients(place, own, cot, pooled, *faces, w_in, w_back, w_up)
    keep, send, (bottom_pad, slope_pad) = scattered_sum(place, keep, send, coarse)

    (active_pad,) = _call(_grow_z_kernel, (((120, 10, 128), BF16),), place, act, *faces, scratch=((120, 24, 128),))
    upward_pad = up_conv(bottom_pad, w_up).astype(BF16)[:, 1:-1, 1:-1, 1:-1]
    joined_pad = jnp.concatenate([active_pad.reshape(2, 6, 10, 10, 128), upward_pad], axis=4)
    mine = keep + paired(send, "gz", 2)
    mine, joined_pad, slope_pad = lax.optimization_barrier((mine, joined_pad, slope_pad))

    output = conv_forward(joined_pad, w_out).astype(BF16)
    mine = mine + paired(mine, "gz", 7)
    total = jnp.sum(mine * mine, axis=0, keepdims=True)
    total = total + paired(total, "core", 1)
    total, output, slope_pad = lax.optimization_barrier((total, output, slope_pad))

    d_pooled = conv_transpose(slope_pad, w_in)
    d_activation = (d_direct.reshape(activation.shape) + spread(d_pooled) * 0.125).astype(BF16)
    total = total + paired(total, "gx", 1)
    total = total + paired(total, "gx", 3)
    total, d_activation = lax.optimization_barrier((total, d_activation))
    for axis, mask in (("x", 1), ("x", 3), ("gz", 1), ("gz", 2)):
        total = total + paired(total, axis, mask)
    (clipped,) = _call(_clip_kernel, (((62, 128), F32),), place, total, mine)
    return (output, d_activation, clipped.reshape(-1))


def solution(mesh):
    gx, gy, gz = mesh.devices.shape
    split = Mesh(mesh.devices.reshape(gx, gy // 2, 2, gz), ("gx", "x", "core", "gz"))
    cells = P(None, "gx", ("x", "core"), "gz", None)
    return jax.shard_map(
        local, mesh=split, in_specs=(cells, P(), P(), P(), cells),
        out_specs=(cells, cells, P(("gx", "x", "core", "gz"))), check_vma=False,
    )
```

```python
import itertools

import jax
import jax.numpy as jnp
import numpy as np
from jax import lax
from jax.experimental import pallas as pl
from jax.experimental.pallas import tpu as pltpu
from jax.sharding import Mesh, PartitionSpec as P

F32 = jnp.float32
BF16 = jnp.bfloat16
PARAMS = 2031616


def conv_forward(padded, weight):
    kernel = weight.reshape(3, 3, 3, padded.shape[4], -1)
    return lax.conv_general_dilated(
        padded, kernel, (1, 1, 1), "VALID",
        dimension_numbers=("NXYZC", "XYZIO", "NXYZC"), preferred_element_type=F32,
    )


def conv_transpose(padded, weight):
    kernel = weight.reshape(3, 3, 3, -1, padded.shape[4])[::-1, ::-1, ::-1]
    return lax.conv_general_dilated(
        padded, kernel, (1, 1, 1), "VALID",
        dimension_numbers=("NXYZC", "XYZOI", "NXYZC"), preferred_element_type=F32,
    )


def spread(volume):
    samples, size_x, size_y, size_z, chans = volume.shape
    wide = jnp.broadcast_to(
        volume[:, :, None, :, None, :, None, :], (samples, size_x, 2, size_y, 2, size_z, 2, chans)
    )
    return wide.reshape(samples, 2 * size_x, 2 * size_y, 2 * size_z, chans)


def up_conv(bottom, w_up):
    samples, size_x, size_y, size_z, wide = bottom.shape
    kernel = w_up.reshape(2, 2, 2, wide, -1)
    result = jnp.einsum("sijkc,abeco->siajbkeo", bottom, kernel, preferred_element_type=F32)
    return result.reshape(samples, 2 * size_x, 2 * size_y, 2 * size_z, -1)


def _picks(sources, width):
    picks = np.zeros((len(sources), width), np.float32)
    picks[np.arange(len(sources)), sources] = 1
    return picks


def _at_y(s, x, y, z):
    line = s * 2 + x
    return 64 + line * 4 + z if y < 0 else 80 + line * 4 + z if y > 3 else (line * 4 + y) * 4 + z


def _at_x(s, x, y, z):
    if 0 <= x <= 1:
        return _at_y(s, x, y, z)
    base = 96 if x < 0 else 144
    return base + (s * 4 + y) * 4 + z if 0 <= y <= 3 else base + 32 + (s * 2 + int(y > 3)) * 4 + z


def _at_z(s, x, y, z):
    line = (s * 4 + x + 1) * 6 + y + 1
    return 192 + line if z < 0 else 240 + line if z > 3 else _at_x(s, x, y, z)


S2, X4, Y6, Z6 = range(2), range(-1, 3), range(-1, 5), range(-1, 5)
Z_FACES = _picks([_at_x(s, x, y, z) for z in (0, 3) for s in S2 for x in X4 for y in Y6], 192)
PADDED = _picks([_at_z(s, x, y, z) for s in S2 for x in X4 for y in Y6 for z in Z6], 288)


def _dot(a, b, contract=((1,), (0,))):
    return lax.dot_general(a, b, (contract, ((), ())), preferred_element_type=F32)


def _flag(condition):
    return jnp.where(condition, 1.0, 0.0)


def _wide(rows, count):
    return jnp.concatenate([rows[i * count : (i + 1) * count] for i in range(4)], axis=1)


def _call(kernel, outs, *args, scratch=()):
    vmem = pl.BlockSpec(memory_space=pltpu.VMEM)
    return pl.pallas_call(
        kernel,
        out_shape=tuple(jax.ShapeDtypeStruct(shape, kind) for shape, kind in outs),
        in_specs=[pl.BlockSpec(memory_space=pltpu.SMEM)] + [vmem] * (len(args) - 1),
        out_specs=(vmem,) * len(outs),
        scratch_shapes=[pltpu.VMEM(shape, F32) for shape in scratch],
        compiler_params=pltpu.CompilerParams(vmem_limit_bytes=12 * 1024 * 1024),
        cost_estimate=pl.CostEstimate(flops=1_000_000, bytes_accessed=4_000_000, transcendentals=0),
    )(*args)


def _sides(place_index, here, there):
    even = _flag(place_index % 2 == 0)
    here, there = here[...].astype(F32), there[...].astype(F32)
    return there * even + here * (1.0 - even), here * even + there * (1.0 - even)


def _pack(place_index, first, last, here_ref, there_ref):
    even = _flag(place_index % 2 == 0)
    here_ref[...] = (last * even + first * (1.0 - even)).astype(BF16)
    there_ref[...] = (first * even + last * (1.0 - even)).astype(BF16)


def _table(rows, columns, chosen, value=1.0):
    row = lax.broadcasted_iota(jnp.int32, (rows, columns), 0)
    column = lax.broadcasted_iota(jnp.int32, (rows, columns), 1)
    return jnp.where(chosen(row, column), value, 0.0).astype(BF16)


def _pool_of(r, c):
    return (((c >> 4) & 3) == (r >> 2)) & (((c >> 1) & 3) == (r & 3))


def _pool_y_faces(r, c):
    return c == ((r >> 2) & 7) * 16 + (r >> 5) * 12 + (r & 3)


def _pool_grow_y(r, c):
    plane = (r * 2731) >> 16
    y, z = (r - plane * 24) >> 2, r & 3
    inside = plane * 16 + (y - 1) * 4 + z
    return c == jnp.where(y == 0, 128 + plane * 4 + z, jnp.where(y == 5, 160 + plane * 4 + z, inside))


def _pool_z_faces(r, c):
    y = r & 7
    return (c == (((r >> 3) & 7) * 6 + y) * 4 + (r >> 6) * 3) & (y < 6)


def _pool_windows(r, c):
    u = r >> 4
    dy = (u * 11) >> 5
    line, k = ((r >> 2) & 3) + dy, (r & 3) + u - 3 * dy - 1
    return c == jnp.where(k < 0, 24 + line, jnp.where(k > 3, 32 + line, line * 4 + k))


def _fine_from_blocks(r, c):
    part = (r >> 6) * 4 + ((r >> 3) & 1) * 2 + (r & 1)
    return c == part * 16 + ((r >> 4) & 3) * 4 + ((r >> 1) & 3)


def _blocks_from_fine(r, c):
    return _fine_from_blocks(c, r)


def _y_faces(r, c):
    return c == (((r >> 2) & 3) * 4 + (r >> 4) * 3) * 4 + (r & 3)


def _x_edges(r, c):
    return c == ((r >> 2) & 1) * 16 + (((r >> 3) & 1) * 2 + (r >> 4)) * 4 + (r & 3)


def _pool_kernel(place_ref, both_ref, act_out, cot_out, pooled_ref, here_ref, there_ref):
    act_out[...] = both_ref[0:512, :]
    cot_out[...] = both_ref[512:1024, :]
    pool_of = _table(16, 128, _pool_of, 0.125)
    planes = [_dot(pool_of, both_ref[g * 128 : (g + 1) * 128, :]) for g in range(4)]
    pooled = jnp.concatenate(planes, axis=0).astype(BF16)
    pooled_ref[...] = pooled

    def face(x):
        fine = [both_ref[s * 256 + x * 192 : s * 256 + x * 192 + 64, :] for s in range(4)]
        return jnp.concatenate(fine + [pooled[s * 32 + x * 16 : s * 32 + x * 16 + 16] for s in range(2)], axis=0).astype(F32)

    _pack(place_ref[0], face(0), face(1), here_ref, there_ref)


def _grow_x_kernel(
    place_ref, act_ref, cot_ref, pooled_ref, got_here, got_there,
    act_out, cot_out, pooled_out, here_ref, there_ref,
):
    low, high = _sides(place_ref[0], got_here, got_there)
    firsts, lasts = [], []
    for i, (ref, out) in enumerate(((act_ref, act_out), (cot_ref, cot_out))):
        fine = ref[...].astype(F32)
        parts = []
        for s in range(2):
            at_face = slice(i * 128 + s * 64, i * 128 + s * 64 + 64)
            parts += [low[at_face], fine[s * 256 : (s + 1) * 256], high[at_face]]
        grown = jnp.concatenate(parts, axis=0)
        out[...] = grown
        firsts += [grown[p * 64 : p * 64 + 8] for p in range(12)]
        lasts += [grown[p * 64 + 56 : p * 64 + 64] for p in range(12)]
    pooled = pooled_ref[...].astype(F32)
    parts = []
    for s in range(2):
        at_face = slice(256 + s * 16, 272 + s * 16)
        parts += [low[at_face], pooled[s * 32 : (s + 1) * 32], high[at_face]]
    grown = jnp.concatenate(parts, axis=0).astype(BF16)
    pooled_out[...] = grown
    faces = _dot(_table(64, 128, _pool_y_faces), grown)
    first = jnp.concatenate(firsts + [faces[0:32]], axis=0)
    last = jnp.concatenate(lasts + [faces[32:64]], axis=0)
    _pack(place_ref[2], first, last, here_ref, there_ref)


def _grow_y_kernel(
    place_ref, act_ref, cot_ref, pooled_ref, got_here, got_there,
    act_out, cot_out, pooled_out, here_ref, there_ref, act_lines, cot_lines,
):
    low, high = _sides(place_ref[2], got_here, got_there)
    firsts, lasts = [], []
    for i, (ref, out) in enumerate(((act_ref, act_lines), (cot_ref, cot_lines))):
        for p in range(12):
            at_face = slice(i * 96 + p * 8, i * 96 + p * 8 + 8)
            out[p * 80 : p * 80 + 8, :] = low[at_face]
            out[p * 80 + 8 : p * 80 + 72, :] = ref[p * 64 : (p + 1) * 64, :]
            out[p * 80 + 72 : p * 80 + 80, :] = high[at_face]
        firsts.append(out[pl.ds(0, 120, 8), :])
        lasts.append(out[pl.ds(7, 120, 8), :])
    rows = jnp.concatenate([pooled_ref[...], low[192:224].astype(BF16), high[192:224].astype(BF16)], axis=0)
    act_out[...] = act_lines[...].astype(BF16)
    cot_out[...] = cot_lines[...].astype(BF16)
    grown = _dot(_table(192, 192, _pool_grow_y), rows)
    pooled_out[...] = grown
    faces = _dot(_table(128, 192, _pool_z_faces), grown.astype(BF16))
    first = jnp.concatenate(firsts + [faces[0:64]], axis=0)
    last = jnp.concatenate(lasts + [faces[64:128]], axis=0)
    _pack(place_ref[3], first, last, here_ref, there_ref)


def _grow_z_kernel(place_ref, act_ref, got_here, got_there, out_ref, lines):
    low, high = _sides(place_ref[3], got_here, got_there)
    lines[:, 8:16, :] = act_ref[...].astype(F32).reshape(120, 8, 128)
    lines[:, 7:8, :] = low[0:120][:, None, :]
    lines[:, 16:17, :] = high[0:120][:, None, :]
    out_ref[...] = lines[:, 7:17, :].astype(BF16)


def traded(here, there, axis):
    count = lax.axis_size(axis)
    first_pairs = [(i, i ^ 1) for i in range(count)]
    second_pairs = [(i, j) for i in range(count) for j in [((i + 1) ^ 1) - 1] if 0 <= j < count]
    return lax.ppermute(here, axis, first_pairs), lax.ppermute(there, axis, second_pairs)


def extended(place, both):
    rows, f32_rows = lambda n: ((n, 128), BF16), lambda n: ((n, 128), F32)
    own, cot, pooled, *faces = _call(_pool_kernel, (rows(512), rows(512), rows(64), rows(288), rows(288)), place, both)
    outs = (f32_rows(768), f32_rows(768), rows(128), rows(224), rows(224))
    act, cot, pooled, *faces = _call(_grow_x_kernel, outs, place, own, cot, pooled, *traded(*faces, "gx"))
    outs = (rows(960), rows(960), f32_rows(192), rows(304), rows(304))
    act, cot, pooled, *faces = _call(
        _grow_y_kernel, outs, place, act, cot, pooled, *traded(*faces, ("x", "core")), scratch=((960, 128),) * 2
    )
    return own, act, cot, pooled, traded(*faces, "gz")


def _gradients_kernel(
    place_ref, act_ref, cot_ref, pool_ref, got_here, got_there,
    w_in_hbm, w_back_hbm, w_up_hbm,
    keep_ref, send_ref, coarse_ref, d_act_ref,
    w_in, w_back, w_up, lines, shifted, pooled, spaced, sums, sem_in, sem_out,
):
    loads = [
        pltpu.make_async_copy(source, target, sem_in.at[i])
        for i, (source, target) in enumerate(((w_in_hbm, w_in), (w_up_hbm, w_up), (w_back_hbm, w_back)))
    ]
    for load in loads:
        load.start()
    core = place_ref[2]
    side = (core, 1 - core)

    def put(row, value, stride=1):
        done, count = 0, value.shape[0]
        while done < count:
            first = row + stride * done
            block = first // 496
            here = min(count - done, -((first - 496 * (block + 1)) // stride))
            start = block // 2 * 496 + first % 496
            where = pl.ds(start, here) if stride == 1 else pl.ds(start, here, stride)
            sums[side[block % 2], where, :] = value[done : done + here]
            done += here

    def ship(index, first, last):
        copy = pltpu.make_async_copy(sums.at[0, pl.ds(first, last - first)], keep_ref.at[pl.ds(first, last - first)], sem_out.at[index])
        copy.start()
        send_ref[first:last, :] = sums[1, first:last, :].astype(BF16)
        return copy

    low, high = _sides(place_ref[3], got_here, got_there)
    lines[:, 8:16, :] = cot_ref[...].astype(F32).reshape(120, 8, 128)
    lines[:, 7:8, :] = low[120:240][:, None, :]
    lines[:, 16:17, :] = high[120:240][:, None, :]
    for dz in range(3):
        window = lines[:, 7 + dz : 15 + dz, :].reshape(2, 6, 10, 8, 128)
        for dy in range(3):
            u = 8 - 3 * dy - dz
            shifted[:, :, :, u * 128 : (u + 1) * 128] = window[:, :, dy : dy + 8].reshape(2, 6, 64, 128).astype(BF16)

    windows = _table(144, 48, _pool_windows)
    for g in range(8):
        at_face = slice(240 + g * 8, 248 + g * 8)
        plane = [pool_ref[g * 24 : (g + 1) * 24, :], low[at_face], high[at_face], jnp.zeros((8, 128), F32)]
        picked = _dot(windows, jnp.concatenate(plane, axis=0).astype(BF16))
        for u in range(9):
            pooled[g // 4, g % 4, :, u * 128 : (u + 1) * 128] = picked[u * 16 : (u + 1) * 16].astype(BF16)
    loads[0].wait()
    before = jnp.zeros((64, 256), F32)
    for dx in range(3):
        before += _dot(pooled[:, dx : dx + 2].reshape(64, 1152), w_in[dx * 1152 : (dx + 1) * 1152, :])
    squash = 1.0 / (1.0 + jnp.exp(-before))
    bottom32 = (before * squash).astype(BF16).astype(F32)
    bottom = bottom32.astype(BF16)
    loads[1].wait()
    parts = [_dot(bottom, w_up[p * 256 : (p + 1) * 256, :]).astype(BF16) for p in range(8)]
    perm = _table(128, 128, _fine_from_blocks)
    upward = jnp.concatenate(
        [_dot(perm, jnp.concatenate([p[g * 16 : (g + 1) * 16] for p in parts], axis=0)) for g in range(4)], axis=0
    )

    loads[2].wait()
    d_joined = jnp.zeros((512, 256), F32)
    for dx in range(3):
        d_joined += _dot(shifted[:, dx : dx + 4].reshape(512, 1152), w_back[(2 - dx) * 1152 : (3 - dx) * 1152, :])
    d_act_ref[...] = d_joined[:, :128]

    joined_t = jnp.concatenate([act_ref[...].astype(F32).T, upward.T], axis=0).astype(BF16)
    for dx in range(3):
        grad = _dot(joined_t, shifted[:, dx : dx + 4].reshape(512, 1152))
        for u in range(9):
            put(8960 + (18 - 9 * dx + u) * 256, grad[:, u * 128 : (u + 1) * 128])
    copies = [ship(0, 4960, 7936)]

    d_upward = d_joined[:, 128:].astype(BF16)
    perm = _table(128, 128, _blocks_from_fine)
    planes = [_dot(perm, d_upward[g * 128 : (g + 1) * 128]).astype(BF16) for g in range(4)]
    blocks = [jnp.concatenate([plane[p * 16 : (p + 1) * 16] for plane in planes], axis=0) for p in range(8)]
    d_bottom = jnp.zeros((64, 256), F32)
    for p in range(8):
        d_bottom += _dot(blocks[p], w_up[p * 256 : (p + 1) * 256, :], ((1,), (1,)))
    bottom_t = bottom32.T.astype(BF16)
    for p in range(8):
        put(6912 + p * 256, _dot(bottom_t, blocks[p]))
    slope = (d_bottom * squash * (1.0 + before * (1.0 - squash))).astype(BF16)
    coarse = jnp.concatenate([bottom, slope], axis=1)
    coarse_ref[...] = coarse
    faces = _dot(_table(32, 64, _y_faces), coarse)
    for lane in range(4):
        send_ref[7936 + lane * 32 : 7968 + lane * 32, :] = faces[:, lane * 128 : (lane + 1) * 128].astype(BF16)

    spaced[...] = jnp.zeros((128, 768), BF16)
    for s in range(2):
        for dx in range(3):
            spaced[s * 64 + dx * 16 : s * 64 + dx * 16 + 32, dx * 256 : (dx + 1) * 256] = slope[s * 32 : (s + 1) * 32]
    for u in range(9):
        picked_t = pooled[:, :, :, u * 128 : (u + 1) * 128].reshape(128, 128).astype(F32).T.astype(BF16)
        grad = _dot(picked_t, spaced[...])
        for dx in range(3):
            for h in range(2):
                put((9 * dx + u) * 256 + h, grad[:, dx * 256 + h * 128 : dx * 256 + (h + 1) * 128], 2)
    copies.append(ship(1, 0, 4960))
    for copy in copies:
        copy.wait()


def gradients(place, act, cot, pool, got_here, got_there, w_in, w_back, w_up):
    shape = jax.ShapeDtypeStruct
    vmem, hbm = pl.BlockSpec(memory_space=pltpu.VMEM), pl.BlockSpec(memory_space=pltpu.HBM)
    return pl.pallas_call(
        _gradients_kernel,
        out_shape=(
            shape((7936, 128), F32), shape((8064, 128), BF16), shape((64, 512), BF16), shape((512, 128), F32),
        ),
        in_specs=[pl.BlockSpec(memory_space=pltpu.SMEM)] + [vmem] * 5 + [hbm] * 3,
        out_specs=(vmem,) * 4,
        scratch_shapes=[
            pltpu.VMEM((3456, 256), BF16), pltpu.VMEM((3456, 256), BF16), pltpu.VMEM((2048, 128), BF16),
            pltpu.VMEM((120, 24, 128), F32), pltpu.VMEM((2, 6, 64, 1152), BF16),
            pltpu.VMEM((2, 4, 16, 1152), BF16), pltpu.VMEM((128, 768), BF16),
            pltpu.VMEM((2, 7936, 128), F32),
            pltpu.SemaphoreType.DMA((3,)), pltpu.SemaphoreType.DMA((2,)),
        ],
        compiler_params=pltpu.CompilerParams(vmem_limit_bytes=26 * 1024 * 1024),
        cost_estimate=pl.CostEstimate(flops=2_500_000_000, bytes_accessed=16_000_000, transcendentals=16384),
    )(
        place, act, cot, pool, got_here, got_there,
        w_in, w_back, w_up,
    )


def turned(array, axis, shift):
    count = lax.axis_size(axis)
    return lax.ppermute(array, axis, [(i, (i + shift) % count) for i in range(count)])


def paired(array, axis, bit):
    count = lax.axis_size(axis)
    return lax.ppermute(array, axis, [(i, i ^ bit) for i in range(count)])


def _split_kernel(place_ref, keep_ref, got_ref, coarse_ref, one_ref, two_ref, faces_ref, *sends):
    for s in range(4):
        rows = [pl.multiple_of(((place_ref[0] + s) % 4 * 4 + j) * 496, 16) for j in range(4)]
        one = jnp.concatenate([keep_ref[pl.ds(r, 248), :] + got_ref[pl.ds(r, 256), :].astype(F32)[:248] for r in rows], axis=0)
        rows = [pl.multiple_of((j * 4 + (place_ref[1] + s) % 4) * 496 + 240, 16) for j in range(4)]
        two = jnp.concatenate([keep_ref[pl.ds(r + 8, 248), :] + got_ref[pl.ds(r, 256), :].astype(F32)[8:] for r in rows], axis=0)
        if s == 0:
            one_ref[...] = one
            two_ref[...] = two
        else:
            sends[s - 1][0:992, :] = one.astype(BF16)
            sends[s + 2][0:992, :] = two.astype(BF16)
    faces = got_ref[7936:8064, :]
    faces_ref[...] = faces
    for lane in range(4):
        sends[3][992 + lane * 16 : 1008 + lane * 16, :] = faces[lane * 32 + 16 : lane * 32 + 32]
        sends[5][992 + lane * 16 : 1008 + lane * 16, :] = faces[lane * 32 : lane * 32 + 16]
        for s in range(2):
            start, channels = 992 + lane * 32 + s * 16, slice(lane * 128, (lane + 1) * 128)
            sends[0][start : start + 16, :] = coarse_ref[s * 32 + 16 : s * 32 + 32, channels]
            sends[2][start : start + 16, :] = coarse_ref[s * 32 : s * 32 + 16, channels]


def _second_one_kernel(place_ref, one_ref, got_1, got_2, got_3, own, send_1, send_2, send_3, one):
    one[...] = one_ref[...] + (got_1[0:992, :].astype(F32) + got_2[...].astype(F32) + got_3[0:992, :].astype(F32))
    for s, out in enumerate((own, send_1, send_2, send_3)):
        out[...] = one[pl.ds(pl.multiple_of((place_ref[1] + s) % 4 * 248, 8), 248), :]


def _second_two_kernel(
    place_ref, faces_ref, two_ref, got_1, got_2, got_3, sides_ref, own, send_1, send_2, send_3, two
):
    x, core = place_ref[1], place_ref[2]
    two[...] = two_ref[...] + (got_1[0:992, :].astype(F32) + got_2[...].astype(F32) + got_3[0:992, :].astype(F32))
    for s, out in enumerate((own, send_1, send_2, send_3)):
        out[0:248, :] = two[pl.ds(pl.multiple_of((place_ref[0] + s) % 4 * 248, 8), 248), :]
    near = faces_ref[...].astype(F32)
    near_first = jnp.concatenate([near[i * 32 : i * 32 + 16] for i in range(4)], axis=0)
    near_last = jnp.concatenate([near[i * 32 + 16 : i * 32 + 32] for i in range(4)], axis=0)
    low = got_1[992:1056, :].astype(F32) * _flag((core == 0) & (x > 0)) + near_last * _flag(core == 1)
    high = got_3[992:1056, :].astype(F32) * _flag((core == 1) & (x < 3)) + near_first * _flag(core == 0)
    sides = jnp.concatenate([_wide(low, 16).astype(BF16), _wide(high, 16).astype(BF16)], axis=0)
    sides_ref[...] = sides
    edges = _dot(_table(32, 32, _x_edges), sides)
    for lane in range(4):
        send_1[248 + lane * 16 : 264 + lane * 16, :] = edges[16:32, lane * 128 : (lane + 1) * 128]
        send_3[248 + lane * 16 : 264 + lane * 16, :] = edges[0:16, lane * 128 : (lane + 1) * 128]


def _third_kernel(
    place_ref, coarse_ref, sides_ref, x_low, x_high, z_faces_ref, one_ref, one_1, one_2, one_3, two_ref, two_1, two_2, two_3,
    grown_out, keep_ref, send_ref, other_ref, rows, chunks,
):
    gx, gz = place_ref[0], place_ref[3]
    rows[0:248, :] = one_ref[...] + (one_1[...] + one_2[...] + one_3[...])
    rows[248:496, :] = two_ref[...] + (two_1[0:248, :] + two_2[...] + two_3[0:248, :])
    chunks[...] = jnp.zeros((2, 256, 128), F32)
    for r, q, p in itertools.product(range(2), repeat=3):
        chunk, place = 4 * r + 2 * q + p, ((q ^ r) * 2 + r) * 64
        chunks[p ^ r, place : place + 62, :] = rows[chunk * 62 : (chunk + 1) * 62, :]
    half = (gz + gz // 4) % 2
    keep_ref[...] = chunks[half]
    send_ref[0:256, :] = chunks[1 - half]
    grown = [coarse_ref[...], sides_ref[...]]
    for cells, edges, there in ((x_low, two_1, _flag(gx > 0)), (x_high, two_3, _flag(gx < 3))):
        grown.append(_wide(cells[992:1120, :].astype(F32) * there, 32).astype(BF16))
        grown.append(_wide(edges[248:312, :] * there, 16).astype(BF16))
    grown = jnp.concatenate(grown, axis=0)
    grown_out[...] = grown
    faces = _dot(z_faces_ref[...], grown)
    even = _flag(gz % 2 == 0)
    here = faces[48:96] * even + faces[0:48] * (1.0 - even)
    there = (faces[0:48] * even + faces[48:96] * (1.0 - even)).astype(BF16)
    for lane in range(4):
        send_ref[256 + lane * 48 : 304 + lane * 48, :] = here[:, lane * 128 : (lane + 1) * 128]
        other_ref[lane * 48 : (lane + 1) * 48, :] = there[:, lane * 128 : (lane + 1) * 128]


def _fourth_kernel(place_ref, keep_ref, got_ref, keep_out, send_out, both):
    gz = place_ref[3]
    mine = keep_ref[...] + got_ref[0:256, :]
    both[0] = mine[0:128]
    both[1] = mine[128:256]
    half = (gz // 2 + gz // 4) % 2
    keep_out[...] = both[half]
    send_out[...] = both[1 - half]


def _pad_kernel(place_ref, grown_ref, padded_ref, got_ref, other_ref, bottom_ref, slope_ref):
    even = _flag(place_ref[3] % 2 == 0)
    here, there = got_ref[256:448, :], other_ref[...].astype(F32)
    low = _wide(there * even + here * (1.0 - even), 48).astype(BF16)
    high = _wide(here * even + there * (1.0 - even), 48).astype(BF16)
    padded = _dot(padded_ref[...], jnp.concatenate([grown_ref[...], low, high], axis=0)).astype(BF16)
    bottom_ref[...] = padded[:, 0:256]
    slope_ref[...] = padded[:, 256:512]


def _clip_kernel(place_ref, total_ref, both_ref, out_ref):
    total = jnp.sum(total_ref[...], axis=1, keepdims=True)
    factor = jnp.minimum(1.0, jnp.sqrt(PARAMS / (total + 1e-06)))
    out_ref[...] = both_ref[pl.ds(pl.multiple_of(place_ref[3] // 4 * 64, 64), 62), :] * factor


def scattered_sum(place, keep, send, coarse):
    def f32_rows(n):
        return ((n, 128), F32)

    def rows(n):
        return ((n, 128), BF16)

    got = paired(send, "core", 1)
    outs = (f32_rows(992), f32_rows(992), rows(128), rows(1120), rows(992), rows(1120), rows(1056), rows(992), rows(1056))
    one, two, faces, *sends = _call(_split_kernel, outs, place, keep, got, coarse)
    got_one = [turned(sends[s - 1], "gx", s) for s in (1, 2, 3)]
    got_two = [turned(sends[s + 2], "x", s) for s in (1, 2, 3)]
    one, *sends_one = _call(_second_one_kernel, (f32_rows(248),) * 4, place, one, *got_one, scratch=((992, 128),))
    x_low, x_high = got_one[0], got_one[2]
    got_one = [turned(sends_one[s - 1], "x", s) for s in (1, 2, 3)]
    outs = (((32, 512), BF16), f32_rows(248), f32_rows(312), f32_rows(248), f32_rows(312))
    sides, two, *sends_two = _call(
        _second_two_kernel, outs, place, faces, two, *got_two, scratch=((992, 128),)
    )
    got_two = [turned(sends_two[s - 1], "gx", s) for s in (1, 2, 3)]
    outs = (((192, 512), BF16), f32_rows(256), f32_rows(448), rows(192))
    grown, keep, send, other = _call(
        _third_kernel, outs, place, coarse, sides, x_low, x_high, jnp.asarray(Z_FACES, BF16), one, *got_one, two, *got_two,
        scratch=((496, 128), (2, 256, 128)),
    )
    got = paired(send, "gz", 1)
    other = lax.ppermute(other, "gz", [(i, j) for i in range(8) for j in [((i + 1) ^ 1) - 1] if 0 <= j < 8])
    keep, send = _call(_fourth_kernel, (f32_rows(128),) * 2, place, keep, got, scratch=((2, 128, 128),))
    return keep, send, grown, got, other


def local(activation, w_in, w_up, w_out, cotangent):
    place = jnp.stack([lax.axis_index(a) for a in ("gx", "x", "core", "gz")]).astype(jnp.int32)
    both = jnp.concatenate([activation.reshape(512, 128), cotangent.reshape(512, 128)], axis=0)
    own, act, cot, pooled, faces = extended(place, both)
    w_back = w_out.reshape(27, 256, 128).transpose(0, 2, 1).reshape(3456, 256)
    keep, send, coarse, d_direct = gradients(place, own, cot, pooled, *faces, w_in, w_back, w_up)
    keep, send, grown, got, other = scattered_sum(place, keep, send, coarse)

    send, grown, act = lax.optimization_barrier((send, grown, act))
    mine = keep + paired(send, "gz", 2)
    pads = _call(_pad_kernel, (((288, 256), BF16),) * 2, place, grown, jnp.asarray(PADDED, BF16), got, other)
    bottom_pad, slope_pad = (p.reshape(2, 4, 6, 6, 256) for p in pads)
    (active_pad,) = _call(_grow_z_kernel, (((120, 10, 128), BF16),), place, act, *faces, scratch=((120, 24, 128),))
    upward_pad = up_conv(bottom_pad, w_up).astype(BF16)[:, 1:-1, 1:-1, 1:-1]
    joined_pad = jnp.concatenate([active_pad.reshape(2, 6, 10, 10, 128), upward_pad], axis=4)
    mine, joined_pad, slope_pad = lax.optimization_barrier((mine, joined_pad, slope_pad))

    output_0 = conv_forward(joined_pad[:1], w_out).astype(BF16)
    mine = mine + paired(mine, "gz", 7)
    total = jnp.sum(mine * mine, axis=0, keepdims=True)
    total, output_0, joined_pad = lax.optimization_barrier((total, output_0, joined_pad))
    total = total + paired(total, "core", 1)
    total, joined_pad = lax.optimization_barrier((total, joined_pad))
    output_1 = conv_forward(joined_pad[1:], w_out).astype(BF16)
    total = total + paired(total, "gx", 1)
    total, output_1, slope_pad = lax.optimization_barrier((total, output_1, slope_pad))
    d_pooled = conv_transpose(slope_pad, w_in)
    d_activation = (d_direct.reshape(activation.shape) + spread(d_pooled) * 0.125).astype(BF16)
    total = total + paired(total, "gx", 3)
    total, d_activation = lax.optimization_barrier((total, d_activation))
    output = jnp.concatenate([output_0, output_1], axis=0)
    for axis, mask in (("x", 1), ("x", 3), ("gz", 1), ("gz", 2)):
        total = total + paired(total, axis, mask)
    (clipped,) = _call(_clip_kernel, (((62, 128), F32),), place, total, mine)
    return (output, d_activation, clipped.reshape(-1))


def solution(mesh):
    gx, gy, gz = mesh.devices.shape
    split = Mesh(mesh.devices.reshape(gx, gy // 2, 2, gz), ("gx", "x", "core", "gz"))
    cells = P(None, "gx", ("x", "core"), "gz", None)
    return jax.shard_map(
        local, mesh=split, in_specs=(cells, P(), P(), P(), cells),
        out_specs=(cells, cells, P(("gx", "x", "core", "gz"))), check_vma=False,
    )
```

```python
import itertools

import jax
import jax.numpy as jnp
import numpy as np
from jax import lax
from jax.experimental import pallas as pl
from jax.experimental.pallas import tpu as pltpu
from jax.sharding import Mesh, PartitionSpec as P

F32 = jnp.float32
BF16 = jnp.bfloat16
PARAMS = 2031616


def conv_forward(padded, weight):
    kernel = weight.reshape(3, 3, 3, padded.shape[4], -1)
    return lax.conv_general_dilated(
        padded, kernel, (1, 1, 1), "VALID",
        dimension_numbers=("NXYZC", "XYZIO", "NXYZC"), preferred_element_type=F32,
    )


def conv_transpose(padded, weight):
    kernel = weight.reshape(3, 3, 3, -1, padded.shape[4])[::-1, ::-1, ::-1]
    return lax.conv_general_dilated(
        padded, kernel, (1, 1, 1), "VALID",
        dimension_numbers=("NXYZC", "XYZOI", "NXYZC"), preferred_element_type=F32,
    )


def spread(volume):
    samples, size_x, size_y, size_z, chans = volume.shape
    wide = jnp.broadcast_to(
        volume[:, :, None, :, None, :, None, :], (samples, size_x, 2, size_y, 2, size_z, 2, chans)
    )
    return wide.reshape(samples, 2 * size_x, 2 * size_y, 2 * size_z, chans)


def up_conv(bottom, w_up):
    samples, size_x, size_y, size_z, wide = bottom.shape
    kernel = w_up.reshape(2, 2, 2, wide, -1)
    result = jnp.einsum("sijkc,abeco->siajbkeo", bottom, kernel, preferred_element_type=F32)
    return result.reshape(samples, 2 * size_x, 2 * size_y, 2 * size_z, -1)


def _picks(sources, width):
    picks = np.zeros((len(sources), width), np.float32)
    picks[np.arange(len(sources)), sources] = 1
    return picks


LINES = [(s * 4 + x) * 6 + y for s in range(2) for x in range(4) for y in range(6)]
Z_FACES = _picks([line * 4 + z for z in (0, 3) for line in LINES], 192)
PADDED = _picks([192 + n if z < 0 else 240 + n if z > 3 else n * 4 + z for n in LINES for z in range(-1, 5)], 288)


def _dot(a, b, contract=((1,), (0,))):
    return lax.dot_general(a, b, (contract, ((), ())), preferred_element_type=F32)


def _flag(condition):
    return jnp.where(condition, 1.0, 0.0)


def _wide(rows, count):
    return jnp.concatenate([rows[i * count : (i + 1) * count] for i in range(4)], axis=1)


def _call(kernel, outs, *args, scratch=()):
    vmem = pl.BlockSpec(memory_space=pltpu.VMEM)
    return pl.pallas_call(
        kernel,
        out_shape=tuple(jax.ShapeDtypeStruct(shape, kind) for shape, kind in outs),
        in_specs=[pl.BlockSpec(memory_space=pltpu.SMEM)] + [vmem] * (len(args) - 1),
        out_specs=(vmem,) * len(outs),
        scratch_shapes=[pltpu.VMEM(shape, F32) for shape in scratch],
        compiler_params=pltpu.CompilerParams(vmem_limit_bytes=12 * 1024 * 1024),
        cost_estimate=pl.CostEstimate(flops=1_000_000, bytes_accessed=4_000_000, transcendentals=0),
    )(*args)


def _sides(place_index, here, there):
    even = _flag(place_index % 2 == 0)
    here, there = here[...].astype(F32), there[...].astype(F32)
    return there * even + here * (1.0 - even), here * even + there * (1.0 - even)


def _pack(place_index, first, last, here_ref, there_ref):
    even = _flag(place_index % 2 == 0)
    here_ref[...] = (last * even + first * (1.0 - even)).astype(BF16)
    there_ref[...] = (first * even + last * (1.0 - even)).astype(BF16)


def _table(rows, columns, chosen, value=1.0):
    row = lax.broadcasted_iota(jnp.int32, (rows, columns), 0)
    column = lax.broadcasted_iota(jnp.int32, (rows, columns), 1)
    return jnp.where(chosen(row, column), value, 0.0).astype(BF16)


def _pool_of(r, c):
    return (((c >> 4) & 3) == (r >> 2)) & (((c >> 1) & 3) == (r & 3))


def _pool_y_faces(r, c):
    return c == ((r >> 2) & 7) * 16 + (r >> 5) * 12 + (r & 3)


def _pool_grow_y(r, c):
    plane = (r * 2731) >> 16
    y, z = (r - plane * 24) >> 2, r & 3
    inside = plane * 16 + (y - 1) * 4 + z
    return c == jnp.where(y == 0, 128 + plane * 4 + z, jnp.where(y == 5, 160 + plane * 4 + z, inside))


def _pool_z_faces(r, c):
    y = r & 7
    return (c == (((r >> 3) & 7) * 6 + y) * 4 + (r >> 6) * 3) & (y < 6)


def _pool_windows(r, c):
    u = r >> 4
    dy = (u * 11) >> 5
    line, k = ((r >> 2) & 3) + dy, (r & 3) + u - 3 * dy - 1
    return c == jnp.where(k < 0, 24 + line, jnp.where(k > 3, 32 + line, line * 4 + k))


def _fine_from_blocks(r, c):
    part = (r >> 6) * 4 + ((r >> 3) & 1) * 2 + (r & 1)
    return c == part * 16 + ((r >> 4) & 3) * 4 + ((r >> 1) & 3)


def _blocks_from_fine(r, c):
    return _fine_from_blocks(c, r)


NOWHERE = 9999


def _chip_cell(s, x, y, z):
    return (y >> 2) * 64 + ((s * 2 + x) * 4 + (y & 3)) * 4 + z


def _first_faces(core, last):
    def chosen(r, c):
        x_face = _chip_cell(r >> 5, last, (r >> 2) & 7, r & 3)
        y_face = jnp.where(r < 16, _chip_cell((r >> 3) & 1, (r >> 2) & 1, last * 7, r & 3), NOWHERE)
        return c == x_face * (1 - core) + y_face * core

    return chosen


def _second_faces(core, last):
    def chosen(r, c):
        s, x, z = r >> 4, ((r >> 2) & 3) - 1, r & 3
        side = s * 32 + last * 28 + z
        y_face = jnp.where(x < 0, 128 + side, jnp.where(x > 1, 192 + side, _chip_cell(s, x, last * 7, z)))
        y_face = jnp.where(r < 32, y_face, NOWHERE)
        s = jnp.where(r < 24, 0, 1)
        y, z = ((r - s * 24) >> 2) + 3, r & 3
        x_face = jnp.where(y > 7, 192 + (s * 2 + last) * 4 + z, _chip_cell(s, last, y, z))
        return c == y_face * (1 - core) + x_face * core

    return chosen


def _grown_cells(core):
    def chosen(r, c):
        plane = (r * 2731) >> 16
        y, z = (r - plane * 24) >> 2, r & 3
        s, x = plane >> 2, (plane & 3) - 1
        side = s * 32 + (y - 1) * 4 + z
        low = jnp.where(x < 0, 128 + side, jnp.where(x > 1, 192 + side, _chip_cell(s, x, y - 1, z)))
        low = jnp.where(y == 0, 256 + s * 16 + (x + 1) * 4 + z, low)
        side = s * 24 + y * 4 + z
        high = jnp.where(y == 5, 192 + (s * 2 + x) * 4 + z, _chip_cell(s, x, y + 3, z))
        high = jnp.where(x < 0, 256 + side, jnp.where(x > 1, 304 + side, high))
        return c == low * (1 - core) + high * core

    return chosen


def _pool_kernel(place_ref, both_ref, act_out, cot_out, pooled_ref, here_ref, there_ref):
    act_out[...] = both_ref[0:512, :]
    cot_out[...] = both_ref[512:1024, :]
    pool_of = _table(16, 128, _pool_of, 0.125)
    planes = [_dot(pool_of, both_ref[g * 128 : (g + 1) * 128, :]) for g in range(4)]
    pooled = jnp.concatenate(planes, axis=0).astype(BF16)
    pooled_ref[...] = pooled

    def face(x):
        fine = [both_ref[s * 256 + x * 192 : s * 256 + x * 192 + 64, :] for s in range(4)]
        return jnp.concatenate(fine + [pooled[s * 32 + x * 16 : s * 32 + x * 16 + 16] for s in range(2)], axis=0).astype(F32)

    _pack(place_ref[0], face(0), face(1), here_ref, there_ref)


def _grow_x_kernel(
    place_ref, act_ref, cot_ref, pooled_ref, got_here, got_there,
    act_out, cot_out, pooled_out, here_ref, there_ref,
):
    low, high = _sides(place_ref[0], got_here, got_there)
    firsts, lasts = [], []
    for i, (ref, out) in enumerate(((act_ref, act_out), (cot_ref, cot_out))):
        fine = ref[...].astype(F32)
        parts = []
        for s in range(2):
            at_face = slice(i * 128 + s * 64, i * 128 + s * 64 + 64)
            parts += [low[at_face], fine[s * 256 : (s + 1) * 256], high[at_face]]
        grown = jnp.concatenate(parts, axis=0)
        out[...] = grown
        firsts += [grown[p * 64 : p * 64 + 8] for p in range(12)]
        lasts += [grown[p * 64 + 56 : p * 64 + 64] for p in range(12)]
    pooled = pooled_ref[...].astype(F32)
    parts = []
    for s in range(2):
        at_face = slice(256 + s * 16, 272 + s * 16)
        parts += [low[at_face], pooled[s * 32 : (s + 1) * 32], high[at_face]]
    grown = jnp.concatenate(parts, axis=0).astype(BF16)
    pooled_out[...] = grown
    faces = _dot(_table(64, 128, _pool_y_faces), grown)
    first = jnp.concatenate(firsts + [faces[0:32]], axis=0)
    last = jnp.concatenate(lasts + [faces[32:64]], axis=0)
    _pack(place_ref[2], first, last, here_ref, there_ref)


def _grow_y_kernel(
    place_ref, act_ref, cot_ref, pooled_ref, got_here, got_there,
    act_out, cot_out, pooled_out, here_ref, there_ref, act_lines, cot_lines,
):
    low, high = _sides(place_ref[2], got_here, got_there)
    firsts, lasts = [], []
    for i, (ref, out) in enumerate(((act_ref, act_lines), (cot_ref, cot_lines))):
        for p in range(12):
            at_face = slice(i * 96 + p * 8, i * 96 + p * 8 + 8)
            out[p * 80 : p * 80 + 8, :] = low[at_face]
            out[p * 80 + 8 : p * 80 + 72, :] = ref[p * 64 : (p + 1) * 64, :]
            out[p * 80 + 72 : p * 80 + 80, :] = high[at_face]
        firsts.append(out[pl.ds(0, 120, 8), :])
        lasts.append(out[pl.ds(7, 120, 8), :])
    rows = jnp.concatenate([pooled_ref[...], low[192:224].astype(BF16), high[192:224].astype(BF16)], axis=0)
    act_out[...] = act_lines[...].astype(BF16)
    cot_out[...] = cot_lines[...].astype(BF16)
    grown = _dot(_table(192, 192, _pool_grow_y), rows)
    pooled_out[...] = grown
    faces = _dot(_table(128, 192, _pool_z_faces), grown.astype(BF16))
    first = jnp.concatenate(firsts + [faces[0:64]], axis=0)
    last = jnp.concatenate(lasts + [faces[64:128]], axis=0)
    _pack(place_ref[3], first, last, here_ref, there_ref)


def _grow_z_kernel(place_ref, act_ref, got_here, got_there, out_ref, lines):
    low, high = _sides(place_ref[3], got_here, got_there)
    lines[:, 8:16, :] = act_ref[...].astype(F32).reshape(120, 8, 128)
    lines[:, 7:8, :] = low[0:120][:, None, :]
    lines[:, 16:17, :] = high[0:120][:, None, :]
    out_ref[...] = lines[:, 7:17, :].astype(BF16)


def traded(here, there, axis):
    count = lax.axis_size(axis)
    first_pairs = [(i, i ^ 1) for i in range(count)]
    second_pairs = [(i, j) for i in range(count) for j in [((i + 1) ^ 1) - 1] if 0 <= j < count]
    return lax.ppermute(here, axis, first_pairs), lax.ppermute(there, axis, second_pairs)


def extended(place, both):
    rows, f32_rows = lambda n: ((n, 128), BF16), lambda n: ((n, 128), F32)
    own, cot, pooled, *faces = _call(_pool_kernel, (rows(512), rows(512), rows(64), rows(288), rows(288)), place, both)
    outs = (f32_rows(768), f32_rows(768), rows(128), rows(224), rows(224))
    act, cot, pooled, *faces = _call(_grow_x_kernel, outs, place, own, cot, pooled, *traded(*faces, "gx"))
    outs = (rows(960), rows(960), f32_rows(192), rows(304), rows(304))
    act, cot, pooled, *faces = _call(
        _grow_y_kernel, outs, place, act, cot, pooled, *traded(*faces, ("x", "core")), scratch=((960, 128),) * 2
    )
    return own, act, cot, pooled, traded(*faces, "gz")


def _gradients_kernel(
    place_ref, act_ref, cot_ref, pool_ref, got_here, got_there,
    w_in_hbm, w_back_hbm, w_up_hbm,
    keep_ref, send_ref, coarse_ref, d_act_ref,
    w_in, w_back, w_up, lines, shifted, pooled, spaced, sums, sem_in, sem_out,
):
    loads = [
        pltpu.make_async_copy(source, target, sem_in.at[i])
        for i, (source, target) in enumerate(((w_in_hbm, w_in), (w_up_hbm, w_up), (w_back_hbm, w_back)))
    ]
    for load in loads:
        load.start()
    core = place_ref[2]
    side = (core, 1 - core)

    def put(row, value, stride=1):
        done, count = 0, value.shape[0]
        while done < count:
            first = row + stride * done
            block = first // 496
            here = min(count - done, -((first - 496 * (block + 1)) // stride))
            start = block // 2 * 496 + first % 496
            where = pl.ds(start, here) if stride == 1 else pl.ds(start, here, stride)
            sums[side[block % 2], where, :] = value[done : done + here]
            done += here

    def ship(index, first, last):
        copy = pltpu.make_async_copy(sums.at[0, pl.ds(first, last - first)], keep_ref.at[pl.ds(first, last - first)], sem_out.at[index])
        copy.start()
        send_ref[first:last, :] = sums[1, first:last, :].astype(BF16)
        return copy

    low, high = _sides(place_ref[3], got_here, got_there)
    lines[:, 8:16, :] = cot_ref[...].astype(F32).reshape(120, 8, 128)
    lines[:, 7:8, :] = low[120:240][:, None, :]
    lines[:, 16:17, :] = high[120:240][:, None, :]
    for dz in range(3):
        window = lines[:, 7 + dz : 15 + dz, :].reshape(2, 6, 10, 8, 128)
        for dy in range(3):
            u = 8 - 3 * dy - dz
            shifted[:, :, :, u * 128 : (u + 1) * 128] = window[:, :, dy : dy + 8].reshape(2, 6, 64, 128).astype(BF16)

    windows = _table(144, 48, _pool_windows)
    for g in range(8):
        at_face = slice(240 + g * 8, 248 + g * 8)
        plane = [pool_ref[g * 24 : (g + 1) * 24, :], low[at_face], high[at_face], jnp.zeros((8, 128), F32)]
        picked = _dot(windows, jnp.concatenate(plane, axis=0).astype(BF16))
        for u in range(9):
            pooled[g // 4, g % 4, :, u * 128 : (u + 1) * 128] = picked[u * 16 : (u + 1) * 16].astype(BF16)
    loads[0].wait()
    before = jnp.zeros((64, 256), F32)
    for dx in range(3):
        before += _dot(pooled[:, dx : dx + 2].reshape(64, 1152), w_in[dx * 1152 : (dx + 1) * 1152, :])
    squash = 1.0 / (1.0 + jnp.exp(-before))
    bottom32 = (before * squash).astype(BF16).astype(F32)
    bottom = bottom32.astype(BF16)
    loads[1].wait()
    parts = [_dot(bottom, w_up[p * 256 : (p + 1) * 256, :]).astype(BF16) for p in range(8)]
    perm = _table(128, 128, _fine_from_blocks)
    upward = jnp.concatenate(
        [_dot(perm, jnp.concatenate([p[g * 16 : (g + 1) * 16] for p in parts], axis=0)) for g in range(4)], axis=0
    )

    loads[2].wait()
    d_joined = jnp.zeros((512, 256), F32)
    for dx in range(3):
        d_joined += _dot(shifted[:, dx : dx + 4].reshape(512, 1152), w_back[(2 - dx) * 1152 : (3 - dx) * 1152, :])
    d_act_ref[...] = d_joined[:, :128]

    joined_t = jnp.concatenate([act_ref[...].astype(F32).T, upward.T], axis=0).astype(BF16)
    for dx in range(3):
        grad = _dot(joined_t, shifted[:, dx : dx + 4].reshape(512, 1152))
        for u in range(9):
            put(8960 + (18 - 9 * dx + u) * 256, grad[:, u * 128 : (u + 1) * 128])
    copies = [ship(0, 4960, 7936)]

    d_upward = d_joined[:, 128:].astype(BF16)
    perm = _table(128, 128, _blocks_from_fine)
    planes = [_dot(perm, d_upward[g * 128 : (g + 1) * 128]).astype(BF16) for g in range(4)]
    blocks = [jnp.concatenate([plane[p * 16 : (p + 1) * 16] for plane in planes], axis=0) for p in range(8)]
    d_bottom = jnp.zeros((64, 256), F32)
    for p in range(8):
        d_bottom += _dot(blocks[p], w_up[p * 256 : (p + 1) * 256, :], ((1,), (1,)))
    bottom_t = bottom32.T.astype(BF16)
    for p in range(8):
        put(6912 + p * 256, _dot(bottom_t, blocks[p]))
    slope = (d_bottom * squash * (1.0 + before * (1.0 - squash))).astype(BF16)
    coarse = jnp.concatenate([bottom, slope], axis=1)
    coarse_ref[...] = coarse
    for lane in range(4):
        send_ref[7936 + lane * 64 : 8000 + lane * 64, :] = coarse[:, lane * 128 : (lane + 1) * 128]

    spaced[...] = jnp.zeros((128, 768), BF16)
    for s in range(2):
        for dx in range(3):
            spaced[s * 64 + dx * 16 : s * 64 + dx * 16 + 32, dx * 256 : (dx + 1) * 256] = slope[s * 32 : (s + 1) * 32]
    for u in range(9):
        picked_t = pooled[:, :, :, u * 128 : (u + 1) * 128].reshape(128, 128).astype(F32).T.astype(BF16)
        grad = _dot(picked_t, spaced[...])
        for dx in range(3):
            for h in range(2):
                put((9 * dx + u) * 256 + h, grad[:, dx * 256 + h * 128 : dx * 256 + (h + 1) * 128], 2)
    copies.append(ship(1, 0, 4960))
    for copy in copies:
        copy.wait()


def gradients(place, act, cot, pool, got_here, got_there, w_in, w_back, w_up):
    shape = jax.ShapeDtypeStruct
    vmem, hbm = pl.BlockSpec(memory_space=pltpu.VMEM), pl.BlockSpec(memory_space=pltpu.HBM)
    return pl.pallas_call(
        _gradients_kernel,
        out_shape=(
            shape((7936, 128), F32), shape((8192, 128), BF16), shape((64, 512), BF16), shape((512, 128), F32),
        ),
        in_specs=[pl.BlockSpec(memory_space=pltpu.SMEM)] + [vmem] * 5 + [hbm] * 3,
        out_specs=(vmem,) * 4,
        scratch_shapes=[
            pltpu.VMEM((3456, 256), BF16), pltpu.VMEM((3456, 256), BF16), pltpu.VMEM((2048, 128), BF16),
            pltpu.VMEM((120, 24, 128), F32), pltpu.VMEM((2, 6, 64, 1152), BF16),
            pltpu.VMEM((2, 4, 16, 1152), BF16), pltpu.VMEM((128, 768), BF16),
            pltpu.VMEM((2, 7936, 128), F32),
            pltpu.SemaphoreType.DMA((3,)), pltpu.SemaphoreType.DMA((2,)),
        ],
        compiler_params=pltpu.CompilerParams(vmem_limit_bytes=26 * 1024 * 1024),
        cost_estimate=pl.CostEstimate(flops=2_500_000_000, bytes_accessed=16_000_000, transcendentals=16384),
    )(
        place, act, cot, pool, got_here, got_there,
        w_in, w_back, w_up,
    )


def crossed(array, shift, along_gx):
    pairs = []
    for gx, x, core in itertools.product(range(4), range(4), range(2)):
        to = ((gx + shift) % 4, x) if core == along_gx else (gx, (x + shift) % 4)
        pairs.append(((gx * 4 + x) * 2 + core, (to[0] * 4 + to[1]) * 2 + core))
    return lax.ppermute(array, ("gx", "x", "core"), pairs)


def paired(array, axis, bit):
    count = lax.axis_size(axis)
    return lax.ppermute(array, axis, [(i, i ^ bit) for i in range(count)])


def _put_faces(ref, start, count, faces):
    for lane in range(4):
        rows = slice(start + lane * count, start + (lane + 1) * count)
        ref[rows, :] = faces[:, lane * 128 : (lane + 1) * 128].astype(ref.dtype)


def _get_faces(ref, start, count, there):
    return _wide(ref[start : start + 4 * count, :].astype(F32) * there, count).astype(BF16)


def _split_kernel(place_ref, keep_ref, got_ref, coarse_ref, own, send_1, send_2, send_3, chip_ref):
    core = place_ref[2]
    for shift, ref in enumerate((own, send_1, send_2, send_3)):
        gx, x = (place_ref[0] + shift) % 4, (place_ref[1] + shift) % 4
        for j in range(4):
            block = (gx * 4 + j) * (1 - core) + (j * 4 + x) * core
            rows = pl.ds(pl.multiple_of(block * 496, 16), 496)
            ref[j * 496 : (j + 1) * 496, :] = (keep_ref[rows, :] + got_ref[rows, :].astype(F32)).astype(ref.dtype)
    mine, other = coarse_ref[...].astype(F32), _wide(got_ref[7936:8192, :].astype(F32), 64)
    zero, one = _flag(core == 0), _flag(core == 1)
    chip = jnp.concatenate([mine * zero + other * one, mine * one + other * zero], axis=0).astype(BF16)
    chip_ref[...] = chip
    _put_faces(send_1, 1984, 64, _dot(_table(64, 128, _first_faces(core, 1)), chip))
    _put_faces(send_3, 1984, 64, _dot(_table(64, 128, _first_faces(core, 0)), chip))


def _second_kernel(place_ref, chip_ref, own_ref, got_1, got_2, got_3, known_ref, own, send_1, send_2, send_3, total):
    gx, x, core = place_ref[0], place_ref[1], place_ref[2]
    first, second = gx * (1 - core) + x * core, x * (1 - core) + gx * core
    total[...] = own_ref[...] + (got_1[0:1984, :].astype(F32) + got_2[...].astype(F32) + got_3[0:1984, :].astype(F32))
    for shift, ref in enumerate((own, send_1, send_2, send_3)):
        ref[0:496, :] = total[pl.ds(pl.multiple_of((second + shift) % 4 * 496, 16), 496), :]
    sides = [_get_faces(got_1, 1984, 64, _flag(first > 0)), _get_faces(got_3, 1984, 64, _flag(first < 3))]
    known = jnp.concatenate([chip_ref[...]] + sides, axis=0)
    known_ref[...] = known
    _put_faces(send_1, 496, 48, _dot(_table(48, 256, _second_faces(core, 1)), known))
    _put_faces(send_3, 496, 48, _dot(_table(48, 256, _second_faces(core, 0)), known))


def _third_kernel(
    place_ref, known_ref, z_faces_ref, own_ref, got_1, got_2, got_3, grown_out, keep_ref, send_ref, other_ref, rows, chunks
):
    gx, x, core, gz = (place_ref[i] for i in range(4))
    second = x * (1 - core) + gx * core
    rows[...] = own_ref[...] + (got_1[0:496, :] + got_2[...] + got_3[0:496, :])
    chunks[...] = jnp.zeros((2, 256, 128), F32)
    for r, q, p in itertools.product(range(2), repeat=3):
        chunk, place = 4 * r + 2 * q + p, ((q ^ r) * 2 + r) * 64
        chunks[p ^ r, place : place + 62, :] = rows[chunk * 62 : (chunk + 1) * 62, :]
    half = (gz + gz // 4) % 2
    keep_ref[...] = chunks[half]
    send_ref[0:256, :] = chunks[1 - half]
    sides = [_get_faces(got_1, 496, 48, _flag(second > 0)), _get_faces(got_3, 496, 48, _flag(second < 3))]
    known = jnp.concatenate([known_ref[...]] + sides, axis=0)
    grown = _dot(_table(192, 352, _grown_cells(core)), known).astype(BF16)
    grown_out[...] = grown
    faces = _dot(z_faces_ref[...], grown)
    even = _flag(gz % 2 == 0)
    _put_faces(send_ref, 256, 48, faces[48:96] * even + faces[0:48] * (1.0 - even))
    _put_faces(other_ref, 0, 48, faces[0:48] * even + faces[48:96] * (1.0 - even))


def _fourth_kernel(place_ref, keep_ref, got_ref, keep_out, send_out, both):
    gz = place_ref[3]
    mine = keep_ref[...] + got_ref[0:256, :]
    both[0] = mine[0:128]
    both[1] = mine[128:256]
    half = (gz // 2 + gz // 4) % 2
    keep_out[...] = both[half]
    send_out[...] = both[1 - half]


def _pad_kernel(place_ref, grown_ref, padded_ref, got_ref, other_ref, bottom_ref, slope_ref):
    even = _flag(place_ref[3] % 2 == 0)
    here, there = got_ref[256:448, :], other_ref[...].astype(F32)
    low = _wide(there * even + here * (1.0 - even), 48).astype(BF16)
    high = _wide(here * even + there * (1.0 - even), 48).astype(BF16)
    padded = _dot(padded_ref[...], jnp.concatenate([grown_ref[...], low, high], axis=0)).astype(BF16)
    bottom_ref[...] = padded[:, 0:256]
    slope_ref[...] = padded[:, 256:512]


def _clip_kernel(place_ref, total_ref, both_ref, out_ref):
    total = jnp.sum(total_ref[...], axis=1, keepdims=True)
    factor = jnp.minimum(1.0, jnp.sqrt(PARAMS / (total + 1e-06)))
    out_ref[...] = both_ref[pl.ds(pl.multiple_of(place_ref[3] // 4 * 64, 64), 62), :] * factor


def scattered_sum(place, keep, send, coarse):
    def f32_rows(n):
        return ((n, 128), F32)

    def rows(n):
        return ((n, 128), BF16)

    got = paired(send, "core", 1)
    outs = (f32_rows(1984), rows(2240), rows(1984), rows(2240), ((128, 512), BF16))
    own, *sends, chip = _call(_split_kernel, outs, place, keep, got, coarse)
    gots = [crossed(sends[s - 1], s, 0) for s in (1, 2, 3)]
    outs = (((256, 512), BF16), f32_rows(496), f32_rows(688), f32_rows(496), f32_rows(688))
    known, own, *sends = _call(_second_kernel, outs, place, chip, own, *gots, scratch=((1984, 128),))
    gots = [crossed(sends[s - 1], s, 1) for s in (1, 2, 3)]
    outs = (((192, 512), BF16), f32_rows(256), f32_rows(448), rows(192))
    grown, keep, send, other = _call(
        _third_kernel, outs, place, known, jnp.asarray(Z_FACES, BF16), own, *gots, scratch=((496, 128), (2, 256, 128))
    )
    got = paired(send, "gz", 1)
    other = lax.ppermute(other, "gz", [(i, j) for i in range(8) for j in [((i + 1) ^ 1) - 1] if 0 <= j < 8])
    keep, send = _call(_fourth_kernel, (f32_rows(128),) * 2, place, keep, got, scratch=((2, 128, 128),))
    return keep, send, grown, got, other


def local(activation, w_in, w_up, w_out, cotangent):
    place = jnp.stack([lax.axis_index(a) for a in ("gx", "x", "core", "gz")]).astype(jnp.int32)
    both = jnp.concatenate([activation.reshape(512, 128), cotangent.reshape(512, 128)], axis=0)
    own, act, cot, pooled, faces = extended(place, both)
    w_back = w_out.reshape(27, 256, 128).transpose(0, 2, 1).reshape(3456, 256)
    keep, send, coarse, d_direct = gradients(place, own, cot, pooled, *faces, w_in, w_back, w_up)
    keep, send, grown, got, other = scattered_sum(place, keep, send, coarse)

    send, grown, act = lax.optimization_barrier((send, grown, act))
    mine = keep + paired(send, "gz", 2)
    pads = _call(_pad_kernel, (((288, 256), BF16),) * 2, place, grown, jnp.asarray(PADDED, BF16), got, other)
    bottom_pad, slope_pad = (p.reshape(2, 4, 6, 6, 256) for p in pads)
    (active_pad,) = _call(_grow_z_kernel, (((120, 10, 128), BF16),), place, act, *faces, scratch=((120, 24, 128),))
    upward_pad = up_conv(bottom_pad, w_up).astype(BF16)[:, 1:-1, 1:-1, 1:-1]
    joined_pad = jnp.concatenate([active_pad.reshape(2, 6, 10, 10, 128), upward_pad], axis=4)
    mine, joined_pad, slope_pad = lax.optimization_barrier((mine, joined_pad, slope_pad))

    output_0 = conv_forward(joined_pad[:1], w_out).astype(BF16)
    mine = mine + paired(mine, "gz", 7)
    total = jnp.sum(mine * mine, axis=0, keepdims=True)
    total, output_0, joined_pad = lax.optimization_barrier((total, output_0, joined_pad))
    total = total + paired(total, "core", 1)
    total, joined_pad = lax.optimization_barrier((total, joined_pad))
    output_1 = conv_forward(joined_pad[1:], w_out).astype(BF16)
    total = total + paired(total, "gx", 1)
    total, output_1, slope_pad = lax.optimization_barrier((total, output_1, slope_pad))
    d_pooled = conv_transpose(slope_pad, w_in)
    d_activation = (d_direct.reshape(activation.shape) + spread(d_pooled) * 0.125).astype(BF16)
    total = total + paired(total, "gx", 3)
    total, d_activation = lax.optimization_barrier((total, d_activation))
    output = jnp.concatenate([output_0, output_1], axis=0)
    for axis, mask in (("x", 1), ("x", 3), ("gz", 1), ("gz", 2)):
        total = total + paired(total, axis, mask)
    (clipped,) = _call(_clip_kernel, (((62, 128), F32),), place, total, mine)
    return (output, d_activation, clipped.reshape(-1))


def solution(mesh):
    gx, gy, gz = mesh.devices.shape
    split = Mesh(mesh.devices.reshape(gx, gy // 2, 2, gz), ("gx", "x", "core", "gz"))
    cells = P(None, "gx", ("x", "core"), "gz", None)
    return jax.shard_map(
        local, mesh=split, in_specs=(cells, P(), P(), P(), cells),
        out_specs=(cells, cells, P(("gx", "x", "core", "gz"))), check_vma=False,
    )
```

```python
import itertools

import jax
import jax.numpy as jnp
import numpy as np
from jax import lax
from jax.experimental import pallas as pl
from jax.experimental.pallas import tpu as pltpu
from jax.sharding import Mesh, PartitionSpec as P

F32 = jnp.float32
BF16 = jnp.bfloat16
PARAMS = 2031616


def conv_forward(padded, weight):
    kernel = weight.reshape(3, 3, 3, padded.shape[4], -1)
    return lax.conv_general_dilated(
        padded, kernel, (1, 1, 1), "VALID",
        dimension_numbers=("NXYZC", "XYZIO", "NXYZC"), preferred_element_type=F32,
    )


def conv_transpose(padded, weight):
    kernel = weight.reshape(3, 3, 3, -1, padded.shape[4])[::-1, ::-1, ::-1]
    return lax.conv_general_dilated(
        padded, kernel, (1, 1, 1), "VALID",
        dimension_numbers=("NXYZC", "XYZOI", "NXYZC"), preferred_element_type=F32,
    )


def spread(volume):
    samples, size_x, size_y, size_z, chans = volume.shape
    wide = jnp.broadcast_to(
        volume[:, :, None, :, None, :, None, :], (samples, size_x, 2, size_y, 2, size_z, 2, chans)
    )
    return wide.reshape(samples, 2 * size_x, 2 * size_y, 2 * size_z, chans)


def up_conv(bottom, w_up):
    samples, size_x, size_y, size_z, wide = bottom.shape
    kernel = w_up.reshape(2, 2, 2, wide, -1)
    result = jnp.einsum("sijkc,abeco->siajbkeo", bottom, kernel, preferred_element_type=F32)
    return result.reshape(samples, 2 * size_x, 2 * size_y, 2 * size_z, -1)


def _picks(sources, width):
    picks = np.zeros((len(sources), width), np.float32)
    picks[np.arange(len(sources)), sources] = 1
    return picks


LINES = [(s * 4 + x) * 6 + y for s in range(2) for x in range(4) for y in range(6)]
Z_FACES = _picks([line * 4 + z for z in (0, 3) for line in LINES], 192)
PADDED = _picks([192 + n if z < 0 else 240 + n if z > 3 else n * 4 + z for n in LINES for z in range(-1, 5)], 288)


def _dot(a, b, contract=((1,), (0,))):
    return lax.dot_general(a, b, (contract, ((), ())), preferred_element_type=F32)


def _flag(condition):
    return jnp.where(condition, 1.0, 0.0)


def _wide(rows, count):
    return jnp.concatenate([rows[i * count : (i + 1) * count] for i in range(4)], axis=1)


def _call(kernel, outs, *args, scratch=()):
    vmem = pl.BlockSpec(memory_space=pltpu.VMEM)
    return pl.pallas_call(
        kernel,
        out_shape=tuple(jax.ShapeDtypeStruct(shape, kind) for shape, kind in outs),
        in_specs=[pl.BlockSpec(memory_space=pltpu.SMEM)] + [vmem] * (len(args) - 1),
        out_specs=(vmem,) * len(outs),
        scratch_shapes=[pltpu.VMEM(shape, F32) for shape in scratch],
        compiler_params=pltpu.CompilerParams(vmem_limit_bytes=12 * 1024 * 1024),
        cost_estimate=pl.CostEstimate(flops=1_000_000, bytes_accessed=4_000_000, transcendentals=0),
    )(*args)


def _sides(place_index, here, there):
    even = _flag(place_index % 2 == 0)
    here, there = here[...].astype(F32), there[...].astype(F32)
    return there * even + here * (1.0 - even), here * even + there * (1.0 - even)


def _pack(place_index, first, last, here_ref, there_ref):
    even = _flag(place_index % 2 == 0)
    here_ref[...] = (last * even + first * (1.0 - even)).astype(BF16)
    there_ref[...] = (first * even + last * (1.0 - even)).astype(BF16)


def _table(rows, columns, chosen, value=1.0):
    row = lax.broadcasted_iota(jnp.int32, (rows, columns), 0)
    column = lax.broadcasted_iota(jnp.int32, (rows, columns), 1)
    return jnp.where(chosen(row, column), value, 0.0).astype(BF16)


def _pool_of(r, c):
    return (((c >> 4) & 3) == (r >> 2)) & (((c >> 1) & 3) == (r & 3))


def _pool_y_faces(r, c):
    return c == ((r >> 2) & 7) * 16 + (r >> 5) * 12 + (r & 3)


def _pool_grow_y(r, c):
    plane = (r * 2731) >> 16
    y, z = (r - plane * 24) >> 2, r & 3
    inside = plane * 16 + (y - 1) * 4 + z
    return c == jnp.where(y == 0, 128 + plane * 4 + z, jnp.where(y == 5, 160 + plane * 4 + z, inside))


def _pool_z_faces(r, c):
    y = r & 7
    return (c == (((r >> 3) & 7) * 6 + y) * 4 + (r >> 6) * 3) & (y < 6)


def _pool_windows(r, c):
    u = r >> 4
    dy = (u * 11) >> 5
    line, k = ((r >> 2) & 3) + dy, (r & 3) + u - 3 * dy - 1
    return c == jnp.where(k < 0, 24 + line, jnp.where(k > 3, 32 + line, line * 4 + k))


def _fine_from_blocks(r, c):
    part = (r >> 6) * 4 + ((r >> 3) & 1) * 2 + (r & 1)
    return c == part * 16 + ((r >> 4) & 3) * 4 + ((r >> 1) & 3)


def _blocks_from_fine(r, c):
    return _fine_from_blocks(c, r)


NOWHERE = 9999


def _chip_cell(s, x, y, z):
    return (y >> 2) * 64 + ((s * 2 + x) * 4 + (y & 3)) * 4 + z


def _first_faces(core, last):
    def chosen(r, c):
        x_face = _chip_cell(r >> 5, last, (r >> 2) & 7, r & 3)
        y_face = jnp.where(r < 16, _chip_cell((r >> 3) & 1, (r >> 2) & 1, last * 7, r & 3), NOWHERE)
        return c == x_face * (1 - core) + y_face * core

    return chosen


def _second_faces(core, last):
    def chosen(r, c):
        s, x, z = r >> 4, ((r >> 2) & 3) - 1, r & 3
        side = s * 32 + last * 28 + z
        y_face = jnp.where(x < 0, 128 + side, jnp.where(x > 1, 192 + side, _chip_cell(s, x, last * 7, z)))
        y_face = jnp.where(r < 32, y_face, NOWHERE)
        s = jnp.where(r < 24, 0, 1)
        y, z = ((r - s * 24) >> 2) + 3, r & 3
        x_face = jnp.where(y > 7, 192 + (s * 2 + last) * 4 + z, _chip_cell(s, last, y, z))
        return c == y_face * (1 - core) + x_face * core

    return chosen


def _grown_cells(core):
    def chosen(r, c):
        plane = (r * 2731) >> 16
        y, z = (r - plane * 24) >> 2, r & 3
        s, x = plane >> 2, (plane & 3) - 1
        side = s * 32 + (y - 1) * 4 + z
        low = jnp.where(x < 0, 128 + side, jnp.where(x > 1, 192 + side, _chip_cell(s, x, y - 1, z)))
        low = jnp.where(y == 0, 256 + s * 16 + (x + 1) * 4 + z, low)
        side = s * 24 + y * 4 + z
        high = jnp.where(y == 5, 192 + (s * 2 + x) * 4 + z, _chip_cell(s, x, y + 3, z))
        high = jnp.where(x < 0, 256 + side, jnp.where(x > 1, 304 + side, high))
        return c == low * (1 - core) + high * core

    return chosen


def _pool_kernel(place_ref, both_ref, act_out, cot_out, pooled_ref, here_ref, there_ref):
    act_out[...] = both_ref[0:512, :]
    cot_out[...] = both_ref[512:1024, :]
    pool_of = _table(16, 128, _pool_of, 0.125)
    planes = [_dot(pool_of, both_ref[g * 128 : (g + 1) * 128, :]) for g in range(4)]
    pooled = jnp.concatenate(planes, axis=0).astype(BF16)
    pooled_ref[...] = pooled

    def face(x):
        fine = [both_ref[s * 256 + x * 192 : s * 256 + x * 192 + 64, :] for s in range(4)]
        return jnp.concatenate(fine + [pooled[s * 32 + x * 16 : s * 32 + x * 16 + 16] for s in range(2)], axis=0).astype(F32)

    _pack(place_ref[0], face(0), face(1), here_ref, there_ref)


def _grow_x_kernel(
    place_ref, act_ref, cot_ref, pooled_ref, got_here, got_there,
    act_out, cot_out, pooled_out, here_ref, there_ref,
):
    low, high = _sides(place_ref[0], got_here, got_there)
    firsts, lasts = [], []
    for i, (ref, out) in enumerate(((act_ref, act_out), (cot_ref, cot_out))):
        fine = ref[...].astype(F32)
        parts = []
        for s in range(2):
            at_face = slice(i * 128 + s * 64, i * 128 + s * 64 + 64)
            parts += [low[at_face], fine[s * 256 : (s + 1) * 256], high[at_face]]
        grown = jnp.concatenate(parts, axis=0)
        out[...] = grown
        firsts += [grown[p * 64 : p * 64 + 8] for p in range(12)]
        lasts += [grown[p * 64 + 56 : p * 64 + 64] for p in range(12)]
    pooled = pooled_ref[...].astype(F32)
    parts = []
    for s in range(2):
        at_face = slice(256 + s * 16, 272 + s * 16)
        parts += [low[at_face], pooled[s * 32 : (s + 1) * 32], high[at_face]]
    grown = jnp.concatenate(parts, axis=0).astype(BF16)
    pooled_out[...] = grown
    faces = _dot(_table(64, 128, _pool_y_faces), grown)
    first = jnp.concatenate(firsts + [faces[0:32]], axis=0)
    last = jnp.concatenate(lasts + [faces[32:64]], axis=0)
    _pack(place_ref[2], first, last, here_ref, there_ref)


def _grow_y_kernel(
    place_ref, act_ref, cot_ref, pooled_ref, got_here, got_there,
    act_out, cot_out, pooled_out, here_ref, there_ref, act_lines, cot_lines,
):
    low, high = _sides(place_ref[2], got_here, got_there)
    firsts, lasts = [], []
    for i, (ref, out) in enumerate(((act_ref, act_lines), (cot_ref, cot_lines))):
        for p in range(12):
            at_face = slice(i * 96 + p * 8, i * 96 + p * 8 + 8)
            out[p * 80 : p * 80 + 8, :] = low[at_face]
            out[p * 80 + 8 : p * 80 + 72, :] = ref[p * 64 : (p + 1) * 64, :]
            out[p * 80 + 72 : p * 80 + 80, :] = high[at_face]
        firsts.append(out[pl.ds(0, 120, 8), :])
        lasts.append(out[pl.ds(7, 120, 8), :])
    rows = jnp.concatenate([pooled_ref[...], low[192:224].astype(BF16), high[192:224].astype(BF16)], axis=0)
    act_out[...] = act_lines[...].astype(BF16)
    cot_out[...] = cot_lines[...].astype(BF16)
    grown = _dot(_table(192, 192, _pool_grow_y), rows)
    pooled_out[...] = grown
    faces = _dot(_table(128, 192, _pool_z_faces), grown.astype(BF16))
    first = jnp.concatenate(firsts + [faces[0:64]], axis=0)
    last = jnp.concatenate(lasts + [faces[64:128]], axis=0)
    _pack(place_ref[3], first, last, here_ref, there_ref)


def _grow_z_kernel(place_ref, act_ref, got_here, got_there, out_ref, lines):
    low, high = _sides(place_ref[3], got_here, got_there)
    lines[:, 8:16, :] = act_ref[...].astype(F32).reshape(120, 8, 128)
    lines[:, 7:8, :] = low[0:120][:, None, :]
    lines[:, 16:17, :] = high[0:120][:, None, :]
    out_ref[...] = lines[:, 7:17, :].astype(BF16)


def traded(here, there, axis):
    count = lax.axis_size(axis)
    first_pairs = [(i, i ^ 1) for i in range(count)]
    second_pairs = [(i, j) for i in range(count) for j in [((i + 1) ^ 1) - 1] if 0 <= j < count]
    return lax.ppermute(here, axis, first_pairs), lax.ppermute(there, axis, second_pairs)


def extended(place, both):
    rows, f32_rows = lambda n: ((n, 128), BF16), lambda n: ((n, 128), F32)
    own, cot, pooled, *faces = _call(_pool_kernel, (rows(512), rows(512), rows(64), rows(288), rows(288)), place, both)
    outs = (f32_rows(768), f32_rows(768), rows(128), rows(224), rows(224))
    act, cot, pooled, *faces = _call(_grow_x_kernel, outs, place, own, cot, pooled, *traded(*faces, "gx"))
    outs = (rows(960), rows(960), f32_rows(192), rows(304), rows(304))
    act, cot, pooled, *faces = _call(
        _grow_y_kernel, outs, place, act, cot, pooled, *traded(*faces, ("x", "core")), scratch=((960, 128),) * 2
    )
    return own, act, cot, pooled, traded(*faces, "gz")


def _gradients_kernel(
    place_ref, act_ref, cot_ref, pool_ref, got_here, got_there,
    w_in_hbm, w_back_hbm, w_up_hbm,
    sums_ref, send_ref, coarse_ref, d_act_ref,
    w_in, w_back, w_up, lines, shifted, pooled, spaced, sem_in,
):
    loads = [
        pltpu.make_async_copy(source, target, sem_in.at[i])
        for i, (source, target) in enumerate(((w_in_hbm, w_in), (w_up_hbm, w_up), (w_back_hbm, w_back)))
    ]
    for load in loads:
        load.start()
    core = place_ref[2]
    side = (core, 1 - core)

    def put(row, value, stride=1):
        done, count = 0, value.shape[0]
        while done < count:
            first = row + stride * done
            block = first // 496
            here = min(count - done, -((first - 496 * (block + 1)) // stride))
            start = block // 2 * 496 + first % 496
            where = pl.ds(start, here) if stride == 1 else pl.ds(start, here, stride)
            sums_ref[side[block % 2], where, :] = value[done : done + here]
            done += here

    def ship(first, last):
        send_ref[first:last, :] = sums_ref[1, first:last, :].astype(BF16)

    low, high = _sides(place_ref[3], got_here, got_there)
    lines[:, 8:16, :] = cot_ref[...].astype(F32).reshape(120, 8, 128)
    lines[:, 7:8, :] = low[120:240][:, None, :]
    lines[:, 16:17, :] = high[120:240][:, None, :]
    for dz in range(3):
        window = lines[:, 7 + dz : 15 + dz, :].reshape(2, 6, 10, 8, 128)
        for dy in range(3):
            u = 8 - 3 * dy - dz
            shifted[:, :, :, u * 128 : (u + 1) * 128] = window[:, :, dy : dy + 8].reshape(2, 6, 64, 128).astype(BF16)

    windows = _table(144, 48, _pool_windows)
    for g in range(8):
        at_face = slice(240 + g * 8, 248 + g * 8)
        plane = [pool_ref[g * 24 : (g + 1) * 24, :], low[at_face], high[at_face], jnp.zeros((8, 128), F32)]
        picked = _dot(windows, jnp.concatenate(plane, axis=0).astype(BF16))
        for u in range(9):
            pooled[g // 4, g % 4, :, u * 128 : (u + 1) * 128] = picked[u * 16 : (u + 1) * 16].astype(BF16)
    loads[0].wait()
    before = jnp.zeros((64, 256), F32)
    for dx in range(3):
        before += _dot(pooled[:, dx : dx + 2].reshape(64, 1152), w_in[dx * 1152 : (dx + 1) * 1152, :])
    squash = 1.0 / (1.0 + jnp.exp(-before))
    bottom32 = (before * squash).astype(BF16).astype(F32)
    bottom = bottom32.astype(BF16)
    loads[1].wait()
    parts = [_dot(bottom, w_up[p * 256 : (p + 1) * 256, :]).astype(BF16) for p in range(8)]
    perm = _table(128, 128, _fine_from_blocks)
    upward = jnp.concatenate(
        [_dot(perm, jnp.concatenate([p[g * 16 : (g + 1) * 16] for p in parts], axis=0)) for g in range(4)], axis=0
    )

    loads[2].wait()
    d_joined = jnp.zeros((512, 256), F32)
    for dx in range(3):
        d_joined += _dot(shifted[:, dx : dx + 4].reshape(512, 1152), w_back[(2 - dx) * 1152 : (3 - dx) * 1152, :])
    d_act_ref[...] = d_joined[:, :128]

    joined_t = jnp.concatenate([act_ref[...].astype(F32).T, upward.T], axis=0).astype(BF16)
    for dx in range(3):
        grad = _dot(joined_t, shifted[:, dx : dx + 4].reshape(512, 1152))
        for u in range(9):
            put(8960 + (18 - 9 * dx + u) * 256, grad[:, u * 128 : (u + 1) * 128])
    ship(4960, 7936)

    d_upward = d_joined[:, 128:].astype(BF16)
    perm = _table(128, 128, _blocks_from_fine)
    planes = [_dot(perm, d_upward[g * 128 : (g + 1) * 128]).astype(BF16) for g in range(4)]
    blocks = [jnp.concatenate([plane[p * 16 : (p + 1) * 16] for plane in planes], axis=0) for p in range(8)]
    d_bottom = jnp.zeros((64, 256), F32)
    for p in range(8):
        d_bottom += _dot(blocks[p], w_up[p * 256 : (p + 1) * 256, :], ((1,), (1,)))
    bottom_t = bottom32.T.astype(BF16)
    for p in range(8):
        put(6912 + p * 256, _dot(bottom_t, blocks[p]))
    slope = (d_bottom * squash * (1.0 + before * (1.0 - squash))).astype(BF16)
    coarse = jnp.concatenate([bottom, slope], axis=1)
    coarse_ref[...] = coarse
    for lane in range(4):
        send_ref[7936 + lane * 64 : 8000 + lane * 64, :] = coarse[:, lane * 128 : (lane + 1) * 128]

    spaced[...] = jnp.zeros((128, 768), BF16)
    for s in range(2):
        for dx in range(3):
            spaced[s * 64 + dx * 16 : s * 64 + dx * 16 + 32, dx * 256 : (dx + 1) * 256] = slope[s * 32 : (s + 1) * 32]
    for u in range(9):
        picked_t = pooled[:, :, :, u * 128 : (u + 1) * 128].reshape(128, 128).astype(F32).T.astype(BF16)
        grad = _dot(picked_t, spaced[...])
        for dx in range(3):
            for h in range(2):
                put((9 * dx + u) * 256 + h, grad[:, dx * 256 + h * 128 : dx * 256 + (h + 1) * 128], 2)
    ship(0, 4960)


def gradients(place, act, cot, pool, got_here, got_there, w_in, w_back, w_up):
    shape = jax.ShapeDtypeStruct
    vmem, hbm = pl.BlockSpec(memory_space=pltpu.VMEM), pl.BlockSpec(memory_space=pltpu.HBM)
    return pl.pallas_call(
        _gradients_kernel,
        out_shape=(
            shape((2, 7936, 128), F32), shape((8192, 128), BF16), shape((64, 512), BF16), shape((512, 128), F32),
        ),
        in_specs=[pl.BlockSpec(memory_space=pltpu.SMEM)] + [vmem] * 5 + [hbm] * 3,
        out_specs=(vmem,) * 4,
        scratch_shapes=[
            pltpu.VMEM((3456, 256), BF16), pltpu.VMEM((3456, 256), BF16), pltpu.VMEM((2048, 128), BF16),
            pltpu.VMEM((120, 24, 128), F32), pltpu.VMEM((2, 6, 64, 1152), BF16),
            pltpu.VMEM((2, 4, 16, 1152), BF16), pltpu.VMEM((128, 768), BF16),
            pltpu.SemaphoreType.DMA((3,)),
        ],
        compiler_params=pltpu.CompilerParams(vmem_limit_bytes=24 * 1024 * 1024),
        cost_estimate=pl.CostEstimate(flops=2_500_000_000, bytes_accessed=16_000_000, transcendentals=16384),
    )(
        place, act, cot, pool, got_here, got_there,
        w_in, w_back, w_up,
    )


def crossed(array, shift, along_gx):
    pairs = []
    for gx, x, core in itertools.product(range(4), range(4), range(2)):
        to = ((gx + shift) % 4, x) if core == along_gx else (gx, (x + shift) % 4)
        pairs.append(((gx * 4 + x) * 2 + core, (to[0] * 4 + to[1]) * 2 + core))
    return lax.ppermute(array, ("gx", "x", "core"), pairs)


def paired(array, axis, bit):
    count = lax.axis_size(axis)
    return lax.ppermute(array, axis, [(i, i ^ bit) for i in range(count)])


def _put_faces(ref, start, count, faces):
    for lane in range(4):
        rows = slice(start + lane * count, start + (lane + 1) * count)
        ref[rows, :] = faces[:, lane * 128 : (lane + 1) * 128].astype(ref.dtype)


def _get_faces(ref, start, count, there):
    return _wide(ref[start : start + 4 * count, :].astype(F32) * there, count).astype(BF16)


def _split_kernel(place_ref, keep_ref, got_ref, coarse_ref, own, send_1, send_2, send_3, chip_ref):
    core = place_ref[2]
    for shift, ref in enumerate((own, send_1, send_2, send_3)):
        gx, x = (place_ref[0] + shift) % 4, (place_ref[1] + shift) % 4
        for j in range(4):
            block = (gx * 4 + j) * (1 - core) + (j * 4 + x) * core
            rows = pl.ds(pl.multiple_of(block * 496, 16), 496)
            ref[j * 496 : (j + 1) * 496, :] = (keep_ref[0, rows, :] + got_ref[rows, :].astype(F32)).astype(ref.dtype)
    mine, other = coarse_ref[...].astype(F32), _wide(got_ref[7936:8192, :].astype(F32), 64)
    zero, one = _flag(core == 0), _flag(core == 1)
    chip = jnp.concatenate([mine * zero + other * one, mine * one + other * zero], axis=0).astype(BF16)
    chip_ref[...] = chip
    _put_faces(send_1, 1984, 64, _dot(_table(64, 128, _first_faces(core, 1)), chip))
    _put_faces(send_3, 1984, 64, _dot(_table(64, 128, _first_faces(core, 0)), chip))


def _second_kernel(place_ref, chip_ref, own_ref, got_2, got_1, got_3, known_ref, own, send_1, send_2, send_3, total):
    gx, x, core = place_ref[0], place_ref[1], place_ref[2]
    first, second = gx * (1 - core) + x * core, x * (1 - core) + gx * core
    total[...] = own_ref[...] + (got_1[0:1984, :].astype(F32) + got_2[...].astype(F32) + got_3[0:1984, :].astype(F32))
    for shift, ref in enumerate((own, send_1, send_2, send_3)):
        ref[0:496, :] = total[pl.ds(pl.multiple_of((second + shift) % 4 * 496, 16), 496), :]
    sides = [_get_faces(got_1, 1984, 64, _flag(first > 0)), _get_faces(got_3, 1984, 64, _flag(first < 3))]
    known = jnp.concatenate([chip_ref[...]] + sides, axis=0)
    known_ref[...] = known
    _put_faces(send_1, 496, 48, _dot(_table(48, 256, _second_faces(core, 1)), known))
    _put_faces(send_3, 496, 48, _dot(_table(48, 256, _second_faces(core, 0)), known))


def _third_kernel(
    place_ref, known_ref, z_faces_ref, own_ref, got_2, got_1, got_3, grown_out, keep_ref, send_ref, other_ref, rows, chunks
):
    gx, x, core, gz = (place_ref[i] for i in range(4))
    second = x * (1 - core) + gx * core
    rows[...] = own_ref[...] + (got_1[0:496, :] + got_2[...] + got_3[0:496, :])
    chunks[...] = jnp.zeros((2, 256, 128), F32)
    for r, q, p in itertools.product(range(2), repeat=3):
        chunk, place = 4 * r + 2 * q + p, ((q ^ r) * 2 + r) * 64
        chunks[p ^ r, place : place + 62, :] = rows[chunk * 62 : (chunk + 1) * 62, :]
    half = (gz + gz // 4) % 2
    keep_ref[...] = chunks[half]
    send_ref[0:256, :] = chunks[1 - half]
    sides = [_get_faces(got_1, 496, 48, _flag(second > 0)), _get_faces(got_3, 496, 48, _flag(second < 3))]
    known = jnp.concatenate([known_ref[...]] + sides, axis=0)
    grown = _dot(_table(192, 352, _grown_cells(core)), known).astype(BF16)
    grown_out[...] = grown
    faces = _dot(z_faces_ref[...], grown)
    even = _flag(gz % 2 == 0)
    _put_faces(send_ref, 256, 48, faces[48:96] * even + faces[0:48] * (1.0 - even))
    _put_faces(other_ref, 0, 48, faces[0:48] * even + faces[48:96] * (1.0 - even))


def _fourth_kernel(place_ref, keep_ref, got_ref, keep_out, send_out, both):
    gz = place_ref[3]
    mine = keep_ref[...] + got_ref[0:256, :]
    both[0] = mine[0:128]
    both[1] = mine[128:256]
    half = (gz // 2 + gz // 4) % 2
    keep_out[...] = both[half]
    send_out[...] = both[1 - half]


def _pad_kernel(place_ref, grown_ref, padded_ref, got_ref, other_ref, bottom_ref, slope_ref):
    even = _flag(place_ref[3] % 2 == 0)
    here, there = got_ref[256:448, :], other_ref[...].astype(F32)
    low = _wide(there * even + here * (1.0 - even), 48).astype(BF16)
    high = _wide(here * even + there * (1.0 - even), 48).astype(BF16)
    padded = _dot(padded_ref[...], jnp.concatenate([grown_ref[...], low, high], axis=0)).astype(BF16)
    bottom_ref[...] = padded[:, 0:256]
    slope_ref[...] = padded[:, 256:512]


def _clip_kernel(place_ref, total_ref, both_ref, out_ref):
    total = jnp.sum(total_ref[...], axis=1, keepdims=True)
    factor = jnp.minimum(1.0, jnp.sqrt(PARAMS / (total + 1e-06)))
    out_ref[...] = both_ref[pl.ds(pl.multiple_of(place_ref[3] // 4 * 64, 64), 62), :] * factor


def scattered_sum(place, keep, send, coarse):
    def f32_rows(n):
        return ((n, 128), F32)

    def rows(n):
        return ((n, 128), BF16)

    got = paired(send, "core", 1)
    outs = (f32_rows(1984), rows(2240), rows(1984), rows(2240), ((128, 512), BF16))
    own, *sends, chip = _call(_split_kernel, outs, place, keep, got, coarse)
    got_2, got_1, got_3 = [crossed(sends[s - 1], s, 0) for s in (2, 1, 3)]
    outs = (((256, 512), BF16), f32_rows(496), f32_rows(688), f32_rows(496), f32_rows(688))
    known, own, *sends = _call(_second_kernel, outs, place, chip, own, got_2, got_1, got_3, scratch=((1984, 128),))
    got_2, got_1, got_3 = [crossed(sends[s - 1], s, 1) for s in (2, 1, 3)]
    outs = (((192, 512), BF16), f32_rows(256), f32_rows(448), rows(192))
    grown, keep, send, other = _call(
        _third_kernel, outs, place, known, jnp.asarray(Z_FACES, BF16), own, got_2, got_1, got_3, scratch=((496, 128), (2, 256, 128))
    )
    got = paired(send, "gz", 1)
    other = lax.ppermute(other, "gz", [(i, j) for i in range(8) for j in [((i + 1) ^ 1) - 1] if 0 <= j < 8])
    keep, send = _call(_fourth_kernel, (f32_rows(128),) * 2, place, keep, got, scratch=((2, 128, 128),))
    return keep, send, grown, got, other


def local(activation, w_in, w_up, w_out, cotangent):
    place = jnp.stack([lax.axis_index(a) for a in ("gx", "x", "core", "gz")]).astype(jnp.int32)
    both = jnp.concatenate([activation.reshape(512, 128), cotangent.reshape(512, 128)], axis=0)
    own, act, cot, pooled, faces = extended(place, both)
    w_back = w_out.reshape(27, 256, 128).transpose(0, 2, 1).reshape(3456, 256)
    keep, send, coarse, d_direct = gradients(place, own, cot, pooled, *faces, w_in, w_back, w_up)
    keep, send, grown, got, other = scattered_sum(place, keep, send, coarse)

    send, grown, act = lax.optimization_barrier((send, grown, act))
    mine = keep + paired(send, "gz", 2)
    pads = _call(_pad_kernel, (((288, 256), BF16),) * 2, place, grown, jnp.asarray(PADDED, BF16), got, other)
    bottom_pad, slope_pad = (p.reshape(2, 4, 6, 6, 256) for p in pads)
    (active_pad,) = _call(_grow_z_kernel, (((120, 10, 128), BF16),), place, act, *faces, scratch=((120, 24, 128),))
    upward_pad = up_conv(bottom_pad, w_up).astype(BF16)[:, 1:-1, 1:-1, 1:-1]
    joined_pad = jnp.concatenate([active_pad.reshape(2, 6, 10, 10, 128), upward_pad], axis=4)
    mine, joined_pad, slope_pad = lax.optimization_barrier((mine, joined_pad, slope_pad))

    output_0 = conv_forward(joined_pad[:1], w_out).astype(BF16)
    mine = mine + paired(mine, "gz", 7)
    total = jnp.sum(mine * mine, axis=0, keepdims=True)
    total, output_0, joined_pad = lax.optimization_barrier((total, output_0, joined_pad))
    total = total + paired(total, "core", 1)
    total, joined_pad = lax.optimization_barrier((total, joined_pad))
    output_1 = conv_forward(joined_pad[1:], w_out).astype(BF16)
    total = total + paired(total, "gx", 1)
    total, output_1, slope_pad = lax.optimization_barrier((total, output_1, slope_pad))
    d_pooled = conv_transpose(slope_pad, w_in)
    d_activation = (d_direct.reshape(activation.shape) + spread(d_pooled) * 0.125).astype(BF16)
    total = total + paired(total, "gx", 3)
    total, d_activation = lax.optimization_barrier((total, d_activation))
    output = jnp.concatenate([output_0, output_1], axis=0)
    for axis, mask in (("x", 1), ("x", 3), ("gz", 1), ("gz", 2)):
        total = total + paired(total, axis, mask)
    (clipped,) = _call(_clip_kernel, (((62, 128), F32),), place, total, mine)
    return (output, d_activation, clipped.reshape(-1))


def solution(mesh):
    gx, gy, gz = mesh.devices.shape
    split = Mesh(mesh.devices.reshape(gx, gy // 2, 2, gz), ("gx", "x", "core", "gz"))
    cells = P(None, "gx", ("x", "core"), "gz", None)
    return jax.shard_map(
        local, mesh=split, in_specs=(cells, P(), P(), P(), cells),
        out_specs=(cells, cells, P(("gx", "x", "core", "gz"))), check_vma=False,
    )
```

```python
import itertools

import jax
import jax.numpy as jnp
import numpy as np
from jax import lax
from jax.experimental import pallas as pl
from jax.experimental.pallas import tpu as pltpu
from jax.sharding import Mesh, PartitionSpec as P

F32 = jnp.float32
BF16 = jnp.bfloat16
PARAMS = 2031616


def conv_forward(padded, weight):
    kernel = weight.reshape(3, 3, 3, padded.shape[4], -1)
    return lax.conv_general_dilated(
        padded, kernel, (1, 1, 1), "VALID",
        dimension_numbers=("NXYZC", "XYZIO", "NXYZC"), preferred_element_type=F32,
    )


def conv_transpose(padded, weight):
    kernel = weight.reshape(3, 3, 3, -1, padded.shape[4])[::-1, ::-1, ::-1]
    return lax.conv_general_dilated(
        padded, kernel, (1, 1, 1), "VALID",
        dimension_numbers=("NXYZC", "XYZOI", "NXYZC"), preferred_element_type=F32,
    )


def spread(volume):
    samples, size_x, size_y, size_z, chans = volume.shape
    wide = jnp.broadcast_to(
        volume[:, :, None, :, None, :, None, :], (samples, size_x, 2, size_y, 2, size_z, 2, chans)
    )
    return wide.reshape(samples, 2 * size_x, 2 * size_y, 2 * size_z, chans)


def up_conv(bottom, w_up):
    samples, size_x, size_y, size_z, wide = bottom.shape
    kernel = w_up.reshape(2, 2, 2, wide, -1)
    result = jnp.einsum("sijkc,abeco->siajbkeo", bottom, kernel, preferred_element_type=F32)
    return result.reshape(samples, 2 * size_x, 2 * size_y, 2 * size_z, -1)


def _picks(sources, width):
    picks = np.zeros((len(sources), width), np.float32)
    picks[np.arange(len(sources)), sources] = 1
    return picks


LINES = [(s * 4 + x) * 6 + y for s in range(2) for x in range(4) for y in range(6)]
Z_FACES = _picks([line * 4 + z for z in (0, 3) for line in LINES], 192)
PADDED = _picks([192 + n if z < 0 else 240 + n if z > 3 else n * 4 + z for n in LINES for z in range(-1, 5)], 288)


def _dot(a, b, contract=((1,), (0,))):
    return lax.dot_general(a, b, (contract, ((), ())), preferred_element_type=F32)


def _flag(condition):
    return jnp.where(condition, 1.0, 0.0)


def _wide(rows, count):
    return jnp.concatenate([rows[i * count : (i + 1) * count] for i in range(4)], axis=1)


def _call(kernel, outs, *args, scratch=()):
    vmem = pl.BlockSpec(memory_space=pltpu.VMEM)
    return pl.pallas_call(
        kernel,
        out_shape=tuple(jax.ShapeDtypeStruct(shape, kind) for shape, kind in outs),
        in_specs=[pl.BlockSpec(memory_space=pltpu.SMEM)] + [vmem] * (len(args) - 1),
        out_specs=(vmem,) * len(outs),
        scratch_shapes=[pltpu.VMEM(shape, F32) for shape in scratch],
        compiler_params=pltpu.CompilerParams(vmem_limit_bytes=12 * 1024 * 1024),
        cost_estimate=pl.CostEstimate(flops=1_000_000, bytes_accessed=4_000_000, transcendentals=0),
    )(*args)


def _sides(place_index, here, there):
    even = _flag(place_index % 2 == 0)
    here, there = here[...].astype(F32), there[...].astype(F32)
    return there * even + here * (1.0 - even), here * even + there * (1.0 - even)


def _pack(place_index, first, last, here_ref, there_ref):
    even = _flag(place_index % 2 == 0)
    here_ref[...] = (last * even + first * (1.0 - even)).astype(BF16)
    there_ref[...] = (first * even + last * (1.0 - even)).astype(BF16)


def _table(rows, columns, chosen, value=1.0):
    row = lax.broadcasted_iota(jnp.int32, (rows, columns), 0)
    column = lax.broadcasted_iota(jnp.int32, (rows, columns), 1)
    return jnp.where(chosen(row, column), value, 0.0).astype(BF16)


def _pool_of(r, c):
    return (((c >> 4) & 3) == (r >> 2)) & (((c >> 1) & 3) == (r & 3))


def _pool_y_faces(r, c):
    return c == ((r >> 2) & 7) * 16 + (r >> 5) * 12 + (r & 3)


def _pool_grow_y(r, c):
    plane = (r * 2731) >> 16
    y, z = (r - plane * 24) >> 2, r & 3
    inside = plane * 16 + (y - 1) * 4 + z
    return c == jnp.where(y == 0, 128 + plane * 4 + z, jnp.where(y == 5, 160 + plane * 4 + z, inside))


def _pool_z_faces(r, c):
    y = r & 7
    return (c == (((r >> 3) & 7) * 6 + y) * 4 + (r >> 6) * 3) & (y < 6)


def _pool_windows(r, c):
    u = r >> 4
    dy = (u * 11) >> 5
    line, k = ((r >> 2) & 3) + dy, (r & 3) + u - 3 * dy - 1
    return c == jnp.where(k < 0, 24 + line, jnp.where(k > 3, 32 + line, line * 4 + k))


def _fine_from_blocks(r, c):
    part = (r >> 6) * 4 + ((r >> 3) & 1) * 2 + (r & 1)
    return c == part * 16 + ((r >> 4) & 3) * 4 + ((r >> 1) & 3)


def _blocks_from_fine(r, c):
    return _fine_from_blocks(c, r)


NOWHERE = 9999


def _chip_cell(s, x, y, z):
    return (y >> 2) * 64 + ((s * 2 + x) * 4 + (y & 3)) * 4 + z


def _first_faces(core, last):
    def chosen(r, c):
        x_face = _chip_cell(r >> 5, last, (r >> 2) & 7, r & 3)
        y_face = jnp.where(r < 16, _chip_cell((r >> 3) & 1, (r >> 2) & 1, last * 7, r & 3), NOWHERE)
        return c == x_face * (1 - core) + y_face * core

    return chosen


def _second_faces(core, last):
    def chosen(r, c):
        s, x, z = r >> 4, ((r >> 2) & 3) - 1, r & 3
        side = s * 32 + last * 28 + z
        y_face = jnp.where(x < 0, 128 + side, jnp.where(x > 1, 192 + side, _chip_cell(s, x, last * 7, z)))
        y_face = jnp.where(r < 32, y_face, NOWHERE)
        s = jnp.where(r < 24, 0, 1)
        y, z = ((r - s * 24) >> 2) + 3, r & 3
        x_face = jnp.where(y > 7, 192 + (s * 2 + last) * 4 + z, _chip_cell(s, last, y, z))
        return c == y_face * (1 - core) + x_face * core

    return chosen


def _grown_cells(core):
    def chosen(r, c):
        plane = (r * 2731) >> 16
        y, z = (r - plane * 24) >> 2, r & 3
        s, x = plane >> 2, (plane & 3) - 1
        side = s * 32 + (y - 1) * 4 + z
        low = jnp.where(x < 0, 128 + side, jnp.where(x > 1, 192 + side, _chip_cell(s, x, y - 1, z)))
        low = jnp.where(y == 0, 256 + s * 16 + (x + 1) * 4 + z, low)
        side = s * 24 + y * 4 + z
        high = jnp.where(y == 5, 192 + (s * 2 + x) * 4 + z, _chip_cell(s, x, y + 3, z))
        high = jnp.where(x < 0, 256 + side, jnp.where(x > 1, 304 + side, high))
        return c == low * (1 - core) + high * core

    return chosen


def _pool_kernel(place_ref, both_ref, act_out, cot_out, pooled_ref, here_ref, there_ref):
    act_out[...] = both_ref[0:512, :]
    cot_out[...] = both_ref[512:1024, :]
    pool_of = _table(16, 128, _pool_of, 0.125)
    planes = [_dot(pool_of, both_ref[g * 128 : (g + 1) * 128, :]) for g in range(4)]
    pooled = jnp.concatenate(planes, axis=0).astype(BF16)
    pooled_ref[...] = pooled

    def face(x):
        fine = [both_ref[s * 256 + x * 192 : s * 256 + x * 192 + 64, :] for s in range(4)]
        return jnp.concatenate(fine + [pooled[s * 32 + x * 16 : s * 32 + x * 16 + 16] for s in range(2)], axis=0).astype(F32)

    _pack(place_ref[0], face(0), face(1), here_ref, there_ref)


def _grow_x_kernel(
    place_ref, act_ref, cot_ref, pooled_ref, got_here, got_there,
    act_out, cot_out, pooled_out, here_ref, there_ref,
):
    low, high = _sides(place_ref[0], got_here, got_there)
    firsts, lasts = [], []
    for i, (ref, out) in enumerate(((act_ref, act_out), (cot_ref, cot_out))):
        fine = ref[...].astype(F32)
        parts = []
        for s in range(2):
            at_face = slice(i * 128 + s * 64, i * 128 + s * 64 + 64)
            parts += [low[at_face], fine[s * 256 : (s + 1) * 256], high[at_face]]
        grown = jnp.concatenate(parts, axis=0)
        out[...] = grown
        firsts += [grown[p * 64 : p * 64 + 8] for p in range(12)]
        lasts += [grown[p * 64 + 56 : p * 64 + 64] for p in range(12)]
    pooled = pooled_ref[...].astype(F32)
    parts = []
    for s in range(2):
        at_face = slice(256 + s * 16, 272 + s * 16)
        parts += [low[at_face], pooled[s * 32 : (s + 1) * 32], high[at_face]]
    grown = jnp.concatenate(parts, axis=0).astype(BF16)
    pooled_out[...] = grown
    faces = _dot(_table(64, 128, _pool_y_faces), grown)
    first = jnp.concatenate(firsts + [faces[0:32]], axis=0)
    last = jnp.concatenate(lasts + [faces[32:64]], axis=0)
    _pack(place_ref[2], first, last, here_ref, there_ref)


def _grow_y_kernel(
    place_ref, act_ref, cot_ref, pooled_ref, got_here, got_there,
    act_out, cot_out, pooled_out, here_ref, there_ref, act_lines, cot_lines,
):
    low, high = _sides(place_ref[2], got_here, got_there)
    firsts, lasts = [], []
    for i, (ref, out) in enumerate(((act_ref, act_lines), (cot_ref, cot_lines))):
        for p in range(12):
            at_face = slice(i * 96 + p * 8, i * 96 + p * 8 + 8)
            out[p * 80 : p * 80 + 8, :] = low[at_face]
            out[p * 80 + 8 : p * 80 + 72, :] = ref[p * 64 : (p + 1) * 64, :]
            out[p * 80 + 72 : p * 80 + 80, :] = high[at_face]
        firsts.append(out[pl.ds(0, 120, 8), :])
        lasts.append(out[pl.ds(7, 120, 8), :])
    rows = jnp.concatenate([pooled_ref[...], low[192:224].astype(BF16), high[192:224].astype(BF16)], axis=0)
    act_out[...] = act_lines[...].astype(BF16)
    cot_out[...] = cot_lines[...].astype(BF16)
    grown = _dot(_table(192, 192, _pool_grow_y), rows)
    pooled_out[...] = grown
    faces = _dot(_table(128, 192, _pool_z_faces), grown.astype(BF16))
    first = jnp.concatenate(firsts + [faces[0:64]], axis=0)
    last = jnp.concatenate(lasts + [faces[64:128]], axis=0)
    _pack(place_ref[3], first, last, here_ref, there_ref)


def _grow_z_kernel(place_ref, act_ref, got_here, got_there, out_ref, lines):
    low, high = _sides(place_ref[3], got_here, got_there)
    lines[:, 8:16, :] = act_ref[...].astype(F32).reshape(120, 8, 128)
    lines[:, 7:8, :] = low[0:120][:, None, :]
    lines[:, 16:17, :] = high[0:120][:, None, :]
    out_ref[...] = lines[:, 7:17, :].astype(BF16)


def traded(here, there, axis):
    count = lax.axis_size(axis)
    first_pairs = [(i, i ^ 1) for i in range(count)]
    second_pairs = [(i, j) for i in range(count) for j in [((i + 1) ^ 1) - 1] if 0 <= j < count]
    return lax.ppermute(here, axis, first_pairs), lax.ppermute(there, axis, second_pairs)


def extended(place, both):
    rows, f32_rows = lambda n: ((n, 128), BF16), lambda n: ((n, 128), F32)
    own, cot, pooled, *faces = _call(_pool_kernel, (rows(512), rows(512), rows(64), rows(288), rows(288)), place, both)
    outs = (f32_rows(768), f32_rows(768), rows(128), rows(224), rows(224))
    act, cot, pooled, *faces = _call(_grow_x_kernel, outs, place, own, cot, pooled, *traded(*faces, "gx"))
    outs = (rows(960), rows(960), f32_rows(192), rows(304), rows(304))
    act, cot, pooled, *faces = _call(
        _grow_y_kernel, outs, place, act, cot, pooled, *traded(*faces, ("x", "core")), scratch=((960, 128),) * 2
    )
    return own, act, cot, pooled, traded(*faces, "gz")


def _gradients_kernel(
    place_ref, act_ref, cot_ref, pool_ref, got_here, got_there,
    w_in_hbm, w_back_hbm, w_up_hbm,
    sums_ref, send_ref, coarse_ref, d_act_ref,
    w_in, w_back, w_up, lines, shifted, pooled, spaced, sem_in,
):
    loads = [
        pltpu.make_async_copy(source, target, sem_in.at[i])
        for i, (source, target) in enumerate(((w_in_hbm, w_in), (w_up_hbm, w_up), (w_back_hbm, w_back)))
    ]
    for load in loads:
        load.start()
    core = place_ref[2]
    side = (core, 1 - core)

    def put(row, value, stride=1):
        done, count = 0, value.shape[0]
        while done < count:
            first = row + stride * done
            block = first // 496
            here = min(count - done, -((first - 496 * (block + 1)) // stride))
            start = block // 2 * 496 + first % 496
            where = pl.ds(start, here) if stride == 1 else pl.ds(start, here, stride)
            sums_ref[side[block % 2], where, :] = value[done : done + here]
            done += here

    def ship(first, last):
        send_ref[first:last, :] = sums_ref[1, first:last, :].astype(BF16)

    low, high = _sides(place_ref[3], got_here, got_there)
    lines[:, 8:16, :] = cot_ref[...].astype(F32).reshape(120, 8, 128)
    lines[:, 7:8, :] = low[120:240][:, None, :]
    lines[:, 16:17, :] = high[120:240][:, None, :]
    for dz in range(3):
        window = lines[:, 7 + dz : 15 + dz, :].reshape(2, 6, 10, 8, 128)
        for dy in range(3):
            u = 8 - 3 * dy - dz
            shifted[:, :, :, u * 128 : (u + 1) * 128] = window[:, :, dy : dy + 8].reshape(2, 6, 64, 128).astype(BF16)

    windows = _table(144, 48, _pool_windows)
    for g in range(8):
        at_face = slice(240 + g * 8, 248 + g * 8)
        plane = [pool_ref[g * 24 : (g + 1) * 24, :], low[at_face], high[at_face], jnp.zeros((8, 128), F32)]
        picked = _dot(windows, jnp.concatenate(plane, axis=0).astype(BF16))
        for u in range(9):
            pooled[g // 4, g % 4, :, u * 128 : (u + 1) * 128] = picked[u * 16 : (u + 1) * 16].astype(BF16)
    loads[0].wait()
    before = jnp.zeros((64, 256), F32)
    for dx in range(3):
        before += _dot(pooled[:, dx : dx + 2].reshape(64, 1152), w_in[dx * 1152 : (dx + 1) * 1152, :])
    squash = 1.0 / (1.0 + jnp.exp(-before))
    bottom32 = (before * squash).astype(BF16).astype(F32)
    bottom = bottom32.astype(BF16)
    loads[1].wait()
    parts = [_dot(bottom, w_up[p * 256 : (p + 1) * 256, :]).astype(BF16) for p in range(8)]
    perm = _table(128, 128, _fine_from_blocks)
    upward = jnp.concatenate(
        [_dot(perm, jnp.concatenate([p[g * 16 : (g + 1) * 16] for p in parts], axis=0)) for g in range(4)], axis=0
    )

    loads[2].wait()
    d_joined = jnp.zeros((512, 256), F32)
    for dx in range(3):
        d_joined += _dot(shifted[:, dx : dx + 4].reshape(512, 1152), w_back[(2 - dx) * 1152 : (3 - dx) * 1152, :])
    d_act_ref[...] = d_joined[:, :128]

    joined_t = jnp.concatenate([act_ref[...].astype(F32).T, upward.T], axis=0).astype(BF16)
    for dx in range(3):
        grad = _dot(joined_t, shifted[:, dx : dx + 4].reshape(512, 1152))
        for u in range(9):
            put(8960 + (18 - 9 * dx + u) * 256, grad[:, u * 128 : (u + 1) * 128])
    ship(4960, 7936)

    d_upward = d_joined[:, 128:].astype(BF16)
    perm = _table(128, 128, _blocks_from_fine)
    planes = [_dot(perm, d_upward[g * 128 : (g + 1) * 128]).astype(BF16) for g in range(4)]
    blocks = [jnp.concatenate([plane[p * 16 : (p + 1) * 16] for plane in planes], axis=0) for p in range(8)]
    d_bottom = jnp.zeros((64, 256), F32)
    for p in range(8):
        d_bottom += _dot(blocks[p], w_up[p * 256 : (p + 1) * 256, :], ((1,), (1,)))
    bottom_t = bottom32.T.astype(BF16)
    for p in range(8):
        put(6912 + p * 256, _dot(bottom_t, blocks[p]))
    slope = (d_bottom * squash * (1.0 + before * (1.0 - squash))).astype(BF16)
    coarse = jnp.concatenate([bottom, slope], axis=1)
    coarse_ref[...] = coarse
    for lane in range(4):
        send_ref[7936 + lane * 64 : 8000 + lane * 64, :] = coarse[:, lane * 128 : (lane + 1) * 128]

    spaced[...] = jnp.zeros((128, 768), BF16)
    for s in range(2):
        for dx in range(3):
            spaced[s * 64 + dx * 16 : s * 64 + dx * 16 + 32, dx * 256 : (dx + 1) * 256] = slope[s * 32 : (s + 1) * 32]
    for u in range(9):
        picked_t = pooled[:, :, :, u * 128 : (u + 1) * 128].reshape(128, 128).astype(F32).T.astype(BF16)
        grad = _dot(picked_t, spaced[...])
        for dx in range(3):
            for h in range(2):
                put((9 * dx + u) * 256 + h, grad[:, dx * 256 + h * 128 : dx * 256 + (h + 1) * 128], 2)
    ship(0, 4960)


def gradients(place, act, cot, pool, got_here, got_there, w_in, w_back, w_up):
    shape = jax.ShapeDtypeStruct
    vmem, hbm = pl.BlockSpec(memory_space=pltpu.VMEM), pl.BlockSpec(memory_space=pltpu.HBM)
    return pl.pallas_call(
        _gradients_kernel,
        out_shape=(
            shape((2, 7936, 128), F32), shape((8192, 128), BF16), shape((64, 512), BF16), shape((512, 128), F32),
        ),
        in_specs=[pl.BlockSpec(memory_space=pltpu.SMEM)] + [vmem] * 5 + [hbm] * 3,
        out_specs=(vmem,) * 4,
        scratch_shapes=[
            pltpu.VMEM((3456, 256), BF16), pltpu.VMEM((3456, 256), BF16), pltpu.VMEM((2048, 128), BF16),
            pltpu.VMEM((120, 24, 128), F32), pltpu.VMEM((2, 6, 64, 1152), BF16),
            pltpu.VMEM((2, 4, 16, 1152), BF16), pltpu.VMEM((128, 768), BF16),
            pltpu.SemaphoreType.DMA((3,)),
        ],
        compiler_params=pltpu.CompilerParams(vmem_limit_bytes=24 * 1024 * 1024),
        cost_estimate=pl.CostEstimate(flops=2_500_000_000, bytes_accessed=16_000_000, transcendentals=16384),
    )(
        place, act, cot, pool, got_here, got_there,
        w_in, w_back, w_up,
    )


def crossed(array, shift, along_gx):
    pairs = []
    for gx, x, core in itertools.product(range(4), range(4), range(2)):
        to = ((gx + shift) % 4, x) if core == along_gx else (gx, (x + shift) % 4)
        pairs.append(((gx * 4 + x) * 2 + core, (to[0] * 4 + to[1]) * 2 + core))
    return lax.ppermute(array, ("gx", "x", "core"), pairs)


def paired(array, axis, bit):
    count = lax.axis_size(axis)
    return lax.ppermute(array, axis, [(i, i ^ bit) for i in range(count)])


def _put_faces(ref, start, count, faces):
    for lane in range(4):
        rows = slice(start + lane * count, start + (lane + 1) * count)
        ref[rows, :] = faces[:, lane * 128 : (lane + 1) * 128].astype(ref.dtype)


def _get_faces(ref, start, count, there):
    return _wide(ref[start : start + 4 * count, :].astype(F32) * there, count).astype(BF16)


def _split_kernel(place_ref, keep_ref, got_ref, coarse_ref, own, send_1, send_2, send_3, chip_ref):
    core = place_ref[2]
    for shift, ref in enumerate((own, send_1, send_2, send_3)):
        gx, x = (place_ref[0] + shift) % 4, (place_ref[1] + shift) % 4
        for j in range(4):
            block = (gx * 4 + j) * (1 - core) + (j * 4 + x) * core
            rows = pl.ds(pl.multiple_of(block * 496, 16), 496)
            ref[j * 496 : (j + 1) * 496, :] = (keep_ref[0, rows, :] + got_ref[rows, :].astype(F32)).astype(ref.dtype)
    mine, other = coarse_ref[...].astype(F32), _wide(got_ref[7936:8192, :].astype(F32), 64)
    zero, one = _flag(core == 0), _flag(core == 1)
    chip = jnp.concatenate([mine * zero + other * one, mine * one + other * zero], axis=0).astype(BF16)
    chip_ref[...] = chip
    _put_faces(send_1, 1984, 64, _dot(_table(64, 128, _first_faces(core, 1)), chip))
    _put_faces(send_3, 1984, 64, _dot(_table(64, 128, _first_faces(core, 0)), chip))


def _second_kernel(place_ref, chip_ref, own_ref, got_2, got_1, got_3, known_ref, own, send_1, send_2, send_3, total):
    gx, x, core = place_ref[0], place_ref[1], place_ref[2]
    first, second = gx * (1 - core) + x * core, x * (1 - core) + gx * core
    total[...] = own_ref[...] + (got_1[0:1984, :].astype(F32) + got_2[...].astype(F32) + got_3[0:1984, :].astype(F32))
    for shift, ref in enumerate((own, send_1, send_2, send_3)):
        ref[0:496, :] = total[pl.ds(pl.multiple_of((second + shift) % 4 * 496, 16), 496), :]
    sides = [_get_faces(got_1, 1984, 64, _flag(first > 0)), _get_faces(got_3, 1984, 64, _flag(first < 3))]
    known = jnp.concatenate([chip_ref[...]] + sides, axis=0)
    known_ref[...] = known
    _put_faces(send_1, 496, 48, _dot(_table(48, 256, _second_faces(core, 1)), known))
    _put_faces(send_3, 496, 48, _dot(_table(48, 256, _second_faces(core, 0)), known))


def _third_kernel(
    place_ref, known_ref, z_faces_ref, own_ref, got_2, got_1, got_3, grown_out, keep_ref, send_ref, other_ref, rows, chunks
):
    gx, x, core, gz = (place_ref[i] for i in range(4))
    second = x * (1 - core) + gx * core
    rows[...] = own_ref[...] + (got_1[0:496, :] + got_2[...] + got_3[0:496, :])
    chunks[...] = jnp.zeros((2, 256, 128), F32)
    for r, q, p in itertools.product(range(2), repeat=3):
        chunk, place = 4 * r + 2 * q + p, ((q ^ r) * 2 + r) * 64
        chunks[p ^ r, place : place + 62, :] = rows[chunk * 62 : (chunk + 1) * 62, :]
    half = (gz + gz // 4) % 2
    keep_ref[...] = chunks[half]
    send_ref[0:256, :] = chunks[1 - half]
    sides = [_get_faces(got_1, 496, 48, _flag(second > 0)), _get_faces(got_3, 496, 48, _flag(second < 3))]
    known = jnp.concatenate([known_ref[...]] + sides, axis=0)
    grown = _dot(_table(192, 352, _grown_cells(core)), known).astype(BF16)
    grown_out[...] = grown
    faces = _dot(z_faces_ref[...], grown)
    even = _flag(gz % 2 == 0)
    _put_faces(send_ref, 256, 48, faces[48:96] * even + faces[0:48] * (1.0 - even))
    _put_faces(other_ref, 0, 48, faces[0:48] * even + faces[48:96] * (1.0 - even))


def _fourth_kernel(place_ref, keep_ref, got_ref, keep_out, send_out, both):
    gz = place_ref[3]
    mine = keep_ref[...] + got_ref[0:256, :]
    both[0] = mine[0:128]
    both[1] = mine[128:256]
    half = (gz // 2 + gz // 4) % 2
    keep_out[...] = both[half]
    send_out[...] = both[1 - half]


def _pad_kernel(place_ref, grown_ref, padded_ref, got_ref, other_ref, bottom_ref, slope_ref):
    even = _flag(place_ref[3] % 2 == 0)
    here, there = got_ref[256:448, :], other_ref[...].astype(F32)
    low = _wide(there * even + here * (1.0 - even), 48).astype(BF16)
    high = _wide(here * even + there * (1.0 - even), 48).astype(BF16)
    padded = _dot(padded_ref[...], jnp.concatenate([grown_ref[...], low, high], axis=0)).astype(BF16)
    bottom_ref[...] = padded[:, 0:256]
    slope_ref[...] = padded[:, 256:512]


def _clip_kernel(place_ref, total_ref, both_ref, out_ref):
    total = jnp.sum(total_ref[...], axis=1, keepdims=True)
    factor = jnp.minimum(1.0, jnp.sqrt(PARAMS / (total + 1e-06)))
    out_ref[...] = both_ref[pl.ds(pl.multiple_of(place_ref[3] // 4 * 64, 64), 62), :] * factor


def scattered_sum(place, keep, send, coarse):
    def f32_rows(n):
        return ((n, 128), F32)

    def rows(n):
        return ((n, 128), BF16)

    got = paired(send, "core", 1)
    outs = (f32_rows(1984), rows(2240), rows(1984), rows(2240), ((128, 512), BF16))
    own, *sends, chip = _call(_split_kernel, outs, place, keep, got, coarse)
    got_2, got_1, got_3 = [crossed(sends[s - 1], s, 0) for s in (2, 1, 3)]
    outs = (((256, 512), BF16), f32_rows(496), f32_rows(688), f32_rows(496), f32_rows(688))
    known, own, *sends = _call(_second_kernel, outs, place, chip, own, got_2, got_1, got_3, scratch=((1984, 128),))
    got_2, got_1, got_3 = [crossed(sends[s - 1], s, 1) for s in (2, 1, 3)]
    outs = (((192, 512), BF16), f32_rows(256), f32_rows(448), rows(192))
    grown, keep, send, other = _call(
        _third_kernel, outs, place, known, jnp.asarray(Z_FACES, BF16), own, got_2, got_1, got_3, scratch=((496, 128), (2, 256, 128))
    )
    got = paired(send, "gz", 1)
    other = lax.ppermute(other, "gz", [(i, j) for i in range(8) for j in [((i + 1) ^ 1) - 1] if 0 <= j < 8])
    keep, send = _call(_fourth_kernel, (f32_rows(128),) * 2, place, keep, got, scratch=((2, 128, 128),))
    return keep, send, grown, got, other


def local(activation, w_in, w_up, w_out, cotangent):
    place = jnp.stack([lax.axis_index(a) for a in ("gx", "x", "core", "gz")]).astype(jnp.int32)
    both = jnp.concatenate([activation.reshape(512, 128), cotangent.reshape(512, 128)], axis=0)
    own, act, cot, pooled, faces = extended(place, both)
    w_back = w_out.reshape(27, 256, 128).transpose(0, 2, 1).reshape(3456, 256)
    keep, send, coarse, d_direct = gradients(place, own, cot, pooled, *faces, w_in, w_back, w_up)
    keep, send, grown, got, other = scattered_sum(place, keep, send, coarse)

    send, grown, act = lax.optimization_barrier((send, grown, act))
    mine = keep + paired(send, "gz", 2)
    pads = _call(_pad_kernel, (((288, 256), BF16),) * 2, place, grown, jnp.asarray(PADDED, BF16), got, other)
    bottom_pad, slope_pad = (p.reshape(2, 4, 6, 6, 256) for p in pads)
    (active_pad,) = _call(_grow_z_kernel, (((120, 10, 128), BF16),), place, act, *faces, scratch=((120, 24, 128),))
    upward_pad = up_conv(bottom_pad, w_up).astype(BF16)[:, 1:-1, 1:-1, 1:-1]
    joined_pad = jnp.concatenate([active_pad.reshape(2, 6, 10, 10, 128), upward_pad], axis=4)
    mine, joined_pad, slope_pad = lax.optimization_barrier((mine, joined_pad, slope_pad))

    output_0 = conv_forward(joined_pad[:1], w_out).astype(BF16)
    mine = mine + paired(mine, "gz", 7)
    total = jnp.sum(mine * mine, axis=0, keepdims=True)
    total, output_0, joined_pad = lax.optimization_barrier((total, output_0, joined_pad))
    total = total + paired(total, "core", 1)
    total, joined_pad = lax.optimization_barrier((total, joined_pad))
    output_1 = conv_forward(joined_pad[1:, :4], w_out).astype(BF16)
    total = total + paired(total, "gx", 1)
    total, output_1, joined_pad = lax.optimization_barrier((total, output_1, joined_pad))
    output_2 = conv_forward(joined_pad[1:, 2:], w_out).astype(BF16)
    total = total + paired(total, "gx", 3)
    total, output_2, slope_pad = lax.optimization_barrier((total, output_2, slope_pad))
    d_pooled = conv_transpose(slope_pad, w_in)
    d_activation = (d_direct.reshape(activation.shape) + spread(d_pooled) * 0.125).astype(BF16)
    total = total + paired(total, "x", 1)
    total, d_activation = lax.optimization_barrier((total, d_activation))
    output = jnp.concatenate([output_0, jnp.concatenate([output_1, output_2], axis=1)], axis=0)
    for axis, mask in (("x", 3), ("gz", 1), ("gz", 2)):
        total = total + paired(total, axis, mask)
    (clipped,) = _call(_clip_kernel, (((62, 128), F32),), place, total, mine)
    return (output, d_activation, clipped.reshape(-1))


def solution(mesh):
    gx, gy, gz = mesh.devices.shape
    split = Mesh(mesh.devices.reshape(gx, gy // 2, 2, gz), ("gx", "x", "core", "gz"))
    cells = P(None, "gx", ("x", "core"), "gz", None)
    return jax.shard_map(
        local, mesh=split, in_specs=(cells, P(), P(), P(), cells),
        out_specs=(cells, cells, P(("gx", "x", "core", "gz"))), check_vma=False,
    )
```

```python
import itertools

import jax
import jax.numpy as jnp
import numpy as np
from jax import lax
from jax.experimental import pallas as pl
from jax.experimental.pallas import tpu as pltpu
from jax.sharding import Mesh, PartitionSpec as P

F32 = jnp.float32
BF16 = jnp.bfloat16
PARAMS = 2031616


def conv_forward(padded, weight):
    kernel = weight.reshape(3, 3, 3, padded.shape[4], -1)
    return lax.conv_general_dilated(
        padded, kernel, (1, 1, 1), "VALID",
        dimension_numbers=("NXYZC", "XYZIO", "NXYZC"), preferred_element_type=F32,
    )


def conv_transpose(padded, weight):
    kernel = weight.reshape(3, 3, 3, -1, padded.shape[4])[::-1, ::-1, ::-1]
    return lax.conv_general_dilated(
        padded, kernel, (1, 1, 1), "VALID",
        dimension_numbers=("NXYZC", "XYZOI", "NXYZC"), preferred_element_type=F32,
    )


def spread(volume):
    samples, size_x, size_y, size_z, chans = volume.shape
    wide = jnp.broadcast_to(
        volume[:, :, None, :, None, :, None, :], (samples, size_x, 2, size_y, 2, size_z, 2, chans)
    )
    return wide.reshape(samples, 2 * size_x, 2 * size_y, 2 * size_z, chans)


def up_conv(bottom, w_up):
    samples, size_x, size_y, size_z, wide = bottom.shape
    kernel = w_up.reshape(2, 2, 2, wide, -1)
    result = jnp.einsum("sijkc,abeco->siajbkeo", bottom, kernel, preferred_element_type=F32)
    return result.reshape(samples, 2 * size_x, 2 * size_y, 2 * size_z, -1)


def _picks(sources, width):
    picks = np.zeros((len(sources), width), np.float32)
    picks[np.arange(len(sources)), sources] = 1
    return picks


LINES = [(s * 4 + x) * 6 + y for s in range(2) for x in range(4) for y in range(6)]
Z_FACES = _picks([line * 4 + z for z in (0, 3) for line in LINES], 192)
PADDED = _picks([192 + n if z < 0 else 240 + n if z > 3 else n * 4 + z for n in LINES for z in range(-1, 5)], 288)


def _dot(a, b, contract=((1,), (0,))):
    return lax.dot_general(a, b, (contract, ((), ())), preferred_element_type=F32)


def _flag(condition):
    return jnp.where(condition, 1.0, 0.0)


def _wide(rows, count):
    return jnp.concatenate([rows[i * count : (i + 1) * count] for i in range(4)], axis=1)


def _call(kernel, outs, *args, scratch=()):
    vmem = pl.BlockSpec(memory_space=pltpu.VMEM)
    return pl.pallas_call(
        kernel,
        out_shape=tuple(jax.ShapeDtypeStruct(shape, kind) for shape, kind in outs),
        in_specs=[pl.BlockSpec(memory_space=pltpu.SMEM)] + [vmem] * (len(args) - 1),
        out_specs=(vmem,) * len(outs),
        scratch_shapes=[pltpu.VMEM(shape, F32) for shape in scratch],
        compiler_params=pltpu.CompilerParams(vmem_limit_bytes=12 * 1024 * 1024),
        cost_estimate=pl.CostEstimate(flops=1_000_000, bytes_accessed=4_000_000, transcendentals=0),
    )(*args)


def _sides(place_index, here, there):
    even = _flag(place_index % 2 == 0)
    here, there = here[...].astype(F32), there[...].astype(F32)
    return there * even + here * (1.0 - even), here * even + there * (1.0 - even)


def _pack(place_index, first, last, here_ref, there_ref):
    even = _flag(place_index % 2 == 0)
    here_ref[...] = (last * even + first * (1.0 - even)).astype(BF16)
    there_ref[...] = (first * even + last * (1.0 - even)).astype(BF16)


def _table(rows, columns, chosen, value=1.0):
    row = lax.broadcasted_iota(jnp.int32, (rows, columns), 0)
    column = lax.broadcasted_iota(jnp.int32, (rows, columns), 1)
    return jnp.where(chosen(row, column), value, 0.0).astype(BF16)


def _pool_of(r, c):
    return (((c >> 4) & 3) == (r >> 2)) & (((c >> 1) & 3) == (r & 3))


def _pool_y_faces(r, c):
    return c == ((r >> 2) & 7) * 16 + (r >> 5) * 12 + (r & 3)


def _pool_grow_y(r, c):
    plane = (r * 2731) >> 16
    y, z = (r - plane * 24) >> 2, r & 3
    inside = plane * 16 + (y - 1) * 4 + z
    return c == jnp.where(y == 0, 128 + plane * 4 + z, jnp.where(y == 5, 160 + plane * 4 + z, inside))


def _pool_z_faces(r, c):
    y = r & 7
    return (c == (((r >> 3) & 7) * 6 + y) * 4 + (r >> 6) * 3) & (y < 6)


def _pool_windows(r, c):
    u = r >> 4
    dy = (u * 11) >> 5
    line, k = ((r >> 2) & 3) + dy, (r & 3) + u - 3 * dy - 1
    return c == jnp.where(k < 0, 24 + line, jnp.where(k > 3, 32 + line, line * 4 + k))


def _fine_from_blocks(r, c):
    part = (r >> 6) * 4 + ((r >> 3) & 1) * 2 + (r & 1)
    return c == part * 16 + ((r >> 4) & 3) * 4 + ((r >> 1) & 3)


def _blocks_from_fine(r, c):
    return _fine_from_blocks(c, r)


NOWHERE = 9999


def _chip_cell(s, x, y, z):
    return (y >> 2) * 64 + ((s * 2 + x) * 4 + (y & 3)) * 4 + z


def _first_faces(core, last):
    def chosen(r, c):
        x_face = _chip_cell(r >> 5, last, (r >> 2) & 7, r & 3)
        y_face = jnp.where(r < 16, _chip_cell((r >> 3) & 1, (r >> 2) & 1, last * 7, r & 3), NOWHERE)
        return c == x_face * (1 - core) + y_face * core

    return chosen


def _second_faces(core, last):
    def chosen(r, c):
        s, x, z = r >> 4, ((r >> 2) & 3) - 1, r & 3
        side = s * 32 + last * 28 + z
        y_face = jnp.where(x < 0, 128 + side, jnp.where(x > 1, 192 + side, _chip_cell(s, x, last * 7, z)))
        y_face = jnp.where(r < 32, y_face, NOWHERE)
        s = jnp.where(r < 24, 0, 1)
        y, z = ((r - s * 24) >> 2) + 3, r & 3
        x_face = jnp.where(y > 7, 192 + (s * 2 + last) * 4 + z, _chip_cell(s, last, y, z))
        return c == y_face * (1 - core) + x_face * core

    return chosen


def _grown_cells(core):
    def chosen(r, c):
        plane = (r * 2731) >> 16
        y, z = (r - plane * 24) >> 2, r & 3
        s, x = plane >> 2, (plane & 3) - 1
        side = s * 32 + (y - 1) * 4 + z
        low = jnp.where(x < 0, 128 + side, jnp.where(x > 1, 192 + side, _chip_cell(s, x, y - 1, z)))
        low = jnp.where(y == 0, 256 + s * 16 + (x + 1) * 4 + z, low)
        side = s * 24 + y * 4 + z
        high = jnp.where(y == 5, 192 + (s * 2 + x) * 4 + z, _chip_cell(s, x, y + 3, z))
        high = jnp.where(x < 0, 256 + side, jnp.where(x > 1, 304 + side, high))
        return c == low * (1 - core) + high * core

    return chosen


def _pool_kernel(place_ref, both_ref, act_out, cot_out, pooled_ref, here_ref, there_ref):
    act_out[...] = both_ref[0:512, :]
    cot_out[...] = both_ref[512:1024, :]
    pool_of = _table(16, 128, _pool_of, 0.125)
    planes = [_dot(pool_of, both_ref[g * 128 : (g + 1) * 128, :]) for g in range(4)]
    pooled = jnp.concatenate(planes, axis=0).astype(BF16)
    pooled_ref[...] = pooled

    def face(x):
        fine = [both_ref[s * 256 + x * 192 : s * 256 + x * 192 + 64, :] for s in range(4)]
        return jnp.concatenate(fine + [pooled[s * 32 + x * 16 : s * 32 + x * 16 + 16] for s in range(2)], axis=0).astype(F32)

    _pack(place_ref[0], face(0), face(1), here_ref, there_ref)


def _grow_x_kernel(
    place_ref, act_ref, cot_ref, pooled_ref, got_here, got_there,
    act_out, cot_out, pooled_out, here_ref, there_ref,
):
    low, high = _sides(place_ref[0], got_here, got_there)
    firsts, lasts = [], []
    for i, (ref, out) in enumerate(((act_ref, act_out), (cot_ref, cot_out))):
        fine = ref[...].astype(F32)
        parts = []
        for s in range(2):
            at_face = slice(i * 128 + s * 64, i * 128 + s * 64 + 64)
            parts += [low[at_face], fine[s * 256 : (s + 1) * 256], high[at_face]]
        grown = jnp.concatenate(parts, axis=0)
        out[...] = grown
        firsts += [grown[p * 64 : p * 64 + 8] for p in range(12)]
        lasts += [grown[p * 64 + 56 : p * 64 + 64] for p in range(12)]
    pooled = pooled_ref[...].astype(F32)
    parts = []
    for s in range(2):
        at_face = slice(256 + s * 16, 272 + s * 16)
        parts += [low[at_face], pooled[s * 32 : (s + 1) * 32], high[at_face]]
    grown = jnp.concatenate(parts, axis=0).astype(BF16)
    pooled_out[...] = grown
    faces = _dot(_table(64, 128, _pool_y_faces), grown)
    first = jnp.concatenate(firsts + [faces[0:32]], axis=0)
    last = jnp.concatenate(lasts + [faces[32:64]], axis=0)
    _pack(place_ref[2], first, last, here_ref, there_ref)


def _grow_y_kernel(
    place_ref, act_ref, cot_ref, pooled_ref, got_here, got_there,
    act_out, cot_out, pooled_out, here_ref, there_ref, act_lines, cot_lines,
):
    low, high = _sides(place_ref[2], got_here, got_there)
    firsts, lasts = [], []
    for i, (ref, out) in enumerate(((act_ref, act_lines), (cot_ref, cot_lines))):
        for p in range(12):
            at_face = slice(i * 96 + p * 8, i * 96 + p * 8 + 8)
            out[p * 80 : p * 80 + 8, :] = low[at_face]
            out[p * 80 + 8 : p * 80 + 72, :] = ref[p * 64 : (p + 1) * 64, :]
            out[p * 80 + 72 : p * 80 + 80, :] = high[at_face]
        firsts.append(out[pl.ds(0, 120, 8), :])
        lasts.append(out[pl.ds(7, 120, 8), :])
    rows = jnp.concatenate([pooled_ref[...], low[192:224].astype(BF16), high[192:224].astype(BF16)], axis=0)
    act_out[...] = act_lines[...].astype(BF16)
    cot_out[...] = cot_lines[...].astype(BF16)
    grown = _dot(_table(192, 192, _pool_grow_y), rows)
    pooled_out[...] = grown
    faces = _dot(_table(128, 192, _pool_z_faces), grown.astype(BF16))
    first = jnp.concatenate(firsts + [faces[0:64]], axis=0)
    last = jnp.concatenate(lasts + [faces[64:128]], axis=0)
    _pack(place_ref[3], first, last, here_ref, there_ref)


def _grow_z_kernel(place_ref, act_ref, got_here, got_there, out_ref, lines):
    low, high = _sides(place_ref[3], got_here, got_there)
    lines[:, 8:16, :] = act_ref[...].astype(F32).reshape(120, 8, 128)
    lines[:, 7:8, :] = low[0:120][:, None, :]
    lines[:, 16:17, :] = high[0:120][:, None, :]
    out_ref[...] = lines[:, 7:17, :].astype(BF16)


def traded(here, there, axis):
    count = lax.axis_size(axis)
    first_pairs = [(i, i ^ 1) for i in range(count)]
    second_pairs = [(i, j) for i in range(count) for j in [((i + 1) ^ 1) - 1] if 0 <= j < count]
    return lax.ppermute(here, axis, first_pairs), lax.ppermute(there, axis, second_pairs)


def extended(place, both):
    rows, f32_rows = lambda n: ((n, 128), BF16), lambda n: ((n, 128), F32)
    own, cot, pooled, *faces = _call(_pool_kernel, (rows(512), rows(512), rows(64), rows(288), rows(288)), place, both)
    outs = (f32_rows(768), f32_rows(768), rows(128), rows(224), rows(224))
    act, cot, pooled, *faces = _call(_grow_x_kernel, outs, place, own, cot, pooled, *traded(*faces, "gx"))
    outs = (rows(960), rows(960), f32_rows(192), rows(304), rows(304))
    act, cot, pooled, *faces = _call(
        _grow_y_kernel, outs, place, act, cot, pooled, *traded(*faces, ("x", "core")), scratch=((960, 128),) * 2
    )
    return own, act, cot, pooled, traded(*faces, "gz")


def _gradients_kernel(
    place_ref, act_ref, cot_ref, pool_ref, got_here, got_there,
    w_in_hbm, w_back_hbm, w_up_hbm,
    sums_ref, send_ref, coarse_ref, d_act_ref,
    w_in, w_back, w_up, lines, shifted, pooled, spaced, sem_in,
):
    loads = [
        pltpu.make_async_copy(source, target, sem_in.at[i])
        for i, (source, target) in enumerate(((w_in_hbm, w_in), (w_up_hbm, w_up), (w_back_hbm, w_back)))
    ]
    for load in loads:
        load.start()
    core = place_ref[2]
    side = (core, 1 - core)

    def put(row, value, stride=1):
        done, count = 0, value.shape[0]
        while done < count:
            first = row + stride * done
            block = first // 496
            here = min(count - done, -((first - 496 * (block + 1)) // stride))
            start = block // 2 * 496 + first % 496
            where = pl.ds(start, here) if stride == 1 else pl.ds(start, here, stride)
            sums_ref[side[block % 2], where, :] = value[done : done + here]
            done += here

    def ship(first, last):
        send_ref[first:last, :] = sums_ref[1, first:last, :].astype(BF16)

    low, high = _sides(place_ref[3], got_here, got_there)
    lines[:, 8:16, :] = cot_ref[...].astype(F32).reshape(120, 8, 128)
    lines[:, 7:8, :] = low[120:240][:, None, :]
    lines[:, 16:17, :] = high[120:240][:, None, :]
    for dz in range(3):
        window = lines[:, 7 + dz : 15 + dz, :].reshape(2, 6, 10, 8, 128)
        for dy in range(3):
            u = 8 - 3 * dy - dz
            shifted[:, :, :, u * 128 : (u + 1) * 128] = window[:, :, dy : dy + 8].reshape(2, 6, 64, 128).astype(BF16)

    windows = _table(144, 48, _pool_windows)
    for g in range(8):
        at_face = slice(240 + g * 8, 248 + g * 8)
        plane = [pool_ref[g * 24 : (g + 1) * 24, :], low[at_face], high[at_face], jnp.zeros((8, 128), F32)]
        picked = _dot(windows, jnp.concatenate(plane, axis=0).astype(BF16))
        for u in range(9):
            pooled[g // 4, g % 4, :, u * 128 : (u + 1) * 128] = picked[u * 16 : (u + 1) * 16].astype(BF16)
    loads[0].wait()
    before = jnp.zeros((64, 256), F32)
    for dx in range(3):
        before += _dot(pooled[:, dx : dx + 2].reshape(64, 1152), w_in[dx * 1152 : (dx + 1) * 1152, :])
    squash = 1.0 / (1.0 + jnp.exp(-before))
    bottom32 = (before * squash).astype(BF16).astype(F32)
    bottom = bottom32.astype(BF16)
    loads[1].wait()
    parts = [_dot(bottom, w_up[p * 256 : (p + 1) * 256, :]).astype(BF16) for p in range(8)]
    perm = _table(128, 128, _fine_from_blocks)
    upward = jnp.concatenate(
        [_dot(perm, jnp.concatenate([p[g * 16 : (g + 1) * 16] for p in parts], axis=0)) for g in range(4)], axis=0
    )

    loads[2].wait()
    d_joined = jnp.zeros((512, 256), F32)
    for dx in range(3):
        d_joined += _dot(shifted[:, dx : dx + 4].reshape(512, 1152), w_back[(2 - dx) * 1152 : (3 - dx) * 1152, :])
    d_act_ref[...] = d_joined[:, :128]

    joined_t = jnp.concatenate([act_ref[...].astype(F32).T, upward.T], axis=0).astype(BF16)
    for dx in range(3):
        grad = _dot(joined_t, shifted[:, dx : dx + 4].reshape(512, 1152))
        for u in range(9):
            put(8960 + (18 - 9 * dx + u) * 256, grad[:, u * 128 : (u + 1) * 128])
    ship(4960, 7936)

    d_upward = d_joined[:, 128:].astype(BF16)
    perm = _table(128, 128, _blocks_from_fine)
    planes = [_dot(perm, d_upward[g * 128 : (g + 1) * 128]).astype(BF16) for g in range(4)]
    blocks = [jnp.concatenate([plane[p * 16 : (p + 1) * 16] for plane in planes], axis=0) for p in range(8)]
    d_bottom = jnp.zeros((64, 256), F32)
    for p in range(8):
        d_bottom += _dot(blocks[p], w_up[p * 256 : (p + 1) * 256, :], ((1,), (1,)))
    bottom_t = bottom32.T.astype(BF16)
    for p in range(8):
        put(6912 + p * 256, _dot(bottom_t, blocks[p]))
    slope = (d_bottom * squash * (1.0 + before * (1.0 - squash))).astype(BF16)
    coarse = jnp.concatenate([bottom, slope], axis=1)
    coarse_ref[...] = coarse
    for lane in range(4):
        send_ref[7936 + lane * 64 : 8000 + lane * 64, :] = coarse[:, lane * 128 : (lane + 1) * 128]

    spaced[...] = jnp.zeros((128, 768), BF16)
    for s in range(2):
        for dx in range(3):
            spaced[s * 64 + dx * 16 : s * 64 + dx * 16 + 32, dx * 256 : (dx + 1) * 256] = slope[s * 32 : (s + 1) * 32]
    for u in range(9):
        picked_t = pooled[:, :, :, u * 128 : (u + 1) * 128].reshape(128, 128).astype(F32).T.astype(BF16)
        grad = _dot(picked_t, spaced[...])
        for dx in range(3):
            for h in range(2):
                put((9 * dx + u) * 256 + h, grad[:, dx * 256 + h * 128 : dx * 256 + (h + 1) * 128], 2)
    ship(0, 4960)


def gradients(place, act, cot, pool, got_here, got_there, w_in, w_back, w_up):
    shape = jax.ShapeDtypeStruct
    vmem, hbm = pl.BlockSpec(memory_space=pltpu.VMEM), pl.BlockSpec(memory_space=pltpu.HBM)
    return pl.pallas_call(
        _gradients_kernel,
        out_shape=(
            shape((2, 7936, 128), F32), shape((8192, 128), BF16), shape((64, 512), BF16), shape((512, 128), F32),
        ),
        in_specs=[pl.BlockSpec(memory_space=pltpu.SMEM)] + [vmem] * 5 + [hbm] * 3,
        out_specs=(vmem,) * 4,
        scratch_shapes=[
            pltpu.VMEM((3456, 256), BF16), pltpu.VMEM((3456, 256), BF16), pltpu.VMEM((2048, 128), BF16),
            pltpu.VMEM((120, 24, 128), F32), pltpu.VMEM((2, 6, 64, 1152), BF16),
            pltpu.VMEM((2, 4, 16, 1152), BF16), pltpu.VMEM((128, 768), BF16),
            pltpu.SemaphoreType.DMA((3,)),
        ],
        compiler_params=pltpu.CompilerParams(vmem_limit_bytes=24 * 1024 * 1024),
        cost_estimate=pl.CostEstimate(flops=2_500_000_000, bytes_accessed=16_000_000, transcendentals=16384),
    )(
        place, act, cot, pool, got_here, got_there,
        w_in, w_back, w_up,
    )


def crossed(array, shift, along_gx):
    pairs = []
    for gx, x, core in itertools.product(range(4), range(4), range(2)):
        to = ((gx + shift) % 4, x) if core == along_gx else (gx, (x + shift) % 4)
        pairs.append(((gx * 4 + x) * 2 + core, (to[0] * 4 + to[1]) * 2 + core))
    return lax.ppermute(array, ("gx", "x", "core"), pairs)


def paired(array, axis, bit):
    count = lax.axis_size(axis)
    return lax.ppermute(array, axis, [(i, i ^ bit) for i in range(count)])


def _put_faces(ref, start, count, faces):
    for lane in range(4):
        rows = slice(start + lane * count, start + (lane + 1) * count)
        ref[rows, :] = faces[:, lane * 128 : (lane + 1) * 128].astype(ref.dtype)


def _get_faces(ref, start, count, there):
    return _wide(ref[start : start + 4 * count, :].astype(F32) * there, count).astype(BF16)


def _split_kernel(place_ref, keep_ref, got_ref, coarse_ref, own, send_1, send_2, send_3, chip_ref):
    core = place_ref[2]
    for shift, ref in enumerate((own, send_1, send_2, send_3)):
        gx, x = (place_ref[0] + shift) % 4, (place_ref[1] + shift) % 4
        for j in range(4):
            block = (gx * 4 + j) * (1 - core) + (j * 4 + x) * core
            rows = pl.ds(pl.multiple_of(block * 496, 16), 496)
            ref[j * 496 : (j + 1) * 496, :] = (keep_ref[0, rows, :] + got_ref[rows, :].astype(F32)).astype(ref.dtype)
    mine, other = coarse_ref[...].astype(F32), _wide(got_ref[7936:8192, :].astype(F32), 64)
    zero, one = _flag(core == 0), _flag(core == 1)
    chip = jnp.concatenate([mine * zero + other * one, mine * one + other * zero], axis=0).astype(BF16)
    chip_ref[...] = chip
    _put_faces(send_1, 1984, 64, _dot(_table(64, 128, _first_faces(core, 1)), chip))
    _put_faces(send_3, 1984, 64, _dot(_table(64, 128, _first_faces(core, 0)), chip))


def _second_kernel(place_ref, chip_ref, own_ref, got_2, got_1, got_3, known_ref, own, send_1, send_2, send_3, total):
    gx, x, core = place_ref[0], place_ref[1], place_ref[2]
    first, second = gx * (1 - core) + x * core, x * (1 - core) + gx * core
    total[...] = own_ref[...] + (got_1[0:1984, :].astype(F32) + got_2[...].astype(F32) + got_3[0:1984, :].astype(F32))
    for shift, ref in enumerate((own, send_1, send_2, send_3)):
        ref[0:496, :] = total[pl.ds(pl.multiple_of((second + shift) % 4 * 496, 16), 496), :]
    sides = [_get_faces(got_1, 1984, 64, _flag(first > 0)), _get_faces(got_3, 1984, 64, _flag(first < 3))]
    known = jnp.concatenate([chip_ref[...]] + sides, axis=0)
    known_ref[...] = known
    _put_faces(send_1, 496, 48, _dot(_table(48, 256, _second_faces(core, 1)), known))
    _put_faces(send_3, 496, 48, _dot(_table(48, 256, _second_faces(core, 0)), known))


def _third_kernel(
    place_ref, known_ref, z_faces_ref, own_ref, got_2, got_1, got_3, grown_out, keep_ref, send_ref, other_ref, rows, chunks
):
    gx, x, core, gz = (place_ref[i] for i in range(4))
    second = x * (1 - core) + gx * core
    rows[...] = own_ref[...] + (got_1[0:496, :] + got_2[...] + got_3[0:496, :])
    chunks[...] = jnp.zeros((2, 256, 128), F32)
    for r, q, p in itertools.product(range(2), repeat=3):
        chunk, place = 4 * r + 2 * q + p, ((q ^ r) * 2 + r) * 64
        chunks[p ^ r, place : place + 62, :] = rows[chunk * 62 : (chunk + 1) * 62, :]
    half = (gz + gz // 4) % 2
    keep_ref[...] = chunks[half]
    send_ref[0:256, :] = chunks[1 - half]
    sides = [_get_faces(got_1, 496, 48, _flag(second > 0)), _get_faces(got_3, 496, 48, _flag(second < 3))]
    known = jnp.concatenate([known_ref[...]] + sides, axis=0)
    grown = _dot(_table(192, 352, _grown_cells(core)), known).astype(BF16)
    grown_out[...] = grown
    faces = _dot(z_faces_ref[...], grown)
    even = _flag(gz % 2 == 0)
    _put_faces(send_ref, 256, 48, faces[48:96] * even + faces[0:48] * (1.0 - even))
    _put_faces(other_ref, 0, 48, faces[0:48] * even + faces[48:96] * (1.0 - even))


def _fourth_kernel(place_ref, keep_ref, got_ref, keep_out, send_out, both):
    gz = place_ref[3]
    mine = keep_ref[...] + got_ref[0:256, :]
    both[0] = mine[0:128]
    both[1] = mine[128:256]
    half = (gz // 2 + gz // 4) % 2
    keep_out[...] = both[half]
    send_out[...] = both[1 - half]


def _pad_kernel(place_ref, grown_ref, padded_ref, got_ref, other_ref, bottom_ref, slope_ref):
    even = _flag(place_ref[3] % 2 == 0)
    here, there = got_ref[256:448, :], other_ref[...].astype(F32)
    low = _wide(there * even + here * (1.0 - even), 48).astype(BF16)
    high = _wide(here * even + there * (1.0 - even), 48).astype(BF16)
    padded = _dot(padded_ref[...], jnp.concatenate([grown_ref[...], low, high], axis=0)).astype(BF16)
    bottom_ref[...] = padded[:, 0:256]
    slope_ref[...] = padded[:, 256:512]


def _clip_kernel(place_ref, total_ref, both_ref, out_ref):
    total = jnp.sum(total_ref[...], axis=1, keepdims=True)
    factor = jnp.minimum(1.0, jnp.sqrt(PARAMS / (total + 1e-06)))
    out_ref[...] = both_ref[pl.ds(pl.multiple_of(place_ref[3] // 4 * 64, 64), 62), :] * factor


def scattered_sum(place, keep, send, coarse):
    def f32_rows(n):
        return ((n, 128), F32)

    def rows(n):
        return ((n, 128), BF16)

    got = paired(send, "core", 1)
    outs = (f32_rows(1984), rows(2240), rows(1984), rows(2240), ((128, 512), BF16))
    own, *sends, chip = _call(_split_kernel, outs, place, keep, got, coarse)
    got_2, got_1, got_3 = [crossed(sends[s - 1], s, 0) for s in (2, 1, 3)]
    outs = (((256, 512), BF16), f32_rows(496), f32_rows(688), f32_rows(496), f32_rows(688))
    known, own, *sends = _call(_second_kernel, outs, place, chip, own, got_2, got_1, got_3, scratch=((1984, 128),))
    got_2, got_1, got_3 = [crossed(sends[s - 1], s, 1) for s in (2, 1, 3)]
    outs = (((192, 512), BF16), f32_rows(256), f32_rows(448), rows(192))
    grown, keep, send, other = _call(
        _third_kernel, outs, place, known, jnp.asarray(Z_FACES, BF16), own, got_2, got_1, got_3, scratch=((496, 128), (2, 256, 128))
    )
    got = paired(send, "gz", 1)
    other = lax.ppermute(other, "gz", [(i, j) for i in range(8) for j in [((i + 1) ^ 1) - 1] if 0 <= j < 8])
    keep, send = _call(_fourth_kernel, (f32_rows(128),) * 2, place, keep, got, scratch=((2, 128, 128),))
    return keep, send, grown, got, other


def local(activation, w_in, w_up, w_out, cotangent):
    place = jnp.stack([lax.axis_index(a) for a in ("gx", "x", "core", "gz")]).astype(jnp.int32)
    both = jnp.concatenate([activation.reshape(512, 128), cotangent.reshape(512, 128)], axis=0)
    own, act, cot, pooled, faces = extended(place, both)
    w_back = w_out.reshape(27, 256, 128).transpose(0, 2, 1).reshape(3456, 256)
    keep, send, coarse, d_direct = gradients(place, own, cot, pooled, *faces, w_in, w_back, w_up)
    keep, send, grown, got, other = scattered_sum(place, keep, send, coarse)

    send, grown, act = lax.optimization_barrier((send, grown, act))
    mine = keep + paired(send, "gz", 2)
    (active_pad,) = _call(_grow_z_kernel, (((120, 10, 128), BF16),), place, act, *faces, scratch=((120, 24, 128),))
    active_pad, grown = lax.optimization_barrier((active_pad, grown))
    pads = _call(_pad_kernel, (((288, 256), BF16),) * 2, place, grown, jnp.asarray(PADDED, BF16), got, other)
    bottom_pad, slope_pad = (p.reshape(2, 4, 6, 6, 256) for p in pads)
    upward_pad = up_conv(bottom_pad, w_up).astype(BF16)[:, 1:-1, 1:-1, 1:-1]
    joined_pad = jnp.concatenate([active_pad.reshape(2, 6, 10, 10, 128), upward_pad], axis=4)
    mine, joined_pad, slope_pad = lax.optimization_barrier((mine, joined_pad, slope_pad))

    output_0 = conv_forward(joined_pad[:1], w_out).astype(BF16)
    mine = mine + paired(mine, "gz", 7)
    total = jnp.sum(mine * mine, axis=0, keepdims=True)
    total, output_0, joined_pad = lax.optimization_barrier((total, output_0, joined_pad))
    total = total + paired(total, "core", 1)
    total, joined_pad = lax.optimization_barrier((total, joined_pad))
    output_1 = conv_forward(joined_pad[1:, :4], w_out).astype(BF16)
    total = total + paired(total, "gx", 1)
    total, output_1, joined_pad = lax.optimization_barrier((total, output_1, joined_pad))
    output_2 = conv_forward(joined_pad[1:, 2:], w_out).astype(BF16)
    total = total + paired(total, "gx", 3)
    total, output_2, slope_pad = lax.optimization_barrier((total, output_2, slope_pad))
    d_pooled = conv_transpose(slope_pad, w_in)
    d_activation = (d_direct.reshape(activation.shape) + spread(d_pooled) * 0.125).astype(BF16)
    total = total + paired(total, "x", 1)
    total, d_activation = lax.optimization_barrier((total, d_activation))
    output = jnp.concatenate([output_0, jnp.concatenate([output_1, output_2], axis=1)], axis=0)
    for axis, mask in (("x", 3), ("gz", 1), ("gz", 2)):
        total = total + paired(total, axis, mask)
    (clipped,) = _call(_clip_kernel, (((62, 128), F32),), place, total, mine)
    return (output, d_activation, clipped.reshape(-1))


def solution(mesh):
    gx, gy, gz = mesh.devices.shape
    split = Mesh(mesh.devices.reshape(gx, gy // 2, 2, gz), ("gx", "x", "core", "gz"))
    cells = P(None, "gx", ("x", "core"), "gz", None)
    return jax.shard_map(
        local, mesh=split, in_specs=(cells, P(), P(), P(), cells),
        out_specs=(cells, cells, P(("gx", "x", "core", "gz"))), check_vma=False,
    )
```

```python
import itertools

import jax
import jax.numpy as jnp
import numpy as np
from jax import lax
from jax.experimental import pallas as pl
from jax.experimental.pallas import tpu as pltpu
from jax.sharding import Mesh, PartitionSpec as P

F32 = jnp.float32
BF16 = jnp.bfloat16
PARAMS = 2031616


def conv_forward(padded, weight):
    kernel = weight.reshape(3, 3, 3, padded.shape[4], -1)
    return lax.conv_general_dilated(
        padded, kernel, (1, 1, 1), "VALID",
        dimension_numbers=("NXYZC", "XYZIO", "NXYZC"), preferred_element_type=F32,
    )


def conv_transpose(padded, weight):
    kernel = weight.reshape(3, 3, 3, -1, padded.shape[4])[::-1, ::-1, ::-1]
    return lax.conv_general_dilated(
        padded, kernel, (1, 1, 1), "VALID",
        dimension_numbers=("NXYZC", "XYZOI", "NXYZC"), preferred_element_type=F32,
    )


def spread(volume):
    samples, size_x, size_y, size_z, chans = volume.shape
    wide = jnp.broadcast_to(
        volume[:, :, None, :, None, :, None, :], (samples, size_x, 2, size_y, 2, size_z, 2, chans)
    )
    return wide.reshape(samples, 2 * size_x, 2 * size_y, 2 * size_z, chans)


def up_conv(bottom, w_up):
    samples, size_x, size_y, size_z, wide = bottom.shape
    kernel = w_up.reshape(2, 2, 2, wide, -1)
    result = jnp.einsum("sijkc,abeco->siajbkeo", bottom, kernel, preferred_element_type=F32)
    return result.reshape(samples, 2 * size_x, 2 * size_y, 2 * size_z, -1)


def _picks(sources, width):
    picks = np.zeros((len(sources), width), np.float32)
    picks[np.arange(len(sources)), sources] = 1
    return picks


LINES = [(s * 4 + x) * 6 + y for s in range(2) for x in range(4) for y in range(6)]
Z_FACES = _picks([line * 4 + z for z in (0, 3) for line in LINES], 192)
PADDED = _picks([192 + n if z < 0 else 240 + n if z > 3 else n * 4 + z for n in LINES for z in range(-1, 5)], 288)


def _dot(a, b, contract=((1,), (0,))):
    return lax.dot_general(a, b, (contract, ((), ())), preferred_element_type=F32)


def _flag(condition):
    return jnp.where(condition, 1.0, 0.0)


def _wide(rows, count):
    return jnp.concatenate([rows[i * count : (i + 1) * count] for i in range(4)], axis=1)


def _call(kernel, outs, *args, scratch=()):
    vmem = pl.BlockSpec(memory_space=pltpu.VMEM)
    return pl.pallas_call(
        kernel,
        out_shape=tuple(jax.ShapeDtypeStruct(shape, kind) for shape, kind in outs),
        in_specs=[pl.BlockSpec(memory_space=pltpu.SMEM)] + [vmem] * (len(args) - 1),
        out_specs=(vmem,) * len(outs),
        scratch_shapes=[pltpu.VMEM(shape, F32) for shape in scratch],
        compiler_params=pltpu.CompilerParams(vmem_limit_bytes=6 * 1024 * 1024),
        cost_estimate=pl.CostEstimate(flops=1_000_000, bytes_accessed=4_000_000, transcendentals=0),
    )(*args)


def _sides(place_index, here, there):
    even = _flag(place_index % 2 == 0)
    here, there = here[...].astype(F32), there[...].astype(F32)
    return there * even + here * (1.0 - even), here * even + there * (1.0 - even)


def _pack(place_index, first, last, here_ref, there_ref):
    even = _flag(place_index % 2 == 0)
    here_ref[...] = (last * even + first * (1.0 - even)).astype(BF16)
    there_ref[...] = (first * even + last * (1.0 - even)).astype(BF16)


def _table(rows, columns, chosen, value=1.0):
    row = lax.broadcasted_iota(jnp.int32, (rows, columns), 0)
    column = lax.broadcasted_iota(jnp.int32, (rows, columns), 1)
    return jnp.where(chosen(row, column), value, 0.0).astype(BF16)


def _pool_of(r, c):
    return (((c >> 4) & 3) == (r >> 2)) & (((c >> 1) & 3) == (r & 3))


def _pool_y_faces(r, c):
    return c == ((r >> 2) & 7) * 16 + (r >> 5) * 12 + (r & 3)


def _pool_grow_y(r, c):
    plane = (r * 2731) >> 16
    y, z = (r - plane * 24) >> 2, r & 3
    inside = plane * 16 + (y - 1) * 4 + z
    return c == jnp.where(y == 0, 128 + plane * 4 + z, jnp.where(y == 5, 160 + plane * 4 + z, inside))


def _pool_z_faces(r, c):
    y = r & 7
    return (c == (((r >> 3) & 7) * 6 + y) * 4 + (r >> 6) * 3) & (y < 6)


def _pool_windows(r, c):
    u = r >> 4
    dy = (u * 11) >> 5
    line, k = ((r >> 2) & 3) + dy, (r & 3) + u - 3 * dy - 1
    return c == jnp.where(k < 0, 24 + line, jnp.where(k > 3, 32 + line, line * 4 + k))


def _fine_from_blocks(r, c):
    part = (r >> 6) * 4 + ((r >> 3) & 1) * 2 + (r & 1)
    return c == part * 16 + ((r >> 4) & 3) * 4 + ((r >> 1) & 3)


def _blocks_from_fine(r, c):
    return _fine_from_blocks(c, r)


NOWHERE = 9999


def _chip_cell(s, x, y, z):
    return (y >> 2) * 64 + ((s * 2 + x) * 4 + (y & 3)) * 4 + z


def _first_faces(core, last):
    def chosen(r, c):
        x_face = _chip_cell(r >> 5, last, (r >> 2) & 7, r & 3)
        y_face = jnp.where(r < 16, _chip_cell((r >> 3) & 1, (r >> 2) & 1, last * 7, r & 3), NOWHERE)
        return c == x_face * (1 - core) + y_face * core

    return chosen


def _second_faces(core, last):
    def chosen(r, c):
        s, x, z = r >> 4, ((r >> 2) & 3) - 1, r & 3
        side = s * 32 + last * 28 + z
        y_face = jnp.where(x < 0, 128 + side, jnp.where(x > 1, 192 + side, _chip_cell(s, x, last * 7, z)))
        y_face = jnp.where(r < 32, y_face, NOWHERE)
        s = jnp.where(r < 24, 0, 1)
        y, z = ((r - s * 24) >> 2) + 3, r & 3
        x_face = jnp.where(y > 7, 192 + (s * 2 + last) * 4 + z, _chip_cell(s, last, y, z))
        return c == y_face * (1 - core) + x_face * core

    return chosen


def _grown_cells(core):
    def chosen(r, c):
        plane = (r * 2731) >> 16
        y, z = (r - plane * 24) >> 2, r & 3
        s, x = plane >> 2, (plane & 3) - 1
        side = s * 32 + (y - 1) * 4 + z
        low = jnp.where(x < 0, 128 + side, jnp.where(x > 1, 192 + side, _chip_cell(s, x, y - 1, z)))
        low = jnp.where(y == 0, 256 + s * 16 + (x + 1) * 4 + z, low)
        side = s * 24 + y * 4 + z
        high = jnp.where(y == 5, 192 + (s * 2 + x) * 4 + z, _chip_cell(s, x, y + 3, z))
        high = jnp.where(x < 0, 256 + side, jnp.where(x > 1, 304 + side, high))
        return c == low * (1 - core) + high * core

    return chosen


def _pool_kernel(place_ref, both_ref, act_out, cot_out, pooled_ref, here_ref, there_ref):
    act_out[...] = both_ref[0:512, :]
    cot_out[...] = both_ref[512:1024, :]
    pool_of = _table(16, 128, _pool_of, 0.125)
    planes = [_dot(pool_of, both_ref[g * 128 : (g + 1) * 128, :]) for g in range(4)]
    pooled = jnp.concatenate(planes, axis=0).astype(BF16)
    pooled_ref[...] = pooled

    def face(x):
        fine = [both_ref[s * 256 + x * 192 : s * 256 + x * 192 + 64, :] for s in range(4)]
        return jnp.concatenate(fine + [pooled[s * 32 + x * 16 : s * 32 + x * 16 + 16] for s in range(2)], axis=0).astype(F32)

    _pack(place_ref[0], face(0), face(1), here_ref, there_ref)


def _grow_x_kernel(
    place_ref, act_ref, cot_ref, pooled_ref, got_here, got_there,
    act_out, cot_out, pooled_out, here_ref, there_ref,
):
    low, high = _sides(place_ref[0], got_here, got_there)
    firsts, lasts = [], []
    for i, (ref, out) in enumerate(((act_ref, act_out), (cot_ref, cot_out))):
        fine = ref[...].astype(F32)
        parts = []
        for s in range(2):
            at_face = slice(i * 128 + s * 64, i * 128 + s * 64 + 64)
            parts += [low[at_face], fine[s * 256 : (s + 1) * 256], high[at_face]]
        grown = jnp.concatenate(parts, axis=0)
        out[...] = grown
        firsts += [grown[p * 64 : p * 64 + 8] for p in range(12)]
        lasts += [grown[p * 64 + 56 : p * 64 + 64] for p in range(12)]
    pooled = pooled_ref[...].astype(F32)
    parts = []
    for s in range(2):
        at_face = slice(256 + s * 16, 272 + s * 16)
        parts += [low[at_face], pooled[s * 32 : (s + 1) * 32], high[at_face]]
    grown = jnp.concatenate(parts, axis=0).astype(BF16)
    pooled_out[...] = grown
    faces = _dot(_table(64, 128, _pool_y_faces), grown)
    first = jnp.concatenate(firsts + [faces[0:32]], axis=0)
    last = jnp.concatenate(lasts + [faces[32:64]], axis=0)
    _pack(place_ref[2], first, last, here_ref, there_ref)


def _grow_y_kernel(
    place_ref, act_ref, cot_ref, pooled_ref, got_here, got_there,
    act_out, cot_out, pooled_out, here_ref, there_ref, act_lines, cot_lines,
):
    low, high = _sides(place_ref[2], got_here, got_there)
    firsts, lasts = [], []
    for i, (ref, out) in enumerate(((act_ref, act_lines), (cot_ref, cot_lines))):
        for p in range(12):
            at_face = slice(i * 96 + p * 8, i * 96 + p * 8 + 8)
            out[p * 80 : p * 80 + 8, :] = low[at_face]
            out[p * 80 + 8 : p * 80 + 72, :] = ref[p * 64 : (p + 1) * 64, :]
            out[p * 80 + 72 : p * 80 + 80, :] = high[at_face]
        firsts.append(out[pl.ds(0, 120, 8), :])
        lasts.append(out[pl.ds(7, 120, 8), :])
    rows = jnp.concatenate([pooled_ref[...], low[192:224].astype(BF16), high[192:224].astype(BF16)], axis=0)
    act_out[...] = act_lines[...].astype(BF16)
    cot_out[...] = cot_lines[...].astype(BF16)
    grown = _dot(_table(192, 192, _pool_grow_y), rows)
    pooled_out[...] = grown
    faces = _dot(_table(128, 192, _pool_z_faces), grown.astype(BF16))
    first = jnp.concatenate(firsts + [faces[0:64]], axis=0)
    last = jnp.concatenate(lasts + [faces[64:128]], axis=0)
    _pack(place_ref[3], first, last, here_ref, there_ref)


def _grow_z_kernel(place_ref, act_ref, got_here, got_there, out_ref, lines):
    low, high = _sides(place_ref[3], got_here, got_there)
    lines[:, 8:16, :] = act_ref[...].astype(F32).reshape(120, 8, 128)
    lines[:, 7:8, :] = low[0:120][:, None, :]
    lines[:, 16:17, :] = high[0:120][:, None, :]
    out_ref[...] = lines[:, 7:17, :].astype(BF16)


def traded(here, there, axis):
    count = lax.axis_size(axis)
    first_pairs = [(i, i ^ 1) for i in range(count)]
    second_pairs = [(i, j) for i in range(count) for j in [((i + 1) ^ 1) - 1] if 0 <= j < count]
    return lax.ppermute(here, axis, first_pairs), lax.ppermute(there, axis, second_pairs)


def extended(place, both):
    rows, f32_rows = lambda n: ((n, 128), BF16), lambda n: ((n, 128), F32)
    own, cot, pooled, *faces = _call(_pool_kernel, (rows(512), rows(512), rows(64), rows(288), rows(288)), place, both)
    outs = (f32_rows(768), f32_rows(768), rows(128), rows(224), rows(224))
    act, cot, pooled, *faces = _call(_grow_x_kernel, outs, place, own, cot, pooled, *traded(*faces, "gx"))
    outs = (rows(960), rows(960), f32_rows(192), rows(304), rows(304))
    act, cot, pooled, *faces = _call(
        _grow_y_kernel, outs, place, act, cot, pooled, *traded(*faces, ("x", "core")), scratch=((960, 128),) * 2
    )
    return own, act, cot, pooled, traded(*faces, "gz")


def _gradients_kernel(
    place_ref, act_ref, cot_ref, pool_ref, got_here, got_there,
    w_in_hbm, w_back_hbm, w_up_hbm,
    sums_ref, send_ref, coarse_ref, d_act_ref,
    w_in, w_back, w_up, lines, shifted, pooled, spaced, sem_in,
):
    loads = [
        pltpu.make_async_copy(source, target, sem_in.at[i])
        for i, (source, target) in enumerate(((w_in_hbm, w_in), (w_up_hbm, w_up), (w_back_hbm, w_back)))
    ]
    for load in loads:
        load.start()
    core = place_ref[2]
    side = (core, 1 - core)

    def put(row, value, stride=1):
        done, count = 0, value.shape[0]
        while done < count:
            first = row + stride * done
            block = first // 496
            here = min(count - done, -((first - 496 * (block + 1)) // stride))
            start = block // 2 * 496 + first % 496
            where = pl.ds(start, here) if stride == 1 else pl.ds(start, here, stride)
            sums_ref[side[block % 2], where, :] = value[done : done + here]
            done += here

    def ship(first, last):
        send_ref[first:last, :] = sums_ref[1, first:last, :].astype(BF16)

    low, high = _sides(place_ref[3], got_here, got_there)
    lines[:, 8:16, :] = cot_ref[...].astype(F32).reshape(120, 8, 128)
    lines[:, 7:8, :] = low[120:240][:, None, :]
    lines[:, 16:17, :] = high[120:240][:, None, :]
    for dz in range(3):
        window = lines[:, 7 + dz : 15 + dz, :].reshape(2, 6, 10, 8, 128)
        for dy in range(3):
            u = 8 - 3 * dy - dz
            shifted[:, :, :, u * 128 : (u + 1) * 128] = window[:, :, dy : dy + 8].reshape(2, 6, 64, 128).astype(BF16)

    windows = _table(144, 48, _pool_windows)
    for g in range(8):
        at_face = slice(240 + g * 8, 248 + g * 8)
        plane = [pool_ref[g * 24 : (g + 1) * 24, :], low[at_face], high[at_face], jnp.zeros((8, 128), F32)]
        picked = _dot(windows, jnp.concatenate(plane, axis=0).astype(BF16))
        for u in range(9):
            pooled[g // 4, g % 4, :, u * 128 : (u + 1) * 128] = picked[u * 16 : (u + 1) * 16].astype(BF16)
    loads[0].wait()
    before = jnp.zeros((64, 256), F32)
    for dx in range(3):
        before += _dot(pooled[:, dx : dx + 2].reshape(64, 1152), w_in[dx * 1152 : (dx + 1) * 1152, :])
    squash = 1.0 / (1.0 + jnp.exp(-before))
    bottom32 = (before * squash).astype(BF16).astype(F32)
    bottom = bottom32.astype(BF16)
    loads[1].wait()
    parts = [_dot(bottom, w_up[p * 256 : (p + 1) * 256, :]).astype(BF16) for p in range(8)]
    perm = _table(128, 128, _fine_from_blocks)
    upward = jnp.concatenate(
        [_dot(perm, jnp.concatenate([p[g * 16 : (g + 1) * 16] for p in parts], axis=0)) for g in range(4)], axis=0
    )

    loads[2].wait()
    d_joined = jnp.zeros((512, 256), F32)
    for dx in range(3):
        d_joined += _dot(shifted[:, dx : dx + 4].reshape(512, 1152), w_back[(2 - dx) * 1152 : (3 - dx) * 1152, :])
    d_act_ref[...] = d_joined[:, :128]

    joined_t = jnp.concatenate([act_ref[...].astype(F32).T, upward.T], axis=0).astype(BF16)
    for dx in range(3):
        grad = _dot(joined_t, shifted[:, dx : dx + 4].reshape(512, 1152))
        for u in range(9):
            put(8960 + (18 - 9 * dx + u) * 256, grad[:, u * 128 : (u + 1) * 128])
    ship(4960, 7936)

    d_upward = d_joined[:, 128:].astype(BF16)
    perm = _table(128, 128, _blocks_from_fine)
    planes = [_dot(perm, d_upward[g * 128 : (g + 1) * 128]).astype(BF16) for g in range(4)]
    blocks = [jnp.concatenate([plane[p * 16 : (p + 1) * 16] for plane in planes], axis=0) for p in range(8)]
    d_bottom = jnp.zeros((64, 256), F32)
    for p in range(8):
        d_bottom += _dot(blocks[p], w_up[p * 256 : (p + 1) * 256, :], ((1,), (1,)))
    bottom_t = bottom32.T.astype(BF16)
    for p in range(8):
        put(6912 + p * 256, _dot(bottom_t, blocks[p]))
    slope = (d_bottom * squash * (1.0 + before * (1.0 - squash))).astype(BF16)
    coarse = jnp.concatenate([bottom, slope], axis=1)
    coarse_ref[...] = coarse
    for lane in range(4):
        send_ref[7936 + lane * 64 : 8000 + lane * 64, :] = coarse[:, lane * 128 : (lane + 1) * 128]

    spaced[...] = jnp.zeros((128, 768), BF16)
    for s in range(2):
        for dx in range(3):
            spaced[s * 64 + dx * 16 : s * 64 + dx * 16 + 32, dx * 256 : (dx + 1) * 256] = slope[s * 32 : (s + 1) * 32]
    for u in range(9):
        picked_t = pooled[:, :, :, u * 128 : (u + 1) * 128].reshape(128, 128).astype(F32).T.astype(BF16)
        grad = _dot(picked_t, spaced[...])
        for dx in range(3):
            for h in range(2):
                put((9 * dx + u) * 256 + h, grad[:, dx * 256 + h * 128 : dx * 256 + (h + 1) * 128], 2)
    ship(0, 4960)


def gradients(place, act, cot, pool, got_here, got_there, w_in, w_back, w_up):
    shape = jax.ShapeDtypeStruct
    vmem, hbm = pl.BlockSpec(memory_space=pltpu.VMEM), pl.BlockSpec(memory_space=pltpu.HBM)
    return pl.pallas_call(
        _gradients_kernel,
        out_shape=(
            shape((2, 7936, 128), F32), shape((8192, 128), BF16), shape((64, 512), BF16), shape((512, 128), F32),
        ),
        in_specs=[pl.BlockSpec(memory_space=pltpu.SMEM)] + [vmem] * 5 + [hbm] * 3,
        out_specs=(vmem,) * 4,
        scratch_shapes=[
            pltpu.VMEM((3456, 256), BF16), pltpu.VMEM((3456, 256), BF16), pltpu.VMEM((2048, 128), BF16),
            pltpu.VMEM((120, 24, 128), F32), pltpu.VMEM((2, 6, 64, 1152), BF16),
            pltpu.VMEM((2, 4, 16, 1152), BF16), pltpu.VMEM((128, 768), BF16),
            pltpu.SemaphoreType.DMA((3,)),
        ],
        compiler_params=pltpu.CompilerParams(vmem_limit_bytes=18 * 1024 * 1024),
        cost_estimate=pl.CostEstimate(flops=2_500_000_000, bytes_accessed=16_000_000, transcendentals=16384),
    )(
        place, act, cot, pool, got_here, got_there,
        w_in, w_back, w_up,
    )


def crossed(array, shift, along_gx):
    pairs = []
    for gx, x, core in itertools.product(range(4), range(4), range(2)):
        to = ((gx + shift) % 4, x) if core == along_gx else (gx, (x + shift) % 4)
        pairs.append(((gx * 4 + x) * 2 + core, (to[0] * 4 + to[1]) * 2 + core))
    return lax.ppermute(array, ("gx", "x", "core"), pairs)


def paired(array, axis, bit):
    count = lax.axis_size(axis)
    return lax.ppermute(array, axis, [(i, i ^ bit) for i in range(count)])


def _put_faces(ref, start, count, faces):
    for lane in range(4):
        rows = slice(start + lane * count, start + (lane + 1) * count)
        ref[rows, :] = faces[:, lane * 128 : (lane + 1) * 128].astype(ref.dtype)


def _get_faces(ref, start, count, there):
    return _wide(ref[start : start + 4 * count, :].astype(F32) * there, count).astype(BF16)


def _split_kernel(place_ref, keep_ref, got_ref, coarse_ref, own, send_1, send_2, send_3, chip_ref):
    core = place_ref[2]
    for shift, ref in enumerate((own, send_1, send_2, send_3)):
        gx, x = (place_ref[0] + shift) % 4, (place_ref[1] + shift) % 4
        for j in range(4):
            block = (gx * 4 + j) * (1 - core) + (j * 4 + x) * core
            rows = pl.ds(pl.multiple_of(block * 496, 16), 496)
            ref[j * 496 : (j + 1) * 496, :] = (keep_ref[0, rows, :] + got_ref[rows, :].astype(F32)).astype(ref.dtype)
    mine, other = coarse_ref[...].astype(F32), _wide(got_ref[7936:8192, :].astype(F32), 64)
    zero, one = _flag(core == 0), _flag(core == 1)
    chip = jnp.concatenate([mine * zero + other * one, mine * one + other * zero], axis=0).astype(BF16)
    chip_ref[...] = chip
    _put_faces(send_1, 1984, 64, _dot(_table(64, 128, _first_faces(core, 1)), chip))
    _put_faces(send_3, 1984, 64, _dot(_table(64, 128, _first_faces(core, 0)), chip))


def _second_kernel(place_ref, chip_ref, own_ref, got_2, got_1, got_3, known_ref, own, send_1, send_2, send_3, total):
    gx, x, core = place_ref[0], place_ref[1], place_ref[2]
    first, second = gx * (1 - core) + x * core, x * (1 - core) + gx * core
    total[...] = own_ref[...] + (got_1[0:1984, :].astype(F32) + got_2[...].astype(F32) + got_3[0:1984, :].astype(F32))
    for shift, ref in enumerate((own, send_1, send_2, send_3)):
        ref[0:496, :] = total[pl.ds(pl.multiple_of((second + shift) % 4 * 496, 16), 496), :]
    sides = [_get_faces(got_1, 1984, 64, _flag(first > 0)), _get_faces(got_3, 1984, 64, _flag(first < 3))]
    known = jnp.concatenate([chip_ref[...]] + sides, axis=0)
    known_ref[...] = known
    _put_faces(send_1, 496, 48, _dot(_table(48, 256, _second_faces(core, 1)), known))
    _put_faces(send_3, 496, 48, _dot(_table(48, 256, _second_faces(core, 0)), known))


def _third_kernel(
    place_ref, known_ref, z_faces_ref, own_ref, got_2, got_1, got_3, grown_out, keep_ref, send_ref, other_ref, rows, chunks
):
    gx, x, core, gz = (place_ref[i] for i in range(4))
    second = x * (1 - core) + gx * core
    rows[...] = own_ref[...] + (got_1[0:496, :] + got_2[...] + got_3[0:496, :])
    chunks[...] = jnp.zeros((2, 256, 128), F32)
    for r, q, p in itertools.product(range(2), repeat=3):
        chunk, place = 4 * r + 2 * q + p, ((q ^ r) * 2 + r) * 64
        chunks[p ^ r, place : place + 62, :] = rows[chunk * 62 : (chunk + 1) * 62, :]
    half = (gz + gz // 4) % 2
    keep_ref[...] = chunks[half]
    send_ref[0:256, :] = chunks[1 - half]
    sides = [_get_faces(got_1, 496, 48, _flag(second > 0)), _get_faces(got_3, 496, 48, _flag(second < 3))]
    known = jnp.concatenate([known_ref[...]] + sides, axis=0)
    grown = _dot(_table(192, 352, _grown_cells(core)), known).astype(BF16)
    grown_out[...] = grown
    faces = _dot(z_faces_ref[...], grown)
    even = _flag(gz % 2 == 0)
    _put_faces(send_ref, 256, 48, faces[48:96] * even + faces[0:48] * (1.0 - even))
    _put_faces(other_ref, 0, 48, faces[0:48] * even + faces[48:96] * (1.0 - even))


def _fourth_kernel(place_ref, keep_ref, got_ref, keep_out, send_out, both):
    gz = place_ref[3]
    mine = keep_ref[...] + got_ref[0:256, :]
    both[0] = mine[0:128]
    both[1] = mine[128:256]
    half = (gz // 2 + gz // 4) % 2
    keep_out[...] = both[half]
    send_out[...] = both[1 - half]


def _pad_kernel(place_ref, grown_ref, padded_ref, got_ref, other_ref, bottom_ref, slope_ref):
    even = _flag(place_ref[3] % 2 == 0)
    here, there = got_ref[256:448, :], other_ref[...].astype(F32)
    low = _wide(there * even + here * (1.0 - even), 48).astype(BF16)
    high = _wide(here * even + there * (1.0 - even), 48).astype(BF16)
    padded = _dot(padded_ref[...], jnp.concatenate([grown_ref[...], low, high], axis=0)).astype(BF16)
    bottom_ref[...] = padded[:, 0:256]
    slope_ref[...] = padded[:, 256:512]


def _clip_kernel(place_ref, total_ref, both_ref, out_ref):
    total = jnp.sum(total_ref[...], axis=1, keepdims=True)
    factor = jnp.minimum(1.0, jnp.sqrt(PARAMS / (total + 1e-06)))
    out_ref[...] = both_ref[pl.ds(pl.multiple_of(place_ref[3] // 4 * 64, 64), 62), :] * factor


def scattered_sum(place, keep, send, coarse):
    def f32_rows(n):
        return ((n, 128), F32)

    def rows(n):
        return ((n, 128), BF16)

    got = paired(send, "core", 1)
    outs = (f32_rows(1984), rows(2240), rows(1984), rows(2240), ((128, 512), BF16))
    own, *sends, chip = _call(_split_kernel, outs, place, keep, got, coarse)
    got_2, got_1, got_3 = [crossed(sends[s - 1], s, 0) for s in (2, 1, 3)]
    outs = (((256, 512), BF16), f32_rows(496), f32_rows(688), f32_rows(496), f32_rows(688))
    known, own, *sends = _call(_second_kernel, outs, place, chip, own, got_2, got_1, got_3, scratch=((1984, 128),))
    got_2, got_1, got_3 = [crossed(sends[s - 1], s, 1) for s in (2, 1, 3)]
    outs = (((192, 512), BF16), f32_rows(256), f32_rows(448), rows(192))
    grown, keep, send, other = _call(
        _third_kernel, outs, place, known, jnp.asarray(Z_FACES, BF16), own, got_2, got_1, got_3, scratch=((496, 128), (2, 256, 128))
    )
    got = paired(send, "gz", 1)
    other = lax.ppermute(other, "gz", [(i, j) for i in range(8) for j in [((i + 1) ^ 1) - 1] if 0 <= j < 8])
    keep, send = _call(_fourth_kernel, (f32_rows(128),) * 2, place, keep, got, scratch=((2, 128, 128),))
    return keep, send, grown, got, other


def local(activation, w_in, w_up, w_out, cotangent):
    place = jnp.stack([lax.axis_index(a) for a in ("gx", "x", "core", "gz")]).astype(jnp.int32)
    both = jnp.concatenate([activation.reshape(512, 128), cotangent.reshape(512, 128)], axis=0)
    own, act, cot, pooled, faces = extended(place, both)
    w_back = w_out.reshape(27, 256, 128).transpose(0, 2, 1).reshape(3456, 256)
    keep, send, coarse, d_direct = gradients(place, own, cot, pooled, *faces, w_in, w_back, w_up)
    keep, send, grown, got, other = scattered_sum(place, keep, send, coarse)

    send, grown, act = lax.optimization_barrier((send, grown, act))
    mine = keep + paired(send, "gz", 2)
    (active_pad,) = _call(_grow_z_kernel, (((120, 10, 128), BF16),), place, act, *faces, scratch=((120, 24, 128),))
    active_pad, grown = lax.optimization_barrier((active_pad, grown))
    pads = _call(_pad_kernel, (((288, 256), BF16),) * 2, place, grown, jnp.asarray(PADDED, BF16), got, other)
    bottom_pad, slope_pad = (p.reshape(2, 4, 6, 6, 256) for p in pads)
    upward_pad = up_conv(bottom_pad, w_up).astype(BF16)[:, 1:-1, 1:-1, 1:-1]
    joined_pad = jnp.concatenate([active_pad.reshape(2, 6, 10, 10, 128), upward_pad], axis=4)
    mine, joined_pad, slope_pad = lax.optimization_barrier((mine, joined_pad, slope_pad))

    output_0 = conv_forward(joined_pad[:1], w_out).astype(BF16)
    mine = mine + paired(mine, "gz", 7)
    total = jnp.sum(mine * mine, axis=0, keepdims=True)
    total, output_0, joined_pad = lax.optimization_barrier((total, output_0, joined_pad))
    total = total + paired(total, "core", 1)
    total, joined_pad = lax.optimization_barrier((total, joined_pad))
    output_1 = conv_forward(joined_pad[1:, :4], w_out).astype(BF16)
    total = total + paired(total, "gx", 1)
    total, output_1, joined_pad = lax.optimization_barrier((total, output_1, joined_pad))
    output_2 = conv_forward(joined_pad[1:, 2:], w_out).astype(BF16)
    total = total + paired(total, "gx", 3)
    total, output_2, slope_pad = lax.optimization_barrier((total, output_2, slope_pad))
    d_pooled = conv_transpose(slope_pad, w_in)
    d_activation = (d_direct.reshape(activation.shape) + spread(d_pooled) * 0.125).astype(BF16)
    total = total + paired(total, "x", 1)
    total, d_activation = lax.optimization_barrier((total, d_activation))
    output = jnp.concatenate([output_0, jnp.concatenate([output_1, output_2], axis=1)], axis=0)
    for axis, mask in (("x", 3), ("gz", 1), ("gz", 2)):
        total = total + paired(total, axis, mask)
    (clipped,) = _call(_clip_kernel, (((62, 128), F32),), place, total, mine)
    return (output, d_activation, clipped.reshape(-1))


def solution(mesh):
    gx, gy, gz = mesh.devices.shape
    split = Mesh(mesh.devices.reshape(gx, gy // 2, 2, gz), ("gx", "x", "core", "gz"))
    cells = P(None, "gx", ("x", "core"), "gz", None)
    return jax.shard_map(
        local, mesh=split, in_specs=(cells, P(), P(), P(), cells),
        out_specs=(cells, cells, P(("gx", "x", "core", "gz"))), check_vma=False,
    )
```
